32 devices in a mesh: dp: 4 (over z), fsdp: 8 (over y, x, core).
Axes of the slice: x: 2, y: 2, z: 4, core: 2. Of those that a mesh axis runs over, the one named last changes fastest.
Arguments:
- inputs: float32 [32768, 768], P(('dp', 'fsdp')), may hold values from -6 to 6
- lengths: int32 [64], P(('dp', 'fsdp')), may hold values from 1 to 512, as said below
- query_weight: bfloat16 [768, 768], P(('dp', 'fsdp')), may hold values from -0.21875 to 0.21875
- key_weight: bfloat16 [768, 768], P(('dp', 'fsdp')), may hold values from -0.21875 to 0.21875
- value_weight: bfloat16 [768, 768], P(('dp', 'fsdp')), may hold values from -0.21875 to 0.21875
- out_weight: bfloat16 [768, 768], P(('dp', 'fsdp')), may hold values from -1.75 to 1.75
- query_bias: bfloat16 [768], P(('dp', 'fsdp')), may hold values from -1.5 to 1.5
- value_bias: bfloat16 [768], P(('dp', 'fsdp')), may hold values from -1.5 to 1.5
- out_bias: bfloat16 [768], P(('dp', 'fsdp')), may hold values from -1.5 to 1.5
- first_gain: bfloat16 [768], P(('dp', 'fsdp')), may hold values from 0.5 to 1.5
- first_shift: bfloat16 [768], P(('dp', 'fsdp')), may hold values from -1.5 to 1.5
- inner_weight: bfloat16 [768, 3072], P(('dp', 'fsdp')), may hold values from -0.21875 to 0.21875
- inner_bias: bfloat16 [3072], P(('dp', 'fsdp')), may hold values from -1.5 to 1.5
- down_weight: bfloat16 [3072, 768], P(('dp', 'fsdp')), may hold values from -0.109375 to 0.109375
- down_bias: bfloat16 [768], P(('dp', 'fsdp')), may hold values from -1.5 to 1.5
- second_gain: bfloat16 [768], P(('dp', 'fsdp')), may hold values from 0.5 to 1.5
- second_shift: bfloat16 [768], P(('dp', 'fsdp')), may hold values from -1.5 to 1.5
- cotangent: float32 [32768, 768], P(('dp', 'fsdp')), may hold values from -6 to 6
Outputs:
- output: float32 [32768, 768], P(('dp', 'fsdp'))
- grad_input: float32 [32768, 768], P(('dp', 'fsdp'))
- grad_query_weight: float32 [768, 768], P(('dp', 'fsdp'))
- grad_key_weight: float32 [768, 768], P(('dp', 'fsdp'))
- grad_value_weight: float32 [768, 768], P(('dp', 'fsdp'))
- grad_out_weight: float32 [768, 768], P(('dp', 'fsdp'))
- grad_query_bias: float32 [768], P(('dp', 'fsdp'))
- grad_value_bias: float32 [768], P(('dp', 'fsdp'))
- grad_out_bias: float32 [768], P(('dp', 'fsdp'))
- grad_first_gain: float32 [768], P(('dp', 'fsdp'))
- grad_first_shift: float32 [768], P(('dp', 'fsdp'))
- grad_inner_weight: float32 [768, 3072], P(('dp', 'fsdp'))
- grad_inner_bias: float32 [3072], P(('dp', 'fsdp'))
- grad_down_weight: float32 [3072, 768], P(('dp', 'fsdp'))
- grad_down_bias: float32 [768], P(('dp', 'fsdp'))
- grad_second_gain: float32 [768], P(('dp', 'fsdp'))
- grad_second_shift: float32 [768], P(('dp', 'fsdp'))
The draws below stay inside these ranges and needn't reach their ends.
Inputs may be any that keep to these rules, and one draw needn't show every extreme that they name: `lengths`: positions of a pair below its entry are tokens, the rest padding; some pair has all 512 positions valid.
All inputs are finite; a program needn't handle non-finite values.
Results may differ from the reference program's by a relative error of at most 0.014.
The reference program's roundings to bfloat16 on the way count: a program that leaves them out, or rounds other values in their place, can miss the bound.
Values may be sent and summed in bfloat16 or wider, within the bound.
No kernel may reach another device: no remote copies, remote signals or barrier semaphores. Data moves between devices by JAX's collectives and lax.ppermute only.
A program may use at most 192 MiB of HBM per device.

```python
import jax
import jax.numpy as jnp
from jax import lax

D = 768
H = 12
DH = 64
FF = 3072
L = 512
SEQ_DEV = 2
PAIRS = 64
TOKENS = 32768
DEVICES = 32


def draw_lengths(key, part):
    key = jax.random.fold_in(key, 11)
    base_key, pick_key = jax.random.split(key)
    sample_len = jax.random.randint(base_key, (PAIRS,), 1, L + 1)
    chosen = jax.random.randint(pick_key, (), 0, PAIRS)
    return jnp.where(jnp.arange(PAIRS) == chosen, L, sample_len).astype(jnp.int32)


def strengthened(values, rng, source, target, parts, factor):
    owner, partner = [(jnp.arange(values.shape[axis_at]) // (values.shape[axis_at] // parts)).reshape([-1 if axis == axis_at else 1 for axis in range(values.ndim)]) for axis_at in (source, target)]
    chosen = jax.random.permutation(rng, parts)[partner]
    strong = (owner == chosen) | (owner == (partner + parts // 2) % parts)
    return jnp.where(strong, factor * values, values)


def block_levels(rng, dims, pieces, least, largest):
    def one(position, shards_of):
        steps = jax.random.uniform(jax.random.fold_in(jax.random.fold_in(rng, 6), position), (shards_of,), jnp.float32, least / len(pieces), largest / len(pieces))
        return jnp.repeat(jnp.exp(steps), dims[position] // shards_of).reshape((-1,) + (1,) * (len(dims) - position - 1))

    gain = one(*pieces[0])
    for cut in pieces[1:]:
        gain = gain * one(*cut)
    return gain


def scatter_about(key, dims, scale, reach, pieces=(), kind=jnp.bfloat16):
    array = scale * jax.random.normal(key, dims, jnp.float32)
    if pieces:
        array = array * block_levels(key, dims, pieces, -0.22, 0.18)
    return jnp.clip(array, -reach, reach).astype(kind)


def heavy_noise(own_key, dims, scale, most, pieces, heavy, kind=jnp.bfloat16):
    result = scale * jax.random.normal(own_key, dims, jnp.float32)
    if pieces:
        result = result * block_levels(own_key, dims, pieces, -0.22, 0.18)
    return jnp.clip(strengthened(result, jax.random.fold_in(own_key, 3), *heavy), -most, most).astype(kind)


def setup_inputs(seed: int = 0) -> dict:
    arg_keys = jax.random.split(jax.random.key(seed), 19)
    return {
        "inputs": scatter_about(arg_keys[0], (TOKENS, D), 1.0, 6.0, ((0, 32),), jnp.float32),
        "lengths": draw_lengths(jax.random.fold_in(arg_keys[18], 71), 0),
        "query_weight": scatter_about(arg_keys[2], (D, D), D ** -0.5, 0.21875, ((0, 32),)),
        "key_weight": scatter_about(arg_keys[3], (D, D), D ** -0.5, 0.21875, ((0, 32),)),
        "value_weight": scatter_about(arg_keys[4], (D, D), D ** -0.5, 0.21875, ((0, 32),)),
        "out_weight": scatter_about(arg_keys[5], (D, D), (D // 64) ** -0.5, 1.75, ((0, 32),)),
        "query_bias": scatter_about(arg_keys[6], (D,), 0.3, 1.5, ((0, 32),)),
        "value_bias": scatter_about(arg_keys[7], (D,), 0.3, 1.5, ((0, 32),)),
        "out_bias": scatter_about(arg_keys[8], (D,), 0.3, 1.5, ((0, 32),)),
        "first_gain": jnp.clip(1.0 + 0.1 * jax.random.normal(arg_keys[9], (D,), jnp.float32), 0.5, 1.5).astype(jnp.bfloat16),
        "first_shift": scatter_about(arg_keys[10], (D,), 0.3, 1.5, ((0, 32),)),
        "inner_weight": scatter_about(arg_keys[11], (D, FF), D ** -0.5, 0.21875, ((0, 32),)),
        "inner_bias": scatter_about(arg_keys[12], (FF,), 0.3, 1.5, ((0, 32),)),
        "down_weight": scatter_about(arg_keys[13], (FF, D), FF ** -0.5, 0.109375, ((0, 32),)),
        "down_bias": scatter_about(arg_keys[14], (D,), 0.3, 1.5, ((0, 32),)),
        "second_gain": jnp.clip(1.0 + 0.1 * jax.random.normal(arg_keys[15], (D,), jnp.float32), 0.5, 1.5).astype(jnp.bfloat16),
        "second_shift": scatter_about(arg_keys[16], (D,), 0.3, 1.5, ((0, 32),)),
        "cotangent": heavy_noise(arg_keys[17], (TOKENS, D), 1.0, 6.0, ((0, 32),), (0, 1, 32, 2.75), jnp.float32),
    }


@jax.custom_vjp
def low(v):
    return lax.optimization_barrier(v.astype(jnp.bfloat16)).astype(jnp.float32)

@jax.custom_vjp
def low_back(v):
    return v

def low_keep(v):
    return (low(v), None)

def low_pass(kept, grad):
    return (grad,)

def back_keep(v):
    return (v, None)

def back_low(kept, grad):
    return (low(grad),)
low.defvjp(low_keep, low_pass)
low_back.defvjp(back_keep, back_low)
NORM_EPSILON = 1e-12
MASKED_SCORE = -1000000000.0

def rounded_both(tensor):
    return low_back(low(tensor))

def product(lhs_rows, rhs_cols):
    return jnp.dot(lhs_rows, rhs_cols, precision=lax.Precision.HIGHEST)

def layer_norm(total_in, norm_gain, norm_shift):
    center = total_in - lax.optimization_barrier(jnp.mean(total_in, axis=-1, keepdims=True))
    norm_scale = lax.rsqrt(lax.optimization_barrier(jnp.mean(center * center, axis=-1, keepdims=True)) + NORM_EPSILON)
    return center * norm_scale * norm_gain + norm_shift

def forward(inputs, lengths, params):
    query_weight, key_weight, value_weight, out_weight, query_bias, value_bias, out_bias, first_gain, first_shift, inner_weight, inner_bias, down_weight, down_bias, second_gain, second_shift = params
    seq_count = inputs.shape[0] // L
    head_shape = (seq_count, L, H, DH)
    lowered = low(inputs)
    queries = rounded_both(product(lowered, query_weight) + query_bias).reshape(head_shape)
    key_rows = rounded_both(product(lowered, key_weight)).reshape(head_shape)
    value_rows = rounded_both(product(lowered, value_weight) + value_bias).reshape(head_shape)
    scores = low_back(jnp.einsum('gqhe,gkhe->ghqk', queries, key_rows, precision=lax.Precision.HIGHEST) * 0.125)
    visible = (jnp.arange(L)[None, :] < lengths[:, None])[:, None, None, :]
    scores = jnp.where(visible, scores, MASKED_SCORE)
    row_peak = lax.optimization_barrier(jnp.max(scores, axis=-1, keepdims=True))
    exponent = jnp.exp(scores - row_peak)
    attention = low(exponent / lax.optimization_barrier(jnp.sum(exponent, axis=-1, keepdims=True)))
    attended = jnp.einsum('ghqk,gkhe->gqhe', attention, value_rows, precision=lax.Precision.HIGHEST)
    attended = rounded_both(attended.reshape(seq_count * L, D))
    branch_out = low_back(product(attended, out_weight) + out_bias)
    hidden = layer_norm(inputs + branch_out, first_gain, first_shift)
    inner_sum = low_back(product(low(hidden), inner_weight) + inner_bias)
    active = low(jax.nn.gelu(inner_sum, approximate=False))
    outer_sum = low_back(product(active, down_weight) + down_bias)
    return layer_norm(hidden + outer_sum, second_gain, second_shift)

def reference(inputs, lengths, query_weight, key_weight, value_weight, out_weight, query_bias, value_bias, out_bias, first_gain, first_shift, inner_weight, inner_bias, down_weight, down_bias, second_gain, second_shift, cotangent):
    params = tuple((weight_arg.astype(jnp.float32) for weight_arg in (query_weight, key_weight, value_weight, out_weight, query_bias, value_bias, out_bias, first_gain, first_shift, inner_weight, inner_bias, down_weight, down_bias, second_gain, second_shift)))
    group_rows = SEQ_DEV * L
    inputs_split = inputs.reshape(DEVICES, group_rows, D)
    lengths_split = lengths.reshape(DEVICES, SEQ_DEV).astype(jnp.int32)
    cotangent_split = cotangent.reshape(DEVICES, group_rows, D)

    def one_group(running, packed):
        group_in, group_lengths, group_cot = packed

        def group_forward(group_x, weights):
            return forward(group_x, group_lengths, weights)
        produced, pullback = jax.vjp(group_forward, group_in, params)
        input_grad, weight_grads = pullback(group_cot)
        running = jax.tree.map(jnp.add, running, weight_grads)
        return (running, (produced, input_grad))
    zero_sums = tuple((jnp.zeros_like(weight_arg) for weight_arg in params))
    totals, (produced, input_grad) = lax.scan(one_group, zero_sums, (inputs_split, lengths_split, cotangent_split))
    return (produced.reshape(TOKENS, D), input_grad.reshape(TOKENS, D), totals[0], totals[1], totals[2], totals[3], totals[4], totals[5], totals[6], totals[7], totals[8], totals[9], totals[10], totals[11], totals[12], totals[13], totals[14])
```

```python
import functools
import math

import jax
import jax.numpy as jnp
from jax import lax
from jax.experimental import pallas as pl
from jax.experimental.pallas import tpu as pltpu
from jax.sharding import PartitionSpec as P

D = 768
H = 12
DH = 64
FF = 3072
SLABS = 32
SLAB = D // SLABS
CHIPS = SLABS // 2
PAIR_ROWS = 2 * SLAB
NORM_EPSILON = 1e-12
MASKED_SCORE = -1000000000.0
GAUSS_DENSITY = 0.3989422804014327
LOG2E = 1.4426950408889634
MIB = 1 << 20

QKV_HALF = 3 * D // 2
QKV_BLOCK = QKV_HALF + 128
OUT_HALF = D // 2
INNER_HALF = FF // 2
FFN_BLOCK = OUT_HALF + INNER_HALF + 2 * D

bf16 = jnp.bfloat16
f32 = jnp.float32
ANY = pl.BlockSpec(memory_space=pl.ANY)
SMEM = pl.BlockSpec(memory_space=pltpu.SMEM)


def dot(a, b):
    return lax.dot_general(a, b, (((1,), (0,)), ((), ())), preferred_element_type=f32)


def dot_t(a, b):
    return lax.dot_general(a, b, (((1,), (1,)), ((), ())), preferred_element_type=f32)


def dot_l(a, b):
    return lax.dot_general(a, b, (((0,), (0,)), ((), ())), preferred_element_type=f32)


def aligned(start, size, unit):
    return pl.ds(pl.multiple_of(start, unit), size)


def qkv_blocks(place, pieces, weights, sem):
    chip, core = place[0], place[1]
    for ref, chips, other in pieces:
        half = 1 - core if other else core
        for slot, rel in enumerate(chips):
            rows = aligned((chip ^ rel) * PAIR_ROWS, PAIR_ROWS, 16)
            yield pltpu.make_async_copy(
                ref.at[slot], weights.at[rows, aligned(half * QKV_BLOCK, QKV_BLOCK, 128)], sem
            )


def ffn_blocks(place, pieces, out_w, inner_w, down_w, sem):
    chip, core = place[0], place[1]
    for ref, chips, other in pieces:
        half = 1 - core if other else core
        for slot, rel in enumerate(chips):
            owner = chip ^ rel
            rows = aligned(owner * PAIR_ROWS, PAIR_ROWS, 16)
            start = OUT_HALF + INNER_HALF
            yield pltpu.make_async_copy(
                ref.at[slot, :, pl.ds(0, OUT_HALF)],
                out_w.at[rows, aligned(half * OUT_HALF, OUT_HALF, 128)],
                sem,
            )
            yield pltpu.make_async_copy(
                ref.at[slot, :, pl.ds(OUT_HALF, INNER_HALF)],
                inner_w.at[rows, aligned(half * INNER_HALF, INNER_HALF, 128)],
                sem,
            )
            for i in range(2):
                down_rows = (owner * 2 + half) * (2 * PAIR_ROWS) + i * PAIR_ROWS
                yield pltpu.make_async_copy(
                    ref.at[slot, :, pl.ds(start + i * D, D)],
                    down_w.at[aligned(down_rows, PAIR_ROWS, 16), :],
                    sem,
                )


class ToCore:
    def __init__(self, source, keep, send, sem, other):
        self.source, self.keep, self.send, self.sem, self.other = source, keep, send, sem, other

    def start(self):
        @pl.when(self.other == 0)
        def _():
            pltpu.make_async_copy(self.source, self.keep, self.sem).start()

        @pl.when(self.other == 1)
        def _():
            pltpu.make_async_copy(self.source, self.send, self.sem).start()

    def wait(self):
        pltpu.make_async_copy(self.source, self.keep, self.sem).wait()


def lane_masks():
    low = (lax.broadcasted_iota(jnp.int32, (1, 128), 1) < DH).astype(f32)
    return low.astype(bf16), (1.0 - low).astype(bf16)


def attend_kernel(meta, n_pieces, place, lengths, x_ref, *refs):
    piece_refs = refs[:n_pieces]
    qkv_ref, att_ref, stat_ref, weights, vectors = refs[n_pieces : n_pieces + 5]
    sem = refs[-1]
    seq = pl.program_id(0)
    rows = x_ref.shape[0]

    @pl.when(seq == 0)
    def _():
        copies = list(qkv_blocks(place, [(r,) + m for r, m in zip(piece_refs, meta)], weights, sem))
        for c in copies:
            c.start()
        for c in copies:
            c.wait()
        small = weights[:, QKV_HALF:QKV_BLOCK].astype(f32)
        vectors[...] = small.T[0:16, :]

    lowered = x_ref[...].astype(bf16)
    first = dot(lowered, weights[:, 0:QKV_HALF])
    qkv_ref[:, 0:D] = (first[:, 0:D] + vectors[0:1, :]).astype(bf16)
    qkv_ref[:, D:QKV_HALF] = first[:, D:QKV_HALF].astype(bf16)
    second = dot(lowered, weights[:, QKV_BLOCK : QKV_BLOCK + QKV_HALF])
    qkv_ref[:, QKV_HALF : 2 * D] = second[:, 0 : D // 2].astype(bf16)
    qkv_ref[:, 2 * D :] = (second[:, D // 2 :] + vectors[1:2, :]).astype(bf16)

    low, high = lane_masks()
    lane = lax.broadcasted_iota(jnp.int32, (1, 128), 1)
    key_at = lax.broadcasted_iota(jnp.int32, (1, rows), 1)
    hidden_keys = jnp.where(key_at < lengths[seq], 0.0, MASKED_SCORE).astype(f32)
    chunk = 256
    ones = jnp.ones((rows, 128), bf16)
    stats = [jnp.zeros((chunk, 128), f32) for _ in range(rows // chunk)]
    for pair in range(H // 2):
        at = pair * 128
        keys = qkv_ref[:, D + at : D + at + 128]
        values = jnp.concatenate([qkv_ref[:, 2 * D + at : 2 * D + at + 128], ones], axis=1)
        keys_of = (keys * low, keys * high)
        for c in range(rows // chunk):
            span = pl.ds(c * chunk, chunk)
            queries = qkv_ref[span, at : at + 128]
            outs = []
            for i in range(2):
                scores = dot_t(queries, keys_of[i]) * (0.125 * LOG2E) + hidden_keys
                peak = jnp.max(scores, axis=-1, keepdims=True)
                weight = jnp.exp2(scores - peak).astype(bf16)
                both = dot(weight, values)
                total = both[:, 128:]
                outs.append(both[:, :128] / total)
                log_total = peak + jnp.log2(total)
                stats[c] = jnp.where(lane == 2 * pair + i, log_total, stats[c])
            att_ref[span, at : at + 128] = jnp.where(lane < DH, outs[0], outs[1]).astype(bf16)
    for c in range(rows // chunk):
        stat_ref[0, :, c * chunk : (c + 1) * chunk] = stats[c].T[0:16, :]


def attend(place, lengths, x, pieces, meta):
    rows = x.shape[0] // lengths.shape[0]
    seqs = lengths.shape[0]
    whole = lambda *shape: pl.BlockSpec(shape, lambda s: (0,) * len(shape))
    return pl.pallas_call(
        functools.partial(attend_kernel, meta, len(pieces)),
        grid=(seqs,),
        in_specs=[SMEM, SMEM, pl.BlockSpec((rows, D), lambda s: (s, 0))] + [ANY] * len(pieces),
        out_specs=[
            pl.BlockSpec((rows, 3 * D), lambda s: (s, 0)),
            pl.BlockSpec((rows, D), lambda s: (s, 0)),
            pl.BlockSpec((1, 16, rows), lambda s: (s, 0, 0)),
            whole(D, 2 * QKV_BLOCK),
            whole(16, D),
        ],
        out_shape=[
            jax.ShapeDtypeStruct((seqs * rows, 3 * D), bf16),
            jax.ShapeDtypeStruct((seqs * rows, D), bf16),
            jax.ShapeDtypeStruct((seqs, 16, rows), f32),
            jax.ShapeDtypeStruct((D, 2 * QKV_BLOCK), bf16),
            jax.ShapeDtypeStruct((16, D), f32),
        ],
        scratch_shapes=[pltpu.SemaphoreType.DMA],
        compiler_params=pltpu.CompilerParams(vmem_limit_bytes=56 * MIB),
        cost_estimate=pl.CostEstimate(
            flops=2 * seqs * rows * D * 3 * D, bytes_accessed=20 * MIB, transcendentals=H * seqs * rows * rows
        ),
        name="attend",
    )(place, lengths, x, *pieces)


def gelu_parts(u):
    size = jnp.abs(u)
    bell = jnp.exp2(u * u * (-0.5 * LOG2E))
    t = 1.0 / (1.0 + (0.3275911 * math.sqrt(0.5)) * size)
    poly = t * (0.127414796 + t * (-0.142248368 + t * (0.7107068705 + t * (-0.7265760135 + t * 0.5307027145))))
    tail = poly * bell
    below = jnp.where(u < 0.0, tail, 1.0 - tail)
    return below, bell


def mean_rows(v):
    return jnp.sum(v, axis=-1, keepdims=True) * (1.0 / D)


def norm_rows(total):
    center = total - mean_rows(total)
    rstd = lax.rsqrt(mean_rows(center * center) + NORM_EPSILON)
    return center * rstd, rstd


def norm_back(upstream, normed, rstd, gain):
    scaled = upstream * gain
    return rstd * (scaled - mean_rows(scaled) - normed * mean_rows(scaled * normed))


BLOCK = 256
PAYLOAD_ROWS = 224
DOWN_STEPS = 8
INNER_STEPS = 2


def ffn_kernel(meta, n_pieces, blocks, place, x_ref, att_ref, cot_ref, vec_ref, b1_ref, *refs):
    piece_refs = refs[:n_pieces]
    (out_ref, fb_ref, ab_ref, small_ref, db1_ref, keep, send) = refs[n_pieces : n_pieces + 7]
    (out_w, inner_w, down_w, act, inner_back, hid, down_back, att, branch, slope, grad, stage, sem, wsem) = refs[
        n_pieces + 7 :
    ]
    step = pl.program_id(0)
    me = place[0] * 2 + place[1]
    down_at, inner_at, out_at = blocks, blocks + DOWN_STEPS, blocks + DOWN_STEPS + INNER_STEPS

    @pl.when(step == 0)
    def _():
        copies = list(ffn_blocks(place, [(r,) + m for r, m in zip(piece_refs, meta)], out_w, inner_w, down_w, sem))
        for c in copies:
            c.start()
        for c in copies:
            c.wait()
        small_ref[...] = jnp.zeros_like(small_ref)
        db1_ref[...] = jnp.zeros_like(db1_ref)

    @pl.when(step < blocks)
    def _():
        rows = aligned(step * BLOCK, BLOCK, BLOCK)
        attended = att_ref[...]
        att[rows, :] = attended
        first_gain, first_shift = vec_ref[3:4, :], vec_ref[4:5, :]
        second_gain, second_shift = vec_ref[6:7, :], vec_ref[7:8, :]
        first_normed, first_rstd = norm_rows(x_ref[...] + dot(attended, out_w[...]) + vec_ref[2:3, :])
        hidden = first_normed * first_gain + first_shift
        hidden_low = hidden.astype(bf16)
        hid[rows, :] = hidden_low
        total = hidden + vec_ref[5:6, :]
        for c in range(FF // D):
            cols = pl.ds(c * D, D)
            u = dot(hidden_low, inner_w[:, cols]) + b1_ref[:, cols]
            below, bell = gelu_parts(u)
            active = (u * below).astype(bf16)
            act[rows, cols] = active
            slope[:, cols] = below + u * bell * GAUSS_DENSITY
            total = total + dot(active, down_w[cols, :])
        second_normed, second_rstd = norm_rows(total)
        out_ref[...] = second_normed * second_gain + second_shift
        cot = cot_ref[...]
        second_back = norm_back(cot, second_normed, second_rstd, second_gain)
        back_low = second_back.astype(bf16)
        down_back[rows, :] = back_low
        hidden_back = second_back
        for c in range(FF // D):
            cols = pl.ds(c * D, D)
            ib = (dot_t(back_low, down_w[cols, :]) * slope[:, cols]).astype(bf16)
            inner_back[rows, cols] = ib
            db1_ref[:, cols] += jnp.sum(ib.astype(f32), axis=0, keepdims=True)
            hidden_back = hidden_back + dot_t(ib, inner_w[:, cols])
        first_back = norm_back(hidden_back, first_normed, first_rstd, first_gain)
        fb_ref[...] = first_back
        branch_low = first_back.astype(bf16)
        branch[rows, :] = branch_low
        ab_ref[...] = dot_t(branch_low, out_w[...]).astype(bf16)
        sums = (
            branch_low.astype(f32),
            hidden_back * first_normed,
            hidden_back,
            back_low.astype(f32),
            cot * second_normed,
            cot,
        )
        for i, v in enumerate(sums):
            small_ref[2 + i : 3 + i, :] += jnp.sum(v, axis=0, keepdims=True)

    def store(slab, first_row, count, slot):
        source = stage.at[slot, pl.ds(0, count)]
        place_in = lambda ref: ref.at[(slab ^ me) >> 1, pl.ds(first_row, count)]
        return ToCore(source, place_in(keep), place_in(send), wsem.at[slot], (slab ^ me) & 1)

    @pl.when((step >= down_at) & (step < inner_at))
    def _():
        chunk = step - down_at
        width = FF // DOWN_STEPS
        per = SLABS // DOWN_STEPS
        g = dot_l(act[:, aligned(chunk * width, width, 128)], down_back[...])
        for i in range(per):
            slab = chunk * per + i

            @pl.when(chunk > 0)
            def _():
                store(slab, 0, 4 * SLAB, i).wait()

            stage[i, 0 : 4 * SLAB, :] = g[i * 4 * SLAB : (i + 1) * 4 * SLAB, :].astype(bf16)
            store(slab, 0, 4 * SLAB, i).start()

        @pl.when(chunk == DOWN_STEPS - 1)
        def _():
            for i in range(per):
                store(0, 0, 4 * SLAB, i).wait()

    def pack(first_row, count):
        def body(k, _):
            for i in range(4):
                slab = k * 4 + i

                @pl.when(k > 0)
                def _():
                    store(slab, first_row, count, i).wait()

                rows = aligned(slab * SLAB, SLAB, 8)
                parts = [grad[j, rows, :] for j in range(2)]
                stage[i, 0:count, :] = jnp.concatenate(parts, axis=0)[0:count].astype(bf16)
                store(slab, first_row, count, i).start()
            return 0

        lax.fori_loop(0, SLABS // 4, body, 0)
        for i in range(4):
            store(0, first_row, count, i).wait()

    @pl.when((step >= inner_at) & (step < out_at))
    def _():
        half = step - inner_at
        for j in range(2):
            grad[j] = dot_l(hid[...], inner_back[:, aligned(half * 2 * D + j * D, D, 128)])
        pack(4 * SLAB + half * 2 * SLAB, 2 * SLAB)

    @pl.when(step == out_at)
    def _():
        grad[0] = dot_l(att[...], branch[...])
        grad[1] = jnp.zeros((D, D), f32)
        pack(8 * SLAB, 32)


def feed_forward(place, x, attended, cotangent, vectors, inner_bias, pieces, meta):
    count = x.shape[0]
    blocks = count // BLOCK
    last = blocks - 1
    token = lambda: pl.BlockSpec((BLOCK, D), lambda s: (jnp.minimum(s, last), 0))
    whole = lambda *shape: pl.BlockSpec(shape, lambda s: (0,) * len(shape))
    return pl.pallas_call(
        functools.partial(ffn_kernel, meta, len(pieces), blocks),
        grid=(blocks + DOWN_STEPS + INNER_STEPS + 1,),
        in_specs=[SMEM, token(), token(), token(), whole(16, D), whole(1, FF)] + [ANY] * len(pieces),
        out_specs=[token(), token(), token(), whole(8, D), whole(1, FF), ANY, ANY],
        out_shape=[
            jax.ShapeDtypeStruct((count, D), f32),
            jax.ShapeDtypeStruct((count, D), f32),
            jax.ShapeDtypeStruct((count, D), bf16),
            jax.ShapeDtypeStruct((8, D), f32),
            jax.ShapeDtypeStruct((1, FF), f32),
            jax.ShapeDtypeStruct((CHIPS, PAYLOAD_ROWS, D), bf16),
            jax.ShapeDtypeStruct((CHIPS, PAYLOAD_ROWS, D), bf16),
        ],
        scratch_shapes=[
            pltpu.VMEM((D, D), bf16),
            pltpu.VMEM((D, FF), bf16),
            pltpu.VMEM((FF, D), bf16),
            pltpu.VMEM((count, FF), bf16),
            pltpu.VMEM((count, FF), bf16),
            pltpu.VMEM((count, D), bf16),
            pltpu.VMEM((count, D), bf16),
            pltpu.VMEM((count, D), bf16),
            pltpu.VMEM((count, D), bf16),
            pltpu.VMEM((BLOCK, FF), f32),
            pltpu.VMEM((2, D, D), f32),
            pltpu.VMEM((4, 4 * SLAB, D), bf16),
            pltpu.SemaphoreType.DMA,
            pltpu.SemaphoreType.DMA((4,)),
        ],
        compiler_params=pltpu.CompilerParams(vmem_limit_bytes=62 * MIB),
        cost_estimate=pl.CostEstimate(
            flops=12 * count * D * FF + 6 * count * D * D, bytes_accessed=40 * MIB, transcendentals=2 * count * FF
        ),
        name="feed_forward",
    )(place, x, attended, cotangent, vectors, inner_bias, *pieces)


def attend_back_kernel(seqs, place, lengths, x_ref, qkv_ref, back_ref, stat_ref, small_ref, db1_ref, *refs):
    (grads_out, keep, send, grads, lowered, grad, stage, sem, wsem) = refs
    step = pl.program_id(0)
    pairs = H // 2
    rows = x_ref.shape[0]
    me = place[0] * 2 + place[1]
    low, high = lane_masks()
    chunk = 256

    @pl.when(step < seqs * pairs)
    def _():
        seq, pair = step // pairs, step % pairs
        at = pair * 128

        @pl.when(pair == 0)
        def _():
            lowered[aligned(seq * rows, rows, rows), :] = x_ref[...].astype(bf16)

        queries = qkv_ref[:, aligned(at, 128, 128)]
        keys = qkv_ref[:, aligned(D + at, 128, 128)]
        values = qkv_ref[:, aligned(2 * D + at, 128, 128)]
        upstream = back_ref[:, aligned(at, 128, 128)]
        key_at = lax.broadcasted_iota(jnp.int32, (rows, 1), 0)
        hidden_keys = jnp.where(key_at < lengths[seq], 0.0, MASKED_SCORE).astype(f32)
        query_back = [jnp.zeros((chunk, 128), f32) for _ in range(rows // chunk)]
        key_back = jnp.zeros((rows, 128), f32)
        value_back = jnp.zeros((rows, 128), f32)
        for i, mask in enumerate((low, high)):
            own_keys, own_values = keys * mask, values * mask
            own_queries, own_up = queries * mask, upstream * mask
            for c in range(rows // chunk):
                span = slice(c * chunk, (c + 1) * chunk)
                log_total = stat_ref[0, pl.ds(2 * pair + i, 1), span]
                scores = dot_t(own_keys, queries[span]) * (0.125 * LOG2E) + hidden_keys
                weight = jnp.exp2(scores - log_total)
                weight_back = dot_t(own_values, upstream[span])
                mean = jnp.sum(weight * weight_back, axis=0, keepdims=True)
                score_back = (weight * (weight_back - mean)).astype(bf16)
                value_back += dot(weight.astype(bf16), own_up[span])
                key_back += dot(score_back, own_queries[span])
                query_back[c] += dot_l(score_back, own_keys)
        to = seq * rows
        for c in range(rows // chunk):
            grads[aligned(to + c * chunk, chunk, chunk), aligned(at, 128, 128)] = (query_back[c] * 0.125).astype(bf16)
        grads[aligned(to, rows, rows), aligned(D + at, 128, 128)] = (key_back * 0.125).astype(bf16)
        grads[aligned(to, rows, rows), aligned(2 * D + at, 128, 128)] = value_back.astype(bf16)

    whole_copy = pltpu.make_async_copy(grads, grads_out, sem)

    @pl.when(step == seqs * pairs)
    def _():
        whole_copy.start()

    @pl.when(step >= seqs * pairs)
    def _():
        which = step - seqs * pairs
        grad[which] = dot_l(lowered[...], grads[:, aligned(which * D, D, 128)])

    def store(slab, slot):
        rel = slab ^ me
        return ToCore(stage.at[slot], keep.at[rel >> 1], send.at[rel >> 1], wsem.at[slot], rel & 1)

    @pl.when(step == seqs * pairs + 2)
    def _():
        query_bias = jnp.sum(grads[:, 0:D].astype(f32), axis=0, keepdims=True)
        value_bias = jnp.sum(grads[:, 2 * D :].astype(f32), axis=0, keepdims=True)
        rows_of = jnp.concatenate([query_bias, value_bias, small_ref[2:8, :], jnp.zeros((120, D), f32)], axis=0)
        columns = rows_of.T
        owner = lax.broadcasted_iota(jnp.int32, (SLABS, FF), 1) // (4 * SLAB)
        mine = jnp.where(owner == lax.broadcasted_iota(jnp.int32, (SLABS, FF), 0), db1_ref[...], 0.0)
        place_of = lax.broadcasted_iota(jnp.int32, (FF, 128), 0) % (4 * SLAB)
        pick = (place_of == lax.broadcasted_iota(jnp.int32, (FF, 128), 1)).astype(f32)
        table = lax.dot_general(
            mine, pick, (((1,), (0,)), ((), ())), precision=lax.Precision.HIGHEST, preferred_element_type=f32
        )
        for slab in range(SLABS):
            slot = slab % 4
            if slab >= 4:
                store(slab, slot).wait()
            at = slab * SLAB
            lanes = [columns[at + 8 * i : at + 8 * i + 8, :] for i in range(3)]
            lanes.append(jnp.broadcast_to(table[slab : slab + 1, :], (8, 128)))
            lanes.append(jnp.zeros((8, 256), f32))
            parts = [grad[j, at : at + SLAB, :] for j in range(3)] + [jnp.concatenate(lanes, axis=1)]
            stage[slot] = jnp.concatenate(parts, axis=0).astype(bf16)
            store(slab, slot).start()
        for slot in range(4):
            store(0, slot).wait()
        whole_copy.wait()


def attend_back(place, lengths, x, qkv, back, stats, small, inner_bias_grad):
    seqs = lengths.shape[0]
    rows = x.shape[0] // seqs
    pairs = H // 2
    seq_of = lambda s: jnp.minimum(s // pairs, seqs - 1)
    whole = lambda *shape: pl.BlockSpec(shape, lambda s: (0,) * len(shape))
    return pl.pallas_call(
        functools.partial(attend_back_kernel, seqs),
        grid=(seqs * pairs + 3,),
        in_specs=[
            SMEM,
            SMEM,
            pl.BlockSpec((rows, D), lambda s: (seq_of(s), 0)),
            pl.BlockSpec((rows, 3 * D), lambda s: (seq_of(s), 0)),
            pl.BlockSpec((rows, D), lambda s: (seq_of(s), 0)),
            pl.BlockSpec((1, 16, rows), lambda s: (seq_of(s), 0, 0)),
            whole(8, D),
            whole(1, FF),
        ],
        out_specs=[ANY, ANY, ANY],
        out_shape=[
            jax.ShapeDtypeStruct((seqs * rows, 3 * D), bf16),
            jax.ShapeDtypeStruct((CHIPS, 80, D), bf16),
            jax.ShapeDtypeStruct((CHIPS, 80, D), bf16),
        ],
        scratch_shapes=[
            pltpu.VMEM((seqs * rows, 3 * D), bf16),
            pltpu.VMEM((seqs * rows, D), bf16),
            pltpu.VMEM((3, D, D), f32),
            pltpu.VMEM((4, 80, D), bf16),
            pltpu.SemaphoreType.DMA,
            pltpu.SemaphoreType.DMA((4,)),
        ],
        compiler_params=pltpu.CompilerParams(vmem_limit_bytes=56 * MIB),
        cost_estimate=pl.CostEstimate(
            flops=2 * seqs * rows * D * 3 * D, bytes_accessed=30 * MIB, transcendentals=H * seqs * rows * rows
        ),
        name="attend_back",
    )(place, lengths, x, qkv, back, stats, small, inner_bias_grad)


def input_back_kernel(fb_ref, grads_ref, w_ref, out_ref):
    half = D + D // 2
    first = dot_t(grads_ref[:, 0:half], w_ref[:, 0:half])
    second = dot_t(grads_ref[:, half:], w_ref[:, QKV_BLOCK : QKV_BLOCK + half])
    out_ref[...] = fb_ref[...] + first + second


def input_back(first_back, grads, weights):
    count = first_back.shape[0]
    return pl.pallas_call(
        input_back_kernel,
        grid=(count // BLOCK,),
        in_specs=[
            pl.BlockSpec((BLOCK, D), lambda s: (s, 0)),
            pl.BlockSpec((BLOCK, 3 * D), lambda s: (s, 0)),
            pl.BlockSpec((D, 2 * QKV_BLOCK), lambda s: (0, 0)),
        ],
        out_specs=pl.BlockSpec((BLOCK, D), lambda s: (s, 0)),
        out_shape=jax.ShapeDtypeStruct((count, D), f32),
        compiler_params=pltpu.CompilerParams(vmem_limit_bytes=56 * MIB),
        cost_estimate=pl.CostEstimate(flops=6 * count * D * D, bytes_accessed=15 * MIB, transcendentals=0),
        name="input_back",
    )(first_back, grads, weights)


AXES = ("dp", "fsdp")


def swap(v, mask, count):
    return lax.ppermute(v, AXES, [(i, i ^ mask) for i in range(count)])


CORE, ALONG_X, ALONG_Y, ALONG_Z = 1, 2, 4, 8
Z_COUNT = 4
FAST_SHAPE = {"dp": Z_COUNT, "fsdp": 8}


def gather_group(block):
    move = lambda v, mask: swap(v, mask, SLABS)
    per_z = [block] + [move(block, k * ALONG_Z) for k in range(1, Z_COUNT)]
    first, second = jnp.stack(per_z[:2]), jnp.stack(per_z[2:])
    first_chips, second_chips = (0, 4), (8, 12)
    shift = lambda chips, by: tuple(c ^ by for c in chips)
    first = jnp.concatenate([first, move(first, ALONG_X)])
    second = jnp.concatenate([second, move(second, ALONG_Y)])
    first_chips += shift(first_chips, 1)
    second_chips += shift(second_chips, 2)
    held = [
        (first, first_chips),
        (second, second_chips),
        (move(first, ALONG_Y), shift(first_chips, 2)),
        (move(second, ALONG_X), shift(second_chips, 1)),
    ]
    arrays = [a for a, _ in held] + [move(a, CORE) for a, _ in held]
    meta = tuple((c, False) for _, c in held) + tuple((c, True) for _, c in held)
    return arrays, meta


def scatter_group(keep, send):
    move = lambda v, mask: swap(v, mask, SLABS)
    wide = lambda v: v.astype(f32)
    shape = (Z_COUNT, 2, 2) + keep.shape[1:]
    got = move(send, CORE).reshape(shape)
    keep = keep.reshape(shape)
    chip = lambda z, y, x: wide(keep[z, y, x]) + wide(got[z, y, x])
    low, high = slice(0, 2), slice(2, 4)
    every = slice(None)
    first = move(chip(low, 1, every).astype(bf16), ALONG_Y)
    second = move(chip(high, every, 1).astype(bf16), ALONG_X)
    first_sum = lambda x: chip(low, 0, x) + wide(first[:, x])
    second_sum = lambda y: chip(high, y, 0) + wide(second[:, y])
    first_more = move(first_sum(1).astype(bf16), ALONG_X)
    second_more = move(second_sum(1).astype(bf16), ALONG_Y)
    low_part = first_sum(0) + wide(first_more)
    high_part = second_sum(0) + wide(second_more)
    parts = [low_part[0], low_part[1], high_part[0], high_part[1]]
    total = parts[0]
    for k in range(1, Z_COUNT):
        total = total + wide(move(parts[k].astype(bf16), k * ALONG_Z))
    return total


def gather_fast(shards, linear):
    (qw, kw, vw, ow, qb, vb, ob, fg, fs, iw, ib, dw, db, sg, ss) = shards
    core = linear & 1
    vectors = jnp.pad(jnp.stack([qb, vb, ob, fg, fs, db, sg, ss], axis=1), ((0, 0), (0, 120)))
    inner_bias = jnp.pad(ib.reshape(1, 4 * SLAB), ((0, SLAB - 1), (0, 128 - 4 * SLAB)))
    half = D // 2
    halves = [
        jnp.concatenate([qw, kw[:, :half], vectors, ow[:, :half], iw[:, :INNER_HALF]], axis=1),
        jnp.concatenate([kw[:, half:], vw, inner_bias, ow[:, half:], iw[:, INNER_HALF:]], axis=1),
    ]
    low_core = core == 0
    own = jnp.where(low_core, halves[0], halves[1])
    other = swap(jnp.where(low_core, halves[1], halves[0]), CORE, SLABS)
    rows = jnp.concatenate([jnp.where(low_core, own, other), jnp.where(low_core, other, own)], axis=0)
    qkv_block = rows[:, :QKV_BLOCK]
    ffn_block = jnp.concatenate([rows[:, QKV_BLOCK:], dw[:PAIR_ROWS], dw[PAIR_ROWS:]], axis=1)
    return gather_group(qkv_block), gather_group(ffn_block)


def gather_plain(shards):
    (qw, kw, vw, ow, qb, vb, ob, fg, fs, iw, ib, dw, db, sg, ss) = [
        lax.all_gather(v, AXES, axis=0, tiled=True) for v in shards
    ]
    vectors = jnp.pad(jnp.stack([qb, vb, ob, fg, fs, db, sg, ss], axis=1), ((0, 0), (0, 120)))
    inner_bias = jnp.pad(ib.reshape(SLABS, 1, 4 * SLAB), ((0, 0), (0, SLAB - 1), (0, 128 - 4 * SLAB))).reshape(D, 128)
    half = D // 2
    chips = lambda v: v.reshape(CHIPS, PAIR_ROWS, -1)
    down = dw.reshape(CHIPS, 2, 2, PAIR_ROWS, D)
    first = [
        chips(jnp.concatenate([qw, kw[:, :half], vectors], axis=1)),
        chips(jnp.concatenate([kw[:, half:], vw, inner_bias], axis=1)),
    ]
    second = [
        jnp.concatenate(
            [
                chips(ow[:, c * half : (c + 1) * half]),
                chips(iw[:, c * INNER_HALF : (c + 1) * INNER_HALF]),
                down[:, c, 0],
                down[:, c, 1],
            ],
            axis=2,
        )
        for c in range(2)
    ]
    meta = ((tuple(range(CHIPS)), False), (tuple(range(CHIPS)), True))
    return (first, meta), (second, meta)


def local(fast, inputs, lengths, *rest):
    shards, cotangent = rest[:15], rest[15]
    if fast:
        linear = lax.axis_index(AXES)
        place = jnp.stack([linear >> 1, linear & 1]).astype(jnp.int32)
        (first, first_meta), (second, second_meta) = gather_fast(shards, linear)
    else:
        place = jnp.zeros((2,), jnp.int32)
        (first, first_meta), (second, second_meta) = gather_plain(shards)
    qkv, attended, stats, weights, vectors = attend(place, lengths, inputs, first, first_meta)
    inner_bias = weights[::SLAB, QKV_BLOCK + QKV_HALF : QKV_BLOCK + QKV_HALF + 4 * SLAB].reshape(1, FF).astype(f32)
    output, first_back, back, small, db1, ffn_keep, ffn_send = feed_forward(
        place, inputs, attended, cotangent, vectors, inner_bias, second, second_meta
    )
    grads, qkv_keep, qkv_send = attend_back(place, lengths, inputs, qkv, back, stats, small, db1)
    grad_input = input_back(first_back, grads, weights)
    if fast:
        ffn = scatter_group(ffn_keep, ffn_send)[None]
        proj = scatter_group(qkv_keep, qkv_send)[None]
    else:
        ffn, proj = (
            jnp.stack(pair, axis=1).reshape((SLABS,) + pair[0].shape[1:]).astype(f32)
            for pair in ((ffn_keep, ffn_send), (qkv_keep, qkv_send))
        )
    count = ffn.shape[0]
    shard = lambda v: v if fast else lax.psum_scatter(v, AXES, scatter_dimension=0, tiled=True)
    square = lambda i: shard(proj[:, SLAB * i : SLAB * (i + 1)].reshape(count * SLAB, D))
    tail = proj[:, 3 * SLAB :].reshape(count, 8, D // 128, 128)
    columns = jnp.swapaxes(tail[:, :, :3], 1, 2).reshape(count * SLAB, 128)
    vec = lambda i: shard(columns[:, i])
    inner_bias_grad = shard(tail[:, 0, 3, : 4 * SLAB].reshape(count * 4 * SLAB))
    down_grad = shard(ffn[:, : 4 * SLAB].reshape(count * 4 * SLAB, D))
    inner_grad = shard(
        jnp.swapaxes(ffn[:, 4 * SLAB : 8 * SLAB].reshape(count, 4, SLAB, D), 1, 2).reshape(count * SLAB, FF)
    )
    out_grad = shard(ffn[:, 8 * SLAB : 9 * SLAB].reshape(count * SLAB, D))
    return (
        output,
        grad_input,
        square(0),
        square(1),
        square(2),
        out_grad,
        vec(0),
        vec(1),
        vec(2),
        vec(3),
        vec(4),
        inner_grad,
        inner_bias_grad,
        down_grad,
        vec(5),
        vec(6),
        vec(7),
    )


def solution(mesh):
    rows, flat = P(AXES, None), P(AXES)
    params = (rows,) * 4 + (flat,) * 5 + (rows, flat, rows, flat, flat, flat)
    return jax.shard_map(
        functools.partial(local, dict(mesh.shape) == FAST_SHAPE),
        mesh=mesh,
        in_specs=(rows, flat) + params + (rows,),
        out_specs=(rows, rows) + params,
        check_vma=False,
    )
```

```python
import functools
import math

import jax
import jax.numpy as jnp
from jax import lax
from jax.experimental import pallas as pl
from jax.experimental.pallas import tpu as pltpu
from jax.sharding import PartitionSpec as P

D = 768
H = 12
DH = 64
FF = 3072
SLABS = 32
SLAB = D // SLABS
CHIPS = SLABS // 2
PAIR_ROWS = 2 * SLAB
NORM_EPSILON = 1e-12
MASKED_SCORE = -1000000000.0
GAUSS_DENSITY = 0.3989422804014327
LOG2E = 1.4426950408889634
MIB = 1 << 20

QKV_HALF = 3 * D // 2
QKV_BLOCK = QKV_HALF + 128
OUT_HALF = D // 2
INNER_HALF = FF // 2
FFN_BLOCK = OUT_HALF + INNER_HALF + 2 * D

bf16 = jnp.bfloat16
f32 = jnp.float32
ANY = pl.BlockSpec(memory_space=pl.ANY)
SMEM = pl.BlockSpec(memory_space=pltpu.SMEM)


def dot(a, b):
    return lax.dot_general(a, b, (((1,), (0,)), ((), ())), preferred_element_type=f32)


def dot_t(a, b):
    return lax.dot_general(a, b, (((1,), (1,)), ((), ())), preferred_element_type=f32)


def dot_l(a, b):
    return lax.dot_general(a, b, (((0,), (0,)), ((), ())), preferred_element_type=f32)


def aligned(start, size, unit):
    return pl.ds(pl.multiple_of(start, unit), size)


def qkv_blocks(place, pieces, weights, sem):
    chip, core = place[0], place[1]
    for ref, chips, other in pieces:
        half = 1 - core if other else core
        for slot, rel in enumerate(chips):
            rows = aligned((chip ^ rel) * PAIR_ROWS, PAIR_ROWS, 16)
            yield pltpu.make_async_copy(
                ref.at[slot], weights.at[rows, aligned(half * QKV_BLOCK, QKV_BLOCK, 128)], sem
            )


def ffn_blocks(place, pieces, out_w, inner_w, down_w, sem):
    chip, core = place[0], place[1]
    for ref, chips, other in pieces:
        half = 1 - core if other else core
        for slot, rel in enumerate(chips):
            owner = chip ^ rel
            rows = aligned(owner * PAIR_ROWS, PAIR_ROWS, 16)
            start = OUT_HALF + INNER_HALF
            yield pltpu.make_async_copy(
                ref.at[slot, :, pl.ds(0, OUT_HALF)],
                out_w.at[rows, aligned(half * OUT_HALF, OUT_HALF, 128)],
                sem.at[0],
            )
            yield pltpu.make_async_copy(
                ref.at[slot, :, pl.ds(OUT_HALF, INNER_HALF)],
                inner_w.at[rows, aligned(half * INNER_HALF, INNER_HALF, 128)],
                sem.at[1],
            )
            for i in range(2):
                down_rows = (owner * 2 + half) * (2 * PAIR_ROWS) + i * PAIR_ROWS
                yield pltpu.make_async_copy(
                    ref.at[slot, :, pl.ds(start + i * D, D)],
                    down_w.at[aligned(down_rows, PAIR_ROWS, 16), :],
                    sem.at[2],
                )


def hand_over(place, chip, half, keep, send, pairs, sem):
    slot = chip ^ place[0]
    for mine, out in ((True, keep), (False, send)):

        @pl.when((place[1] == half) == mine)
        def _():
            for source, lanes in pairs:
                pltpu.make_async_copy(source, out.at[slot, :, lanes], sem).start()


def wait_whole(ref, sem):
    pltpu.make_async_copy(ref, ref, sem).wait()


def lane_masks():
    low = (lax.broadcasted_iota(jnp.int32, (1, 128), 1) < DH).astype(f32)
    return low.astype(bf16), (1.0 - low).astype(bf16)


def attend_kernel(meta, n_pieces, place, lengths, x_ref, *refs):
    piece_refs = refs[:n_pieces]
    qkv_ref, att_ref, stat_ref, weights, vectors = refs[n_pieces : n_pieces + 5]
    sem = refs[-1]
    seq = pl.program_id(0)
    rows = x_ref.shape[0]

    @pl.when(seq == 0)
    def _():
        copies = list(qkv_blocks(place, [(r,) + m for r, m in zip(piece_refs, meta)], weights, sem))
        for c in copies:
            c.start()
        for c in copies:
            c.wait()
        small = weights[:, QKV_HALF:QKV_BLOCK].astype(f32)
        vectors[...] = small.T[0:16, :]

    lowered = x_ref[...].astype(bf16)
    first = dot(lowered, weights[:, 0:QKV_HALF])
    qkv_ref[:, 0:D] = (first[:, 0:D] + vectors[0:1, :]).astype(bf16)
    qkv_ref[:, D:QKV_HALF] = first[:, D:QKV_HALF].astype(bf16)
    second = dot(lowered, weights[:, QKV_BLOCK : QKV_BLOCK + QKV_HALF])
    qkv_ref[:, QKV_HALF : 2 * D] = second[:, 0 : D // 2].astype(bf16)
    qkv_ref[:, 2 * D :] = (second[:, D // 2 :] + vectors[1:2, :]).astype(bf16)

    low, high = lane_masks()
    lane = lax.broadcasted_iota(jnp.int32, (1, 128), 1)
    key_at = lax.broadcasted_iota(jnp.int32, (1, rows), 1)
    hidden_keys = jnp.where(key_at < lengths[seq], 0.0, MASKED_SCORE).astype(f32)
    chunk = 256
    ones = jnp.ones((rows, 128), bf16)
    stats = [jnp.zeros((chunk, 128), f32) for _ in range(rows // chunk)]
    for pair in range(H // 2):
        at = pair * 128
        keys = qkv_ref[:, D + at : D + at + 128]
        values = jnp.concatenate([qkv_ref[:, 2 * D + at : 2 * D + at + 128], ones], axis=1)
        keys_of = (keys * low, keys * high)
        for c in range(rows // chunk):
            span = pl.ds(c * chunk, chunk)
            queries = qkv_ref[span, at : at + 128]
            outs = []
            for i in range(2):
                scores = dot_t(queries, keys_of[i]) * (0.125 * LOG2E) + hidden_keys
                peak = jnp.max(scores, axis=-1, keepdims=True)
                weight = jnp.exp2(scores - peak).astype(bf16)
                both = dot(weight, values)
                total = both[:, 128:]
                outs.append(both[:, :128] / total)
                log_total = peak + jnp.log2(total)
                stats[c] = jnp.where(lane == 2 * pair + i, log_total, stats[c])
            att_ref[span, at : at + 128] = jnp.where(lane < DH, outs[0], outs[1]).astype(bf16)
    for c in range(rows // chunk):
        stat_ref[0, :, c * chunk : (c + 1) * chunk] = stats[c].T[0:16, :]


def attend(place, lengths, x, pieces, meta):
    rows = x.shape[0] // lengths.shape[0]
    seqs = lengths.shape[0]
    whole = lambda *shape: pl.BlockSpec(shape, lambda s: (0,) * len(shape))
    return pl.pallas_call(
        functools.partial(attend_kernel, meta, len(pieces)),
        grid=(seqs,),
        in_specs=[SMEM, SMEM, pl.BlockSpec((rows, D), lambda s: (s, 0))] + [ANY] * len(pieces),
        out_specs=[
            pl.BlockSpec((rows, 3 * D), lambda s: (s, 0)),
            pl.BlockSpec((rows, D), lambda s: (s, 0)),
            pl.BlockSpec((1, 16, rows), lambda s: (s, 0, 0)),
            whole(D, 2 * QKV_BLOCK),
            whole(16, D),
        ],
        out_shape=[
            jax.ShapeDtypeStruct((seqs * rows, 3 * D), bf16),
            jax.ShapeDtypeStruct((seqs * rows, D), bf16),
            jax.ShapeDtypeStruct((seqs, 16, rows), f32),
            jax.ShapeDtypeStruct((D, 2 * QKV_BLOCK), bf16),
            jax.ShapeDtypeStruct((16, D), f32),
        ],
        scratch_shapes=[pltpu.SemaphoreType.DMA],
        compiler_params=pltpu.CompilerParams(vmem_limit_bytes=56 * MIB),
        cost_estimate=pl.CostEstimate(flops=18_000_000_000, bytes_accessed=20 * MIB, transcendentals=0),
        name="attend",
    )(place, lengths, x, *pieces)


def gelu_parts(u):
    size = jnp.abs(u)
    bell = jnp.exp2(u * u * (-0.5 * LOG2E))
    t = 1.0 / (1.0 + (0.3275911 * math.sqrt(0.5)) * size)
    poly = t * (0.127414796 + t * (-0.142248368 + t * (0.7107068705 + t * (-0.7265760135 + t * 0.5307027145))))
    tail = poly * bell
    below = jnp.where(u < 0.0, tail, 1.0 - tail)
    return below, bell


def mean_rows(v):
    return jnp.sum(v, axis=-1, keepdims=True) * (1.0 / D)


def norm_rows(total):
    center = total - mean_rows(total)
    rstd = lax.rsqrt(mean_rows(center * center) + NORM_EPSILON)
    return center * rstd, rstd


def norm_back(upstream, normed, rstd, gain):
    scaled = upstream * gain
    return rstd * (scaled - mean_rows(scaled) - normed * mean_rows(scaled * normed))


BLOCK = 256
DOWN_STEPS = 8
INNER_STEPS = 4


def ffn_kernel(meta, n_pieces, blocks, place, x_ref, att_ref, cot_ref, vec_ref, b1_ref, *refs):
    piece_refs = refs[:n_pieces]
    (out_ref, fb_ref, ab_ref, small_ref, db1_ref, keep, send) = refs[n_pieces : n_pieces + 7]
    (out_w, inner_w, down_w, act, inner_back, hid, down_back, att, branch, slope, sem, wsem) = refs[
        n_pieces + 7 :
    ]
    step = pl.program_id(0)
    down_at, inner_at, out_at = blocks, blocks + DOWN_STEPS, blocks + DOWN_STEPS + INNER_STEPS

    @pl.when(step == 0)
    def _():
        copies = list(ffn_blocks(place, [(r,) + m for r, m in zip(piece_refs, meta)], out_w, inner_w, down_w, sem))
        for c in copies:
            c.start()
        small_ref[...] = jnp.zeros_like(small_ref)
        db1_ref[...] = jnp.zeros_like(db1_ref)

    @pl.when(step < blocks)
    def _():
        rows = aligned(step * BLOCK, BLOCK, BLOCK)

        @pl.when(step == 0)
        def _():
            wait_whole(out_w, sem.at[0])

        attended = att_ref[...]
        att[rows, :] = attended
        first_gain, first_shift = vec_ref[3:4, :], vec_ref[4:5, :]
        second_gain, second_shift = vec_ref[6:7, :], vec_ref[7:8, :]
        first_normed, first_rstd = norm_rows(x_ref[...] + dot(attended, out_w[...]) + vec_ref[2:3, :])
        hidden = first_normed * first_gain + first_shift
        hidden_low = hidden.astype(bf16)
        hid[rows, :] = hidden_low
        total = hidden + vec_ref[5:6, :]

        @pl.when(step == 0)
        def _():
            wait_whole(inner_w, sem.at[1])
            wait_whole(down_w, sem.at[2])

        for c in range(FF // D):
            cols = pl.ds(c * D, D)
            u = dot(hidden_low, inner_w[:, cols]) + b1_ref[:, cols]
            below, bell = gelu_parts(u)
            active = (u * below).astype(bf16)
            act[rows, cols] = active
            slope[:, cols] = below + u * bell * GAUSS_DENSITY
            total = total + dot(active, down_w[cols, :])
        second_normed, second_rstd = norm_rows(total)
        out_ref[...] = second_normed * second_gain + second_shift
        cot = cot_ref[...]
        second_back = norm_back(cot, second_normed, second_rstd, second_gain)
        back_low = second_back.astype(bf16)
        down_back[rows, :] = back_low
        hidden_back = second_back
        for c in range(FF // D):
            cols = pl.ds(c * D, D)
            ib = (dot_t(back_low, down_w[cols, :]) * slope[:, cols]).astype(bf16)
            inner_back[rows, cols] = ib
            db1_ref[:, cols] += jnp.sum(ib.astype(f32), axis=0, keepdims=True)
            hidden_back = hidden_back + dot_t(ib, inner_w[:, cols])
        first_back = norm_back(hidden_back, first_normed, first_rstd, first_gain)
        fb_ref[...] = first_back
        branch_low = first_back.astype(bf16)
        branch[rows, :] = branch_low
        ab_ref[...] = dot_t(branch_low, out_w[...]).astype(bf16)
        sums = (
            branch_low.astype(f32),
            hidden_back * first_normed,
            hidden_back,
            back_low.astype(f32),
            cot * second_normed,
            cot,
        )
        for i, v in enumerate(sums):
            small_ref[2 + i : 3 + i, :] += jnp.sum(v, axis=0, keepdims=True)

    @pl.when((step >= down_at) & (step < inner_at))
    def _():
        chunk = step - down_at
        width = FF // DOWN_STEPS
        rows = aligned(chunk * width, width, 128)
        down_w[rows, :] = dot_l(act[:, rows], down_back[...]).astype(bf16)
        for i in range(CHIPS // DOWN_STEPS):
            chip = chunk * (CHIPS // DOWN_STEPS) + i
            for half in range(2):
                at = (chip * 2 + half) * (2 * PAIR_ROWS)
                pairs = [
                    (down_w.at[aligned(at + k * PAIR_ROWS, PAIR_ROWS, 16)], pl.ds(OUT_HALF + INNER_HALF + k * D, D))
                    for k in range(2)
                ]
                hand_over(place, chip, half, keep, send, pairs, wsem)

    def give(weights, half, width, lane):
        for chip in range(CHIPS):
            block = weights.at[pl.ds(chip * PAIR_ROWS, PAIR_ROWS), pl.ds(half * width, width)]
            hand_over(place, chip, half, keep, send, [(block, pl.ds(lane, width))], wsem)

    @pl.when((step >= inner_at) & (step < out_at))
    def _():
        cols = aligned((step - inner_at) * D, D, 128)
        inner_w[:, cols] = dot_l(hid[...], inner_back[:, cols]).astype(bf16)
        for half in range(2):

            @pl.when(step == inner_at + 2 * half + 1)
            def _():
                give(inner_w, half, INNER_HALF, OUT_HALF)

    @pl.when(step == out_at)
    def _():
        out_w[...] = dot_l(att[...], branch[...]).astype(bf16)
        for half in range(2):
            give(out_w, half, OUT_HALF, 0)
        wait_whole(keep, wsem)
        wait_whole(send, wsem)


def feed_forward(place, x, attended, cotangent, vectors, inner_bias, pieces, meta):
    count = x.shape[0]
    blocks = count // BLOCK
    last = blocks - 1
    token = lambda: pl.BlockSpec((BLOCK, D), lambda s: (jnp.minimum(s, last), 0))
    whole = lambda *shape: pl.BlockSpec(shape, lambda s: (0,) * len(shape))
    return pl.pallas_call(
        functools.partial(ffn_kernel, meta, len(pieces), blocks),
        grid=(blocks + DOWN_STEPS + INNER_STEPS + 1,),
        in_specs=[SMEM, token(), token(), token(), whole(16, D), whole(1, FF)] + [ANY] * len(pieces),
        out_specs=[token(), token(), token(), whole(8, D), whole(1, FF), ANY, ANY],
        out_shape=[
            jax.ShapeDtypeStruct((count, D), f32),
            jax.ShapeDtypeStruct((count, D), f32),
            jax.ShapeDtypeStruct((count, D), bf16),
            jax.ShapeDtypeStruct((8, D), f32),
            jax.ShapeDtypeStruct((1, FF), f32),
            jax.ShapeDtypeStruct((CHIPS, PAIR_ROWS, FFN_BLOCK), bf16),
            jax.ShapeDtypeStruct((CHIPS, PAIR_ROWS, FFN_BLOCK), bf16),
        ],
        scratch_shapes=[
            pltpu.VMEM((D, D), bf16),
            pltpu.VMEM((D, FF), bf16),
            pltpu.VMEM((FF, D), bf16),
            pltpu.VMEM((count, FF), bf16),
            pltpu.VMEM((count, FF), bf16),
            pltpu.VMEM((count, D), bf16),
            pltpu.VMEM((count, D), bf16),
            pltpu.VMEM((count, D), bf16),
            pltpu.VMEM((count, D), bf16),
            pltpu.VMEM((BLOCK, FF), f32),
            pltpu.SemaphoreType.DMA((3,)),
            pltpu.SemaphoreType.DMA,
        ],
        compiler_params=pltpu.CompilerParams(vmem_limit_bytes=62 * MIB),
        cost_estimate=pl.CostEstimate(flops=60_000_000_000, bytes_accessed=40 * MIB, transcendentals=0),
        name="feed_forward",
    )(place, x, attended, cotangent, vectors, inner_bias, *pieces)


def attend_back_pair(seq, pair, to, lengths, qkv_ref, back_ref, stat_ref, grads):
    rows = qkv_ref.shape[0]
    chunk = 256
    low, high = lane_masks()
    at = pair * 128
    queries = qkv_ref[:, aligned(at, 128, 128)]
    keys = qkv_ref[:, aligned(D + at, 128, 128)]
    values = qkv_ref[:, aligned(2 * D + at, 128, 128)]
    upstream = back_ref[:, aligned(at, 128, 128)]
    key_at = lax.broadcasted_iota(jnp.int32, (rows, 1), 0)
    hidden_keys = jnp.where(key_at < lengths[seq], 0.0, MASKED_SCORE).astype(f32)
    query_back = [jnp.zeros((chunk, 128), f32) for _ in range(rows // chunk)]
    key_back = jnp.zeros((rows, 128), f32)
    value_back = jnp.zeros((rows, 128), f32)
    for i, mask in enumerate((low, high)):
        own_keys, own_values = keys * mask, values * mask
        own_queries, own_up = queries * mask, upstream * mask
        for c in range(rows // chunk):
            span = slice(c * chunk, (c + 1) * chunk)
            log_total = stat_ref[0, pl.ds(2 * pair + i, 1), span]
            scores = dot_t(own_keys, queries[span]) * (0.125 * LOG2E) + hidden_keys
            weight = jnp.exp2(scores - log_total)
            weight_back = dot_t(own_values, upstream[span])
            mean = jnp.sum(weight * weight_back, axis=0, keepdims=True)
            score_back = (weight * (weight_back - mean)).astype(bf16)
            value_back += dot(weight.astype(bf16), own_up[span])
            key_back += dot(score_back, own_queries[span])
            query_back[c] += dot_l(score_back, own_keys)
    for c in range(rows // chunk):
        grads[aligned(to + c * chunk, chunk, chunk), aligned(at, 128, 128)] = (query_back[c] * 0.125).astype(bf16)
    grads[aligned(to, rows, rows), aligned(D + at, 128, 128)] = (key_back * 0.125).astype(bf16)
    grads[aligned(to, rows, rows), aligned(2 * D + at, 128, 128)] = value_back.astype(bf16)


def attend_back_first_kernel(lengths, qkv_ref, back_ref, stat_ref, grads):
    attend_back_pair(0, pl.program_id(0), 0, lengths, qkv_ref, back_ref, stat_ref, grads)


def attend_back_first(lengths, qkv, back, stats):
    rows = stats.shape[2]
    whole = lambda *shape: pl.BlockSpec(shape, lambda s: (0,) * len(shape))
    return pl.pallas_call(
        attend_back_first_kernel,
        grid=(H // 2,),
        in_specs=[SMEM, whole(rows, 3 * D), whole(rows, D), whole(1, 16, rows)],
        out_specs=whole(rows, 3 * D),
        out_shape=jax.ShapeDtypeStruct((rows, 3 * D), bf16),
        compiler_params=pltpu.CompilerParams(vmem_limit_bytes=56 * MIB),
        cost_estimate=pl.CostEstimate(flops=14_000_000_000, bytes_accessed=9 * MIB, transcendentals=0),
        name="attend_back_first",
    )(lengths, qkv, back, stats)


def attend_back_kernel(seqs, place, lengths, x_ref, qkv_ref, back_ref, stat_ref, small_ref, db1_ref, first, *refs):
    (grads_out, keep, send, grads, lowered, packed, sem, wsem) = refs
    step = pl.program_id(0)
    pairs = H // 2
    rows = stat_ref.shape[2]
    steps = (seqs - 1) * pairs
    first_in = pltpu.make_async_copy(first, grads.at[pl.ds(0, rows)], sem)
    whole_copy = pltpu.make_async_copy(grads, grads_out, sem)

    @pl.when(step == 0)
    def _():
        first_in.start()
        lowered[...] = x_ref[...].astype(bf16)

    @pl.when(step < steps)
    def _():
        seq = 1 + step // pairs
        attend_back_pair(seq, step % pairs, seq * rows, lengths, qkv_ref, back_ref, stat_ref, grads)

    @pl.when(step == steps)
    def _():
        first_in.wait()
        whole_copy.start()

    for which in range(3):

        @pl.when(step == steps + which)
        def _():
            g = dot_l(lowered[...], grads[:, which * D : (which + 1) * D]).astype(bf16)
            if which == 1:
                packed[:, D:QKV_HALF] = g[:, : D // 2]
                packed[:, QKV_BLOCK : QKV_BLOCK + D // 2] = g[:, D // 2 :]
            else:
                at = 0 if which == 0 else QKV_BLOCK + D // 2
                packed[:, at : at + D] = g

    @pl.when(step == steps + 2)
    def _():
        query_bias = jnp.sum(grads[:, 0:D].astype(f32), axis=0, keepdims=True)
        value_bias = jnp.sum(grads[:, 2 * D :].astype(f32), axis=0, keepdims=True)
        rows_of = jnp.concatenate([query_bias, value_bias, small_ref[2:8, :], jnp.zeros((120, D), f32)], axis=0)
        packed[:, QKV_HALF:QKV_BLOCK] = rows_of.T.astype(bf16)
        owner = lax.broadcasted_iota(jnp.int32, (SLABS, FF), 1) // (4 * SLAB)
        mine = jnp.where(owner == lax.broadcasted_iota(jnp.int32, (SLABS, FF), 0), db1_ref[...], 0.0)
        place_of = lax.broadcasted_iota(jnp.int32, (FF, 128), 0) % (4 * SLAB)
        pick = (place_of == lax.broadcasted_iota(jnp.int32, (FF, 128), 1)).astype(f32)
        table = lax.dot_general(
            mine, pick, (((1,), (0,)), ((), ())), precision=lax.Precision.HIGHEST, preferred_element_type=f32
        )
        spread = jnp.broadcast_to(table[:, None, :], (SLABS, SLAB, 128)).reshape(D, 128)
        packed[:, QKV_BLOCK + QKV_HALF :] = spread.astype(bf16)
        for chip in range(CHIPS):
            for half in range(2):
                block = packed.at[pl.ds(chip * PAIR_ROWS, PAIR_ROWS), pl.ds(half * QKV_BLOCK, QKV_BLOCK)]
                hand_over(place, chip, half, keep, send, [(block, pl.ds(0, QKV_BLOCK))], wsem)
        wait_whole(keep, wsem)
        wait_whole(send, wsem)
        whole_copy.wait()


def attend_back(place, lengths, x, qkv, back, stats, small, inner_bias_grad, first):
    seqs = lengths.shape[0]
    count = x.shape[0]
    rows = count // seqs
    pairs = H // 2
    seq_of = lambda s: jnp.minimum(1 + s // pairs, seqs - 1)
    whole = lambda *shape: pl.BlockSpec(shape, lambda s: (0,) * len(shape))
    return pl.pallas_call(
        functools.partial(attend_back_kernel, seqs),
        grid=((seqs - 1) * pairs + 3,),
        in_specs=[
            SMEM,
            SMEM,
            whole(count, D),
            pl.BlockSpec((rows, 3 * D), lambda s: (seq_of(s), 0)),
            pl.BlockSpec((rows, D), lambda s: (seq_of(s), 0)),
            pl.BlockSpec((1, 16, rows), lambda s: (seq_of(s), 0, 0)),
            whole(8, D),
            whole(1, FF),
            ANY,
        ],
        out_specs=[ANY, ANY, ANY],
        out_shape=[
            jax.ShapeDtypeStruct((count, 3 * D), bf16),
            jax.ShapeDtypeStruct((CHIPS, PAIR_ROWS, QKV_BLOCK), bf16),
            jax.ShapeDtypeStruct((CHIPS, PAIR_ROWS, QKV_BLOCK), bf16),
        ],
        scratch_shapes=[
            pltpu.VMEM((count, 3 * D), bf16),
            pltpu.VMEM((count, D), bf16),
            pltpu.VMEM((D, 2 * QKV_BLOCK), bf16),
            pltpu.SemaphoreType.DMA,
            pltpu.SemaphoreType.DMA,
        ],
        compiler_params=pltpu.CompilerParams(vmem_limit_bytes=56 * MIB),
        cost_estimate=pl.CostEstimate(flops=23_000_000_000, bytes_accessed=20 * MIB, transcendentals=0),
        name="attend_back",
    )(place, lengths, x, qkv, back, stats, small, inner_bias_grad, first)


def input_back_kernel(fb_ref, grads_ref, w_ref, out_ref):
    half = D + D // 2
    first = dot_t(grads_ref[:, 0:half], w_ref[:, 0:half])
    second = dot_t(grads_ref[:, half:], w_ref[:, QKV_BLOCK : QKV_BLOCK + half])
    out_ref[...] = fb_ref[...] + first + second


def input_back(first_back, grads, weights):
    count = first_back.shape[0]
    return pl.pallas_call(
        input_back_kernel,
        grid=(count // BLOCK,),
        in_specs=[
            pl.BlockSpec((BLOCK, D), lambda s: (s, 0)),
            pl.BlockSpec((BLOCK, 3 * D), lambda s: (s, 0)),
            pl.BlockSpec((D, 2 * QKV_BLOCK), lambda s: (0, 0)),
        ],
        out_specs=pl.BlockSpec((BLOCK, D), lambda s: (s, 0)),
        out_shape=jax.ShapeDtypeStruct((count, D), f32),
        compiler_params=pltpu.CompilerParams(vmem_limit_bytes=56 * MIB),
        cost_estimate=pl.CostEstimate(flops=9_000_000_000, bytes_accessed=15 * MIB, transcendentals=0),
        name="input_back",
    )(first_back, grads, weights)


AXES = ("dp", "fsdp")


def swap(v, mask, count):
    return lax.ppermute(v, AXES, [(i, i ^ mask) for i in range(count)])


CORE, ALONG_X, ALONG_Y, ALONG_Z = 1, 2, 4, 8
Z_COUNT = 4
FAST_SHAPE = {"dp": Z_COUNT, "fsdp": 8}


def after(values, *others):
    out = lax.optimization_barrier(tuple(values) + others)
    return out[: len(values)]


def move(v, mask):
    return swap(v, mask, SLABS)


def gather_z(block):
    return [block] + [move(block, k * ALONG_Z) for k in range(1, Z_COUNT)]


def gather_one(per_z):
    first, second = jnp.stack(per_z[:2]), jnp.stack(per_z[2:])
    return first, second, move(first, ALONG_X), move(second, ALONG_Y)


def gather_two(state):
    first, second, first_x, second_y = state
    first_chips, second_chips = (0, 4), (8, 12)
    shift = lambda chips, by: tuple(c ^ by for c in chips)
    first = jnp.concatenate([first, first_x])
    second = jnp.concatenate([second, second_y])
    first_chips += shift(first_chips, 1)
    second_chips += shift(second_chips, 2)
    return [
        (first, first_chips),
        (second, second_chips),
        (move(first, ALONG_Y), shift(first_chips, 2)),
        (move(second, ALONG_X), shift(second_chips, 1)),
    ]


def gather_core(held):
    arrays = [a for a, _ in held] + [move(a, CORE) for a, _ in held]
    meta = tuple((c, False) for _, c in held) + tuple((c, True) for _, c in held)
    return arrays, meta


def wide(v):
    return v.astype(f32)


LOW_Z, HIGH_Z, EVERY = slice(0, 2), slice(2, 4), slice(None)


class ChipSums:
    def __init__(self, keep, got):
        shape = (Z_COUNT, 2, 2) + keep.shape[1:]
        self.keep, self.got = keep.reshape(shape), got.reshape(shape)

    def part(self, z, y, x):
        return wide(self.keep[z, y, x]) + wide(self.got[z, y, x])


def scatter_ready(sums):
    return sums.part(LOW_Z, 1, EVERY).astype(bf16), sums.part(HIGH_Z, EVERY, 1).astype(bf16)


def scatter_one(first, second):
    return move(first, ALONG_Y), move(second, ALONG_X)


def scatter_two(sums, first, second):
    first_sum = lambda x: sums.part(LOW_Z, 0, x) + wide(first[:, x])
    second_sum = lambda y: sums.part(HIGH_Z, y, 0) + wide(second[:, y])
    first_more = move(first_sum(1).astype(bf16), ALONG_X)
    second_more = move(second_sum(1).astype(bf16), ALONG_Y)
    low_part = first_sum(0) + wide(first_more)
    high_part = second_sum(0) + wide(second_more)
    return [low_part[0], low_part[1], high_part[0], high_part[1]]


def scatter_z(parts):
    total = parts[0]
    for k in range(1, Z_COUNT):
        total = total + wide(move(parts[k].astype(bf16), k * ALONG_Z))
    return total


def fast_blocks(shards, core):
    (qw, kw, vw, ow, qb, vb, ob, fg, fs, iw, ib, dw, db, sg, ss) = shards
    vectors = jnp.pad(jnp.stack([qb, vb, ob, fg, fs, db, sg, ss], axis=1), ((0, 0), (0, 120)))
    inner_bias = jnp.pad(ib.reshape(1, 4 * SLAB), ((0, SLAB - 1), (0, 128 - 4 * SLAB)))
    half = D // 2
    halves = [
        jnp.concatenate([qw, kw[:, :half], vectors, ow[:, :half], iw[:, :INNER_HALF]], axis=1),
        jnp.concatenate([kw[:, half:], vw, inner_bias, ow[:, half:], iw[:, INNER_HALF:]], axis=1),
    ]
    low_core = core == 0
    own = jnp.where(low_core, halves[0], halves[1])
    other = move(jnp.where(low_core, halves[1], halves[0]), CORE)
    rows = jnp.concatenate([jnp.where(low_core, own, other), jnp.where(low_core, other, own)], axis=0)
    qkv_block = rows[:, :QKV_BLOCK]
    ffn_block = jnp.concatenate([rows[:, QKV_BLOCK:], dw[:PAIR_ROWS], dw[PAIR_ROWS:]], axis=1)
    return qkv_block, ffn_block


def both_halves(total, core):
    mine = lax.dynamic_slice_in_dim(total, core * SLAB, SLAB, 0)
    other = move(lax.dynamic_slice_in_dim(total, (1 - core) * SLAB, SLAB, 0), CORE)
    low_core = core == 0
    return jnp.where(low_core, mine, other), jnp.where(low_core, other, mine)


def gather_plain(shards):
    (qw, kw, vw, ow, qb, vb, ob, fg, fs, iw, ib, dw, db, sg, ss) = [
        lax.all_gather(v, AXES, axis=0, tiled=True) for v in shards
    ]
    vectors = jnp.pad(jnp.stack([qb, vb, ob, fg, fs, db, sg, ss], axis=1), ((0, 0), (0, 120)))
    inner_bias = jnp.pad(ib.reshape(SLABS, 1, 4 * SLAB), ((0, 0), (0, SLAB - 1), (0, 128 - 4 * SLAB))).reshape(D, 128)
    half = D // 2
    chips = lambda v: v.reshape(CHIPS, PAIR_ROWS, -1)
    down = dw.reshape(CHIPS, 2, 2, PAIR_ROWS, D)
    first = [
        chips(jnp.concatenate([qw, kw[:, :half], vectors], axis=1)),
        chips(jnp.concatenate([kw[:, half:], vw, inner_bias], axis=1)),
    ]
    second = [
        jnp.concatenate(
            [
                chips(ow[:, c * half : (c + 1) * half]),
                chips(iw[:, c * INNER_HALF : (c + 1) * INNER_HALF]),
                down[:, c, 0],
                down[:, c, 1],
            ],
            axis=2,
        )
        for c in range(2)
    ]
    meta = ((tuple(range(CHIPS)), False), (tuple(range(CHIPS)), True))
    return (first, meta), (second, meta)


def local(fast, inputs, lengths, *rest):
    shards, cotangent = rest[:15], rest[15]
    if fast:
        linear = lax.axis_index(AXES)
        core = linear & 1
        place = jnp.stack([linear >> 1, core]).astype(jnp.int32)
        qkv_block, ffn_block = fast_blocks(shards, core)
        qkv_z = gather_z(qkv_block)
        (ffn_block,) = after((ffn_block,), *qkv_z[1:])
        ffn_z = gather_z(ffn_block)
        qkv_two = gather_two(gather_one(qkv_z))
        first, first_meta = gather_core(qkv_two)
        ffn_z = after(ffn_z, *(v for v, _ in qkv_two))
        ffn_one = gather_one(ffn_z)
    else:
        place = jnp.zeros((2,), jnp.int32)
        (first, first_meta), (second, second_meta) = gather_plain(shards)
    qkv, attended, stats, weights, vectors = attend(place, lengths, inputs, first, first_meta)
    bias_at = QKV_BLOCK + QKV_HALF
    inner_bias = weights[::SLAB, bias_at : bias_at + 4 * SLAB].reshape(1, FF).astype(f32)
    if fast:
        ffn_one = after(ffn_one, attended)
        second, second_meta = gather_core(gather_two(ffn_one))
    output, first_back, back, small, db1, ffn_keep, ffn_send = feed_forward(
        place, inputs, attended, cotangent, vectors, inner_bias, second, second_meta
    )
    half_grads = attend_back_first(lengths, qkv, back, stats)
    if fast:
        ffn_got = move(ffn_send, CORE)
        (ffn_got,) = after((ffn_got,), half_grads)
        ffn_sums = ChipSums(ffn_keep, ffn_got)
        ffn_ready = scatter_ready(ffn_sums)
        half_grads, *ffn_ready = after((half_grads,) + ffn_ready)
        ffn_first = scatter_one(*ffn_ready)
    grads, qkv_keep, qkv_send = attend_back(place, lengths, inputs, qkv, back, stats, small, db1, half_grads)
    if fast:
        qkv_got = move(qkv_send, CORE)
        ffn_first = after(ffn_first, qkv_keep)
        ffn_parts = scatter_two(ffn_sums, *ffn_first)
        qkv_sums = ChipSums(qkv_keep, qkv_got)
        ffn = scatter_z(ffn_parts)
        proj = scatter_z(scatter_two(qkv_sums, *scatter_one(*scatter_ready(qkv_sums))))
        grad_input = input_back(first_back, grads, weights)
        narrow = both_halves(ffn[:, : OUT_HALF + INNER_HALF], core)
        down_grad = jnp.concatenate([ffn[:, -2 * D : -D], ffn[:, -D:]], axis=0)
        proj = both_halves(proj, core)
        shard = lambda v: v
    else:
        grad_input = input_back(first_back, grads, weights)
        shard = lambda v: lax.psum_scatter(v, AXES, scatter_dimension=0, tiled=True)
        flat = lambda v: v.astype(f32).reshape(D, -1)
        narrow = [flat(v[:, :, : OUT_HALF + INNER_HALF]) for v in (ffn_keep, ffn_send)]
        parts = [jnp.stack([v[:, :, -2 * D : -D], v[:, :, -D:]], axis=1) for v in (ffn_keep, ffn_send)]
        down_grad = jnp.stack(parts, axis=1).reshape(FF, D).astype(f32)
        proj = [flat(v) for v in (qkv_keep, qkv_send)]
    low, high = proj
    wide = lambda *v: shard(jnp.concatenate(v, axis=1))
    vec = lambda i: shard(low[:, QKV_HALF + i])
    return (
        output,
        grad_input,
        shard(low[:, :D]),
        wide(low[:, D:QKV_HALF], high[:, : D // 2]),
        shard(high[:, D // 2 : QKV_HALF]),
        wide(narrow[0][:, :OUT_HALF], narrow[1][:, :OUT_HALF]),
        vec(0),
        vec(1),
        vec(2),
        vec(3),
        vec(4),
        wide(narrow[0][:, OUT_HALF:], narrow[1][:, OUT_HALF:]),
        shard(high[::SLAB, QKV_HALF : QKV_HALF + 4 * SLAB].reshape(-1)),
        shard(down_grad),
        vec(5),
        vec(6),
        vec(7),
    )


def solution(mesh):
    rows, flat = P(AXES, None), P(AXES)
    params = (rows,) * 4 + (flat,) * 5 + (rows, flat, rows, flat, flat, flat)
    return jax.shard_map(
        functools.partial(local, dict(mesh.shape) == FAST_SHAPE),
        mesh=mesh,
        in_specs=(rows, flat) + params + (rows,),
        out_specs=(rows, rows) + params,
        check_vma=False,
    )
```

```python
import functools
import math

import jax
import jax.numpy as jnp
import numpy as np
from jax import lax
from jax.experimental import pallas as pl
from jax.experimental.pallas import tpu as pltpu
from jax.sharding import PartitionSpec as P

D = 768
H = 12
DH = 64
FF = 3072
SLABS = 32
SLAB = D // SLABS
CHIPS = SLABS // 2
PAIR_ROWS = 2 * SLAB
NORM_EPSILON = 1e-12
MASKED_SCORE = -1000000000.0
GAUSS_DENSITY = 0.3989422804014327
LOG2E = 1.4426950408889634
MIB = 1 << 20
VMEM = 62 * MIB
LITTLE = 16 * MIB

QKV_HALF = 3 * D // 2
QKV_BLOCK = QKV_HALF + 128
OUT_HALF = D // 2
PROJ_BLOCK = QKV_BLOCK + OUT_HALF
INNER_HALF = FF // 2
INNER_BLOCK = OUT_HALF + INNER_HALF
DOWN_BLOCK = 2 * D

SLOT_BITS = ((8, 4, 1, 2), (4, 8, 2, 1))
SLOT_CHIPS = tuple(
    tuple(sum(bit for i, bit in enumerate(bits) if slot >> i & 1) for slot in range(CHIPS)) for bits in SLOT_BITS
)

bf16 = jnp.bfloat16
f32 = jnp.float32
ANY = pl.BlockSpec(memory_space=pl.ANY)
SMEM = pl.BlockSpec(memory_space=pltpu.SMEM)


def dot(a, b):
    return lax.dot_general(a, b, (((1,), (0,)), ((), ())), preferred_element_type=f32)


def dot_t(a, b):
    return lax.dot_general(a, b, (((1,), (1,)), ((), ())), preferred_element_type=f32)


def dot_l(a, b):
    return lax.dot_general(a, b, (((0,), (0,)), ((), ())), preferred_element_type=f32)


def call(kernel, operands, deps, in_specs, **options):
    count = len(operands)

    def body(*refs):
        kernel(*refs[:count], *refs[count + len(deps) :])

    in_specs = in_specs + [whole(8, 128) if v.shape == (8, 128) else ANY for v in deps]
    return pl.pallas_call(body, in_specs=in_specs, **options)(*operands, *deps)


def aligned(start, size, unit):
    return pl.ds(pl.multiple_of(start, unit), size)


def chip_of(slot, half):
    return jnp.where(half == 0, SLOT_CHIPS[0][slot], SLOT_CHIPS[1][slot])


def slot_of(chip, half):
    bits = SLOT_BITS[half]
    return sum(jnp.where((chip & bit) != 0, 1 << i, 0) for i, bit in enumerate(bits))


def blocks_of(place, pieces):
    for ref, (first, other) in pieces:
        half = 1 - place[1] if other else place[1]
        for i in range(ref.shape[0]):
            yield ref, i, place[0] ^ chip_of(first + i, half), half


def proj_blocks(place, pieces, weights, sem):
    for ref, i, chip, half in blocks_of(place, pieces):
        rows = aligned(chip * PAIR_ROWS, PAIR_ROWS, 16)
        yield pltpu.make_async_copy(ref.at[i], weights.at[rows, aligned(half * PROJ_BLOCK, PROJ_BLOCK, 128)], sem)


def inner_blocks(place, pieces, inner_w, sem):
    for ref, i, chip, half in blocks_of(place, pieces):
        rows = aligned(chip * PAIR_ROWS, PAIR_ROWS, 16)
        yield pltpu.make_async_copy(
            ref.at[i, :, pl.ds(0, INNER_HALF)],
            inner_w.at[rows, aligned(half * INNER_HALF, INNER_HALF, 128)],
            sem,
        )


def down_blocks(place, pieces, down_w, sem):
    for ref, i, chip, half in blocks_of(place, pieces):
        for k in range(2):
            at = (chip * 2 + half) * (2 * PAIR_ROWS) + k * PAIR_ROWS
            yield pltpu.make_async_copy(
                ref.at[i, :, pl.ds(INNER_HALF + k * D, D)], down_w.at[aligned(at, PAIR_ROWS, 16), :], sem
            )


def start_all(copies):
    for c in copies:
        c.start()


def whole(*shape):
    return pl.BlockSpec(shape, lambda *s: (0,) * len(shape))


def fold_rows(v):
    return jnp.sum(v.reshape(v.shape[0] // 8, 8, v.shape[1]), axis=0)


def hand_over(place, chip, half, keep, send, pairs, sem):
    slot = slot_of(chip ^ place[0], half)
    for mine, out in ((True, keep), (False, send)):

        @pl.when((place[1] == half) == mine)
        def _():
            for source, lanes in pairs:
                pltpu.make_async_copy(source, out.at[slot, :, lanes], sem).start()


def wait_whole(ref, sem):
    pltpu.make_async_copy(ref, ref, sem).wait()


def lane_masks():
    low = (lax.broadcasted_iota(jnp.int32, (1, 128), 1) < DH).astype(f32)
    return low.astype(bf16), (1.0 - low).astype(bf16)


def attend_kernel(meta, n_pieces, place, lengths, x_ref, *refs):
    piece_refs = refs[:n_pieces]
    qkv_ref, att_ref, stat_ref, weights, vectors = refs[n_pieces : n_pieces + 5]
    sem = refs[-1]
    seq = pl.program_id(0)
    rows = x_ref.shape[0]

    @pl.when(seq == 0)
    def _():
        start_all(proj_blocks(place, zip(piece_refs, meta), weights, sem))
        wait_whole(weights, sem)
        small = weights[:, QKV_HALF:QKV_BLOCK].astype(f32)
        vectors[...] = small.T[0:16, :]

    lowered = x_ref[...].astype(bf16)
    first = dot(lowered, weights[:, 0:QKV_HALF])
    qkv_ref[:, 0:D] = (first[:, 0:D] + vectors[0:1, :]).astype(bf16)
    qkv_ref[:, D:QKV_HALF] = first[:, D:QKV_HALF].astype(bf16)
    second = dot(lowered, weights[:, PROJ_BLOCK : PROJ_BLOCK + QKV_HALF])
    qkv_ref[:, QKV_HALF : 2 * D] = second[:, 0 : D // 2].astype(bf16)
    qkv_ref[:, 2 * D :] = (second[:, D // 2 :] + vectors[1:2, :]).astype(bf16)

    low, high = lane_masks()
    lane = lax.broadcasted_iota(jnp.int32, (1, 128), 1)
    key_at = lax.broadcasted_iota(jnp.int32, (1, rows), 1)
    hidden_keys = jnp.where(key_at < lengths[seq], 0.0, MASKED_SCORE).astype(f32)
    chunk = 256
    ones = jnp.ones((rows, 128), bf16)
    stats = [jnp.zeros((chunk, 128), f32) for _ in range(rows // chunk)]
    for pair in range(H // 2):
        at = pair * 128
        keys = qkv_ref[:, D + at : D + at + 128]
        values = jnp.concatenate([qkv_ref[:, 2 * D + at : 2 * D + at + 128], ones], axis=1)
        keys_of = (keys * low, keys * high)
        for c in range(rows // chunk):
            span = pl.ds(c * chunk, chunk)
            queries = qkv_ref[span, at : at + 128]
            outs = []
            for i in range(2):
                scores = dot_t(queries, keys_of[i]) * (0.125 * LOG2E) + hidden_keys
                peak = jnp.max(scores, axis=-1, keepdims=True)
                weight = jnp.exp2(scores - peak).astype(bf16)
                both = dot(weight, values)
                total = both[:, 128:]
                outs.append(both[:, :128] / total)
                log_total = peak + jnp.log2(total)
                stats[c] = jnp.where(lane == 2 * pair + i, log_total, stats[c])
            att_ref[span, at : at + 128] = jnp.where(lane < DH, outs[0], outs[1]).astype(bf16)
    for c in range(rows // chunk):
        stat_ref[0, :, c * chunk : (c + 1) * chunk] = stats[c].T[0:16, :]


def attend(place, lengths, x, pieces, meta):
    rows = x.shape[0] // lengths.shape[0]
    seqs = lengths.shape[0]
    return pl.pallas_call(
        functools.partial(attend_kernel, meta, len(pieces)),
        grid=(seqs,),
        in_specs=[SMEM, SMEM, pl.BlockSpec((rows, D), lambda s: (s, 0))] + [ANY] * len(pieces),
        out_specs=[
            pl.BlockSpec((rows, 3 * D), lambda s: (s, 0)),
            pl.BlockSpec((rows, D), lambda s: (s, 0)),
            pl.BlockSpec((1, 16, rows), lambda s: (s, 0, 0)),
            whole(D, 2 * PROJ_BLOCK),
            whole(16, D),
        ],
        out_shape=[
            jax.ShapeDtypeStruct((seqs * rows, 3 * D), bf16),
            jax.ShapeDtypeStruct((seqs * rows, D), bf16),
            jax.ShapeDtypeStruct((seqs, 16, rows), f32),
            jax.ShapeDtypeStruct((D, 2 * PROJ_BLOCK), bf16),
            jax.ShapeDtypeStruct((16, D), f32),
        ],
        scratch_shapes=[pltpu.SemaphoreType.DMA],
        compiler_params=pltpu.CompilerParams(vmem_limit_bytes=VMEM),
        cost_estimate=pl.CostEstimate(flops=18_000_000_000, bytes_accessed=20 * MIB, transcendentals=0),
        name="attend",
    )(place, lengths, x, *pieces)


def gelu_parts(u):
    size = jnp.abs(u)
    bell = jnp.exp2(u * u * (-0.5 * LOG2E))
    t = 1.0 / (1.0 + (0.3275911 * math.sqrt(0.5)) * size)
    poly = t * (0.127414796 + t * (-0.142248368 + t * (0.7107068705 + t * (-0.7265760135 + t * 0.5307027145))))
    tail = poly * bell
    below = jnp.where(u < 0.0, tail, 1.0 - tail)
    return below, bell


def mean_rows(v):
    return jnp.sum(v, axis=-1, keepdims=True) * (1.0 / D)


def norm_rows(total):
    center = total - mean_rows(total)
    rstd = lax.rsqrt(mean_rows(center * center) + NORM_EPSILON)
    return center * rstd, rstd


def norm_back(upstream, normed, rstd, gain):
    scaled = upstream * gain
    return rstd * (scaled - mean_rows(scaled) - normed * mean_rows(scaled * normed))


BLOCK = 256
WIDTH = 768
DOWN_STEPS = 8


def out_weight_copies(proj_w, out_w, sem):
    for half in range(2):
        lanes = pl.ds(half * PROJ_BLOCK + QKV_BLOCK, OUT_HALF)
        yield pltpu.make_async_copy(proj_w.at[:, lanes], out_w.at[:, pl.ds(half * OUT_HALF, OUT_HALF)], sem)


def probs_kernel(seq, lengths, q_ref, k_ref, stat_ref, *refs):
    prob_ref = refs[-1]
    pair = pl.program_id(0)
    rows = q_ref.shape[0]
    chunk = 256
    key_at = lax.broadcasted_iota(jnp.int32, (rows, 1), 0)
    hidden_keys = jnp.where(key_at < lengths[seq], 0.0, MASKED_SCORE).astype(f32)
    for i, mask in enumerate(lane_masks()):
        own_keys = k_ref[...] * mask
        for c in range(rows // chunk):
            span = slice(c * chunk, (c + 1) * chunk)
            log_total = stat_ref[0, pl.ds(2 * pair + i, 1), span]
            scores = dot_t(own_keys, q_ref[span, :]) * (0.125 * LOG2E) + hidden_keys
            prob_ref[i, :, span] = jnp.exp2(scores - log_total).astype(bf16)


def probs_specs(seq, rows):
    pairs = H // 2
    lane = lambda kind: pl.BlockSpec((rows, 128), lambda s: (seq, kind * pairs + s))
    specs = [SMEM, lane(0), lane(1), pl.BlockSpec((1, 16, rows), lambda s: (seq, 0, 0))]
    return specs, pl.BlockSpec((2, rows, rows), lambda s: (seq * pairs + s, 0, 0))


def probs(seq, lengths, qkv, stats, deps=()):
    seqs, _, rows = stats.shape
    specs, out = probs_specs(seq, rows)
    return call(
        functools.partial(probs_kernel, seq),
        (lengths, qkv, qkv, stats),
        deps,
        grid=(H // 2,),
        in_specs=specs,
        out_specs=out,
        out_shape=jax.ShapeDtypeStruct((seqs * H, rows, rows), bf16),
        compiler_params=pltpu.CompilerParams(vmem_limit_bytes=VMEM),
        cost_estimate=pl.CostEstimate(flops=8_000_000_000, bytes_accessed=MIB, transcendentals=0),
        name="probs",
    )


def window_kernel(seq, blocks, lengths, q_ref, k_ref, stat_ref, _, x_ref, att_ref, vec_ref, proj_w, *refs):
    prob_ref, normed_ref, rstd_ref, hid_ref, x_t, att_t, hid_t, out_w, sem = refs
    g = pl.program_id(0)

    @pl.when(g == 0)
    def _():
        start_all(out_weight_copies(proj_w, out_w, sem))

    probs_kernel(seq, lengths, q_ref, k_ref, stat_ref, prob_ref)

    @pl.when(g == 0)
    def _():
        wait_whole(out_w, sem)

    @pl.when(g < blocks)
    def _():
        x, attended = x_ref[...], att_ref[...]
        normed, rstd = norm_rows(x + dot(attended, out_w[...]) + vec_ref[2:3, :])
        normed_ref[...] = normed
        rstd_ref[...] = jnp.broadcast_to(rstd, rstd_ref.shape)
        hidden = normed * vec_ref[3:4, :] + vec_ref[4:5, :]
        hid_ref[...] = hidden.astype(bf16)
        x_t[...] = x.T.astype(bf16)
        att_t[...] = attended.astype(f32).T.astype(bf16)
        hid_t[...] = hidden.T.astype(bf16)


def window(seq, lengths, x, qkv, attended, stats, weights, vectors, prob, deps=()):
    count = x.shape[0]
    _, _, rows = stats.shape
    blocks = count // BLOCK
    block = lambda s: jnp.minimum(s, blocks - 1)
    token = lambda width: pl.BlockSpec((BLOCK, width), lambda s: (block(s), 0))
    turned = pl.BlockSpec((D, BLOCK), lambda s: (0, block(s)))
    specs, out = probs_specs(seq, rows)
    return call(
        functools.partial(window_kernel, seq, blocks),
        (lengths, qkv, qkv, stats, prob, x, attended, vectors, weights),
        deps,
        grid=(H // 2,),
        in_specs=specs + [ANY, token(D), token(D), whole(16, D), ANY],
        out_specs=[out, token(D), token(128), token(D)] + [turned] * 3,
        out_shape=[
            jax.ShapeDtypeStruct(prob.shape, bf16),
            jax.ShapeDtypeStruct((count, D), f32),
            jax.ShapeDtypeStruct((count, 128), f32),
            jax.ShapeDtypeStruct((count, D), bf16),
        ]
        + [jax.ShapeDtypeStruct((D, count), bf16)] * 3,
        input_output_aliases={4: 0},
        scratch_shapes=[pltpu.VMEM((D, D), bf16), pltpu.SemaphoreType.DMA],
        compiler_params=pltpu.CompilerParams(vmem_limit_bytes=VMEM),
        cost_estimate=pl.CostEstimate(flops=14_000_000_000, bytes_accessed=MIB, transcendentals=0),
        name="window",
    )


def ffn_kernel(meta, pieces, blocks, place, normed_ref, rstd_ref, hid_ref, cot_ref, vec_ref, b1_ref, proj_w, *refs):
    piece_refs = refs[:pieces]
    (out_ref, fb_ref, ab_ref, ib_ref, branch_ref, small_ref, db1_ref, keep, send) = refs[pieces : pieces + 9]
    (out_w, inner_w, down_w, act, down_back, sem, wsem) = refs[pieces + 9 :]
    step = pl.program_id(0)

    @pl.when(step == 0)
    def _():
        start_all(inner_blocks(place, zip(piece_refs, meta), inner_w, sem.at[0]))
        start_all(down_blocks(place, zip(piece_refs, meta), down_w, sem.at[1]))
        start_all(out_weight_copies(proj_w, out_w, sem.at[2]))
        small_ref[...] = jnp.zeros_like(small_ref)
        db1_ref[...] = jnp.zeros_like(db1_ref)
        wait_whole(inner_w, sem.at[0])
        wait_whole(down_w, sem.at[1])
        wait_whole(out_w, sem.at[2])

    @pl.when(step < blocks)
    def _():
        rows = aligned(step * BLOCK, BLOCK, BLOCK)
        first_gain, first_shift = vec_ref[3:4, :], vec_ref[4:5, :]
        second_gain, second_shift = vec_ref[6:7, :], vec_ref[7:8, :]
        first_normed = normed_ref[...]
        hidden_low = hid_ref[...]
        total = first_normed * first_gain + first_shift + vec_ref[5:6, :]
        slopes = []
        for c in range(FF // WIDTH):
            cols = pl.ds(c * WIDTH, WIDTH)
            u = dot(hidden_low, inner_w[:, cols]) + b1_ref[:, cols]
            below, bell = gelu_parts(u)
            active = (u * below).astype(bf16)
            act[rows, cols] = active
            slopes.append(below + u * bell * GAUSS_DENSITY)
            total = total + dot(active, down_w[cols, :])
        second_normed, second_rstd = norm_rows(total)
        out_ref[...] = second_normed * second_gain + second_shift
        cot = cot_ref[...]
        second_back = norm_back(cot, second_normed, second_rstd, second_gain)
        back_low = second_back.astype(bf16)
        down_back[rows, :] = back_low
        hidden_back = second_back
        for c in range(FF // WIDTH):
            cols = pl.ds(c * WIDTH, WIDTH)
            ib = (dot_t(back_low, down_w[cols, :]) * slopes[c]).astype(bf16)
            ib_ref[:, cols] = ib
            db1_ref[:, cols] += fold_rows(ib.astype(f32))
            hidden_back = hidden_back + dot_t(ib, inner_w[:, cols])
        first_back = norm_back(hidden_back, first_normed, rstd_ref[:, 0:1], first_gain)
        fb_ref[...] = first_back
        branch_low = first_back.astype(bf16)
        branch_ref[...] = branch_low
        ab_ref[...] = dot_t(branch_low, out_w[...]).astype(bf16)
        sums = (
            branch_low.astype(f32),
            hidden_back * first_normed,
            hidden_back,
            back_low.astype(f32),
            cot * second_normed,
            cot,
        )
        for i, v in enumerate(sums):
            small_ref[i] += fold_rows(v)

    @pl.when(step >= blocks)
    def _():
        chunk = step - blocks
        width = FF // DOWN_STEPS
        rows = aligned(chunk * width, width, 128)
        down_w[rows, :] = dot_l(act[:, rows], down_back[...]).astype(bf16)
        for i in range(CHIPS // DOWN_STEPS):
            chip = chunk * (CHIPS // DOWN_STEPS) + i
            for half in range(2):
                at = (chip * 2 + half) * (2 * PAIR_ROWS)
                pairs = [
                    (down_w.at[aligned(at + k * PAIR_ROWS, PAIR_ROWS, 16)], pl.ds(k * D, D)) for k in range(2)
                ]
                hand_over(place, chip, half, keep, send, pairs, wsem)

    @pl.when(step == blocks + DOWN_STEPS - 1)
    def _():
        wait_whole(keep, wsem)
        wait_whole(send, wsem)


def feed_forward(place, normed, rstd, hid, cotangent, vectors, inner_bias, weights, pieces, meta):
    count = normed.shape[0]
    blocks = count // BLOCK
    token = lambda width: pl.BlockSpec((BLOCK, width), lambda s: (jnp.minimum(s, blocks - 1), 0))
    return pl.pallas_call(
        functools.partial(ffn_kernel, meta, len(pieces), blocks),
        grid=(blocks + DOWN_STEPS,),
        in_specs=[SMEM, token(D), token(128), token(D), token(D), whole(16, D), whole(1, FF), ANY]
        + [ANY] * len(pieces),
        out_specs=[token(D), token(D), token(D), token(FF), token(D), whole(6, 8, D), whole(8, FF), ANY, ANY],
        out_shape=[
            jax.ShapeDtypeStruct((count, D), f32),
            jax.ShapeDtypeStruct((count, D), f32),
            jax.ShapeDtypeStruct((count, D), bf16),
            jax.ShapeDtypeStruct((count, FF), bf16),
            jax.ShapeDtypeStruct((count, D), bf16),
            jax.ShapeDtypeStruct((6, 8, D), f32),
            jax.ShapeDtypeStruct((8, FF), f32),
            jax.ShapeDtypeStruct((CHIPS, PAIR_ROWS, DOWN_BLOCK), bf16),
            jax.ShapeDtypeStruct((CHIPS, PAIR_ROWS, DOWN_BLOCK), bf16),
        ],
        scratch_shapes=[
            pltpu.VMEM((D, D), bf16),
            pltpu.VMEM((D, FF), bf16),
            pltpu.VMEM((FF, D), bf16),
            pltpu.VMEM((count, FF), bf16),
            pltpu.VMEM((count, D), bf16),
            pltpu.SemaphoreType.DMA((3,)),
            pltpu.SemaphoreType.DMA,
        ],
        compiler_params=pltpu.CompilerParams(vmem_limit_bytes=VMEM),
        cost_estimate=pl.CostEstimate(flops=52_000_000_000, bytes_accessed=40 * MIB, transcendentals=0),
        name="feed_forward",
    )(place, normed, rstd, hid, cotangent, vectors, inner_bias, weights, *pieces)


def inner_grads_kernel(hid_t, ib_ref, place, att_in, branch_in, keep, send, att_t, branch, out_g, inner_g, sem, wsem):
    step = pl.program_id(0)
    steps = FF // D
    later = [pltpu.make_async_copy(att_in, att_t, sem.at[0]), pltpu.make_async_copy(branch_in, branch, sem.at[1])]

    @pl.when(step == 0)
    def _():
        start_all(later)

    def give(grads, half, width, lane):
        for chip in range(CHIPS):
            block = grads.at[pl.ds(chip * PAIR_ROWS, PAIR_ROWS), pl.ds(half * width, width)]
            hand_over(place, chip, half, keep, send, [(block, pl.ds(lane, width))], wsem)

    @pl.when(step < steps)
    def _():
        cols = aligned(step * D, D, 128)
        inner_g[:, cols] = dot(hid_t[...], ib_ref[...]).astype(bf16)
        for half in range(2):

            @pl.when(step == (half + 1) * (steps // 2) - 1)
            def _():
                give(inner_g, half, INNER_HALF, OUT_HALF)

    @pl.when(step == steps)
    def _():
        for copy in later:
            copy.wait()
        out_g[...] = dot(att_t[...], branch[...]).astype(bf16)
        for half in range(2):
            give(out_g, half, OUT_HALF, 0)
        wait_whole(keep, wsem)
        wait_whole(send, wsem)


def inner_grads(place, hid_t, inner_back, att_t, branch):
    count = hid_t.shape[1]
    steps = FF // D
    return pl.pallas_call(
        inner_grads_kernel,
        grid=(steps + 1,),
        in_specs=[
            whole(D, count),
            pl.BlockSpec((count, D), lambda s: (0, jnp.minimum(s, steps - 1))),
            SMEM,
            ANY,
            ANY,
        ],
        out_specs=[ANY, ANY],
        out_shape=[jax.ShapeDtypeStruct((CHIPS, PAIR_ROWS, INNER_BLOCK), bf16)] * 2,
        scratch_shapes=[
            pltpu.VMEM((D, count), bf16),
            pltpu.VMEM((count, D), bf16),
            pltpu.VMEM((D, D), bf16),
            pltpu.VMEM((D, FF), bf16),
            pltpu.SemaphoreType.DMA((2,)),
            pltpu.SemaphoreType.DMA,
        ],
        compiler_params=pltpu.CompilerParams(vmem_limit_bytes=VMEM),
        cost_estimate=pl.CostEstimate(flops=4_000_000_000, bytes_accessed=MIB, transcendentals=0),
        name="inner_grads",
    )(hid_t, inner_back, place, att_t, branch)


def attend_back_pair(queries, keys, values, upstream, prob_ref, dq_ref, dk_ref, dv_ref):
    rows = queries.shape[0]
    chunk = 256
    query_back = [jnp.zeros((chunk, 128), f32) for _ in range(rows // chunk)]
    key_back = jnp.zeros((rows, 128), f32)
    value_back = jnp.zeros((rows, 128), f32)
    for i, mask in enumerate(lane_masks()):
        own_keys, own_values = keys * mask, values * mask
        own_queries, own_up = queries * mask, upstream * mask
        for c in range(rows // chunk):
            span = slice(c * chunk, (c + 1) * chunk)
            low = prob_ref[i, :, span]
            weight = low.astype(f32)
            weight_back = dot_t(own_values, upstream[span])
            mean = jnp.sum(weight * weight_back, axis=0, keepdims=True)
            score_back = (weight * (weight_back - mean)).astype(bf16)
            value_back += dot(low, own_up[span])
            key_back += dot(score_back, own_queries[span])
            query_back[c] += dot_l(score_back, own_keys)
    dq_ref[...] = (jnp.concatenate(query_back, axis=0) * 0.125).astype(bf16)
    dk_ref[...] = (key_back * 0.125).astype(bf16)
    dv_ref[...] = value_back.astype(bf16)


def attend_back_kernel(q_ref, k_ref, v_ref, up_ref, prob_ref, *refs):
    attend_back_pair(q_ref[...], k_ref[...], v_ref[...], up_ref[...], prob_ref, *refs[-3:])


def pair_specs(rows, first, last):
    pairs = H // 2
    pair = lambda s: jnp.minimum(first + s, last)
    lane = lambda kind: pl.BlockSpec((rows, 128), lambda s: (pair(s) // pairs, kind * pairs + pair(s) % pairs))
    return [lane(0), lane(1), lane(2), lane(0), pl.BlockSpec((2, rows, rows), lambda s: (pair(s), 0, 0))]


def attend_back(first, count, qkv, back, prob, grads=(), deps=()):
    specs = pair_specs(prob.shape[1], first, first + count - 1)
    return call(
        attend_back_kernel,
        (qkv, qkv, qkv, back, prob, *grads),
        deps,
        grid=(count,),
        in_specs=specs + [ANY] * len(grads),
        out_specs=[specs[0]] * 3,
        out_shape=[jax.ShapeDtypeStruct(back.shape, bf16)] * 3,
        input_output_aliases={5 + i: i for i in range(len(grads))},
        compiler_params=pltpu.CompilerParams(vmem_limit_bytes=VMEM),
        cost_estimate=pl.CostEstimate(flops=3_000_000_000, bytes_accessed=MIB, transcendentals=0),
        name=f"attend_back_{first}",
    )


def proj_grads_kernel(place, turned, small_ref, db1_ref, dq, dk, dv, keep, send, grads, packed, bias, sem, wsem):
    step = pl.program_id(0)
    copies = [pltpu.make_async_copy(v, grads.at[i], sem.at[i]) for i, v in enumerate((dq, dk, dv))]

    @pl.when(step == 0)
    def _():
        start_all([copies[1], copies[2], copies[0]])

    for turn, which in enumerate((1, 2, 0)):

        @pl.when(step == turn)
        def _():
            copies[which].wait()
            g = dot(turned[...], grads[which]).astype(bf16)
            if which == 1:
                packed[:, D:QKV_HALF] = g[:, : D // 2]
                packed[:, QKV_BLOCK : QKV_BLOCK + D // 2] = g[:, D // 2 :]
            else:
                at = 0 if which == 0 else QKV_BLOCK + D // 2
                packed[:, at : at + D] = g
                bias[which // 2] = fold_rows(grads[which].astype(f32))

    @pl.when(step == 0)
    def _():
        owner = lax.broadcasted_iota(jnp.int32, (SLABS, FF), 1) // (4 * SLAB)
        one = lax.broadcasted_iota(jnp.int32, (SLABS, FF), 0)
        mine = jnp.where(owner == one, jnp.sum(db1_ref[...], axis=0, keepdims=True), 0.0)
        place_of = lax.broadcasted_iota(jnp.int32, (FF, 128), 0) % (4 * SLAB)
        pick = (place_of == lax.broadcasted_iota(jnp.int32, (FF, 128), 1)).astype(f32)
        table = lax.dot_general(
            mine, pick, (((1,), (0,)), ((), ())), precision=lax.Precision.HIGHEST, preferred_element_type=f32
        )
        spread = jnp.broadcast_to(table[:, None, :], (SLABS, SLAB, 128)).reshape(D, 128)
        packed[:, QKV_BLOCK + QKV_HALF :] = spread.astype(bf16)

    def give(half):
        for chip in range(CHIPS):
            block = packed.at[pl.ds(chip * PAIR_ROWS, PAIR_ROWS), pl.ds(half * QKV_BLOCK, QKV_BLOCK)]
            hand_over(place, chip, half, keep, send, [(block, pl.ds(0, QKV_BLOCK))], wsem)

    @pl.when(step == 1)
    def _():
        give(1)

    @pl.when(step == 2)
    def _():
        rows_of = [bias[...], small_ref[...], jnp.zeros((120, 8, D), f32)]
        packed[:, QKV_HALF:QKV_BLOCK] = jnp.sum(jnp.concatenate(rows_of, axis=0), axis=1).T.astype(bf16)
        give(0)
        wait_whole(keep, wsem)
        wait_whole(send, wsem)


def proj_grads(place, turned, small, inner_bias_grad, grads, deps=()):
    count = turned.shape[1]
    return call(
        proj_grads_kernel,
        (place, turned, small, inner_bias_grad, *grads),
        deps,
        grid=(3,),
        in_specs=[SMEM, whole(D, count), whole(6, 8, D), whole(8, FF), ANY, ANY, ANY],
        out_specs=[ANY, ANY],
        out_shape=[jax.ShapeDtypeStruct((CHIPS, PAIR_ROWS, QKV_BLOCK), bf16)] * 2,
        scratch_shapes=[
            pltpu.VMEM((3, count, D), bf16),
            pltpu.VMEM((D, 2 * QKV_BLOCK), bf16),
            pltpu.VMEM((2, 8, D), f32),
            pltpu.SemaphoreType.DMA((3,)),
            pltpu.SemaphoreType.DMA,
        ],
        compiler_params=pltpu.CompilerParams(vmem_limit_bytes=VMEM),
        cost_estimate=pl.CostEstimate(flops=4_000_000_000, bytes_accessed=MIB, transcendentals=0),
        name="proj_grads",
    )


def input_back_kernel(fb_ref, dq_ref, dk_ref, dv_ref, w_ref, *refs):
    half = D // 2
    total = fb_ref[...] + dot_t(dq_ref[...], w_ref[:, 0:D])
    total = total + dot_t(dk_ref[:, :half], w_ref[:, D:QKV_HALF])
    total = total + dot_t(dk_ref[:, half:], w_ref[:, PROJ_BLOCK : PROJ_BLOCK + half])
    out_ref, small_ref = refs[-2:]
    small_ref[...] = total[0:8, 0:128]
    out_ref[...] = total + dot_t(dv_ref[...], w_ref[:, PROJ_BLOCK + half : PROJ_BLOCK + QKV_HALF])


def input_back(first, blocks, first_back, grads, weights, given=(), deps=()):
    token = pl.BlockSpec((BLOCK, D), lambda s: (first + s, 0))
    return call(
        input_back_kernel,
        (first_back, *grads, weights, *given),
        deps,
        grid=(blocks,),
        in_specs=[token] * 4 + [whole(D, 2 * PROJ_BLOCK)] + [ANY] * len(given),
        out_specs=[token, whole(8, 128)],
        out_shape=[jax.ShapeDtypeStruct(first_back.shape, f32), jax.ShapeDtypeStruct((8, 128), f32)],
        input_output_aliases={5: 0} if given else {},
        compiler_params=pltpu.CompilerParams(vmem_limit_bytes=VMEM),
        cost_estimate=pl.CostEstimate(flops=1000, bytes_accessed=1000, transcendentals=0),
        name=f"input_back_{first}",
    )


def add_up_kernel(jobs, passed, place, *refs):
    refs[len(refs) - 1][...] = refs[0][0, 0:8, 0:128].astype(f32)
    first, out = 0, sum(count for count, _ in jobs) + passed
    for count, kind in jobs:
        terms = [ref[...].astype(f32) for ref in refs[first : first + count]]
        first += count
        total = sum(terms[1:], terms[0])
        if kind == "upper":
            results = [total.astype(bf16)]
        elif kind == "both":
            half = total.shape[0] // 2
            results = [total[half:].astype(bf16), total[:half]]
        elif kind == "down":
            results = [jnp.concatenate([total[0, :, :D], total[0, :, D:]], axis=0)]
        else:
            low_core = place[1] == 0
            low, high = total[0, :SLAB], total[0, SLAB:]
            results = [jnp.where(low_core, low, high), jnp.where(low_core, high, low)]
        for result in results:
            refs[out][...] = result.astype(refs[out].dtype)
            out += 1


def add_up(place, *groups, passed=(), deps=(), vmem=VMEM):
    operands, specs, out_specs, shapes, jobs = [], [], [], [], []
    steps = 3 if any(size == CHIPS for size, _ in groups) else 1
    one_step = all(size > 1 for size, _ in groups)
    steps = steps if one_step else 1
    for size, terms in groups:
        _, rows, lanes = terms[0].shape
        half, block = size // 2, rows // steps
        kind = "upper" if size == CHIPS else "both" if size > 1 else "down" if lanes == DOWN_BLOCK else "halves"
        operands += terms
        take = (half, 1) if kind == "upper" else (size, 0)
        specs += [pl.BlockSpec((take[0], block, lanes), lambda s, at=take[1]: (at, s, 0))] * len(terms)
        if size > 1:
            kinds = [bf16] if kind == "upper" else [bf16, f32]
            out_specs += [pl.BlockSpec((half, block, lanes), lambda s: (0, s, 0))] * len(kinds)
            shapes += [jax.ShapeDtypeStruct((half, rows, lanes), dtype) for dtype in kinds]
        else:
            ends = [(2 * PAIR_ROWS, D)] if kind == "down" else [(SLAB, lanes)] * 2
            out_specs += [whole(*end) for end in ends]
            shapes += [jax.ShapeDtypeStruct(end, f32) for end in ends]
        jobs.append((len(terms), kind))
    return call(
        lambda *refs: add_up_kernel(jobs, len(passed), refs[0], *refs[1:]),
        [place] + operands + list(passed),
        deps,
        grid=(steps,),
        in_specs=[SMEM] + specs + [ANY] * len(passed),
        out_specs=out_specs + [ANY] * len(passed) + [whole(8, 128)],
        out_shape=shapes
        + [jax.ShapeDtypeStruct(v.shape, v.dtype) for v in passed]
        + [jax.ShapeDtypeStruct((8, 128), f32)],
        input_output_aliases={1 + len(operands) + i: len(shapes) + i for i in range(len(passed))},
        compiler_params=pltpu.CompilerParams(vmem_limit_bytes=vmem),
        cost_estimate=pl.CostEstimate(flops=1000, bytes_accessed=1000, transcendentals=0),
        name="add_up",
    )


def finish_inner_kernel(place, mine, other, out_g, inner_g, small):
    low_core = place[1] == 0
    low = jnp.where(low_core, mine[...], other[...])
    high = jnp.where(low_core, other[...], mine[...])
    out_g[:, :OUT_HALF], out_g[:, OUT_HALF:] = low[:, :OUT_HALF], high[:, :OUT_HALF]
    inner_g[:, :INNER_HALF], inner_g[:, INNER_HALF:] = low[:, OUT_HALF:], high[:, OUT_HALF:]
    small[...] = low[0:8, 0:128]


def finish_proj_kernel(place, mine, other, dq, dk, dv, bias, *vectors):
    low_core = place[1] == 0
    low = jnp.where(low_core, mine[...], other[...])
    high = jnp.where(low_core, other[...], mine[...])
    half = D // 2
    dq[...] = low[:, :D]
    dk[:, :half], dk[:, half:] = low[:, D:QKV_HALF], high[:, :half]
    dv[...] = high[:, half:QKV_HALF]
    bias[...] = high[0, QKV_HALF : QKV_HALF + 4 * SLAB]
    rows = low[:, QKV_HALF:].T
    for i, out in enumerate(vectors):
        out[...] = rows[i, 0:SLAB]


def finish(kernel, place, mine, other, shapes, name, deps=()):
    at = lambda shape: pl.BlockSpec(shape, lambda s: (0,) * len(shape))
    return call(
        kernel,
        (place, mine, other),
        deps,
        grid=(1,),
        in_specs=[SMEM, at(mine.shape), at(mine.shape)],
        out_specs=[at(shape) for shape in shapes],
        out_shape=[jax.ShapeDtypeStruct(shape, f32) for shape in shapes],
        compiler_params=pltpu.CompilerParams(vmem_limit_bytes=LITTLE),
        cost_estimate=pl.CostEstimate(flops=1000, bytes_accessed=1000, transcendentals=0),
        name=name,
    )


def finish_inner(place, mine, other):
    return finish(finish_inner_kernel, place, mine, other, [(SLAB, D), (SLAB, FF), (8, 128)], "finish_inner")


def finish_proj(place, mine, other, deps=()):
    shapes = [(SLAB, D)] * 3 + [(4 * SLAB,)] + [(SLAB,)] * 8
    return finish(finish_proj_kernel, place, mine, other, shapes, "finish_proj", deps)


AXES = ("dp", "fsdp")


CORE = (1, 1)
ALONG_Z_FIRST, ALONG_Z_THEN, ALONG_Z_BOTH, ALONG_XY_FIRST, ALONG_XY_THEN = (16, 8), (8, 16), (24, 24), (2, 4), (4, 2)
FAST_SHAPE = {"dp": 4, "fsdp": 8}


def move(v, masks):
    return lax.ppermute(v, AXES, [(i, i ^ masks[i & 1]) for i in range(SLABS)])


SUM_STEPS = (ALONG_XY_THEN, ALONG_XY_FIRST, ALONG_Z_THEN, ALONG_Z_FIRST)


def after(*values):
    return lax.optimization_barrier(values)


class Sums:
    def __init__(self, keep, got):
        self.size, self.terms, self.step = CHIPS, [keep, got], 0

    def job(self):
        return self.size, self.terms

    def send(self, outs):
        ready = outs.pop(0)
        if self.size < CHIPS:
            self.terms = [outs.pop(0)]
        self.size //= 2
        self.terms = self.terms + [move(ready, SUM_STEPS[self.step])]
        self.step += 1


def add_and_send(place, *groups, **options):
    outs = list(add_up(place, *[g.job() for g in groups], **options))
    for g in groups:
        if g.size > 1:
            g.send(outs)
    return outs


def fast_blocks(shards, core):
    (qw, kw, vw, ow, qb, vb, ob, fg, fs, iw, ib, dw, db, sg, ss) = shards
    vectors = jnp.pad(jnp.stack([qb, vb, ob, fg, fs, db, sg, ss], axis=1), ((0, 0), (0, 120)))
    inner_bias = jnp.pad(ib.reshape(1, 4 * SLAB), ((0, SLAB - 1), (0, 128 - 4 * SLAB)))
    half = D // 2
    halves = [
        jnp.concatenate([qw, kw[:, :half], vectors, ow[:, :half], iw[:, :INNER_HALF]], axis=1),
        jnp.concatenate([kw[:, half:], vw, inner_bias, ow[:, half:], iw[:, INNER_HALF:]], axis=1),
    ]
    low_core = core == 0
    own = jnp.where(low_core, halves[0], halves[1])
    other = move(jnp.where(low_core, halves[1], halves[0]), CORE)
    rows = jnp.concatenate([jnp.where(low_core, own, other), jnp.where(low_core, other, own)], axis=0)
    return rows[:, :PROJ_BLOCK], rows[:, PROJ_BLOCK:], jnp.concatenate([dw[:PAIR_ROWS], dw[PAIR_ROWS:]], axis=1)


def gather_plain(shards):
    (qw, kw, vw, ow, qb, vb, ob, fg, fs, iw, ib, dw, db, sg, ss) = [
        lax.all_gather(v, AXES, axis=0, tiled=True) for v in shards
    ]
    vectors = jnp.pad(jnp.stack([qb, vb, ob, fg, fs, db, sg, ss], axis=1), ((0, 0), (0, 120)))
    inner_bias = jnp.pad(ib.reshape(SLABS, 1, 4 * SLAB), ((0, 0), (0, SLAB - 1), (0, 128 - 4 * SLAB))).reshape(D, 128)
    half = D // 2
    chips = lambda v: v.reshape(CHIPS, PAIR_ROWS, -1)
    down = dw.reshape(CHIPS, 2, 2, PAIR_ROWS, D)
    first = [
        chips(jnp.concatenate([qw, kw[:, :half], vectors, ow[:, :half]], axis=1)),
        chips(jnp.concatenate([kw[:, half:], vw, inner_bias, ow[:, half:]], axis=1)),
    ]
    second = [
        jnp.concatenate([chips(iw[:, c * INNER_HALF : (c + 1) * INNER_HALF]), down[:, c, 0], down[:, c, 1]], axis=2)
        for c in range(2)
    ]
    slots = lambda halves: [v[np.array(SLOT_CHIPS[c])] for c, v in enumerate(halves)]
    return slots(first), slots(second)


def local(fast, inputs, lengths, *rest):
    shards, cotangent = rest[:15], rest[15]
    both = lambda v, came: jnp.concatenate([v, came])
    if fast:
        linear = lax.axis_index(AXES)
        core = linear & 1
        place = jnp.stack([linear >> 1, core]).astype(jnp.int32)
        first, inner, down = fast_blocks(shards, core)
        first = first[None]
        first = both(first, move(first, ALONG_Z_FIRST))
        first, second = after(first, jnp.concatenate([inner, down], axis=1)[None])
        second = jnp.concatenate([second] + [move(second, steps) for steps in (ALONG_Z_FIRST, ALONG_Z_THEN, ALONG_Z_BOTH)])
        first = both(first, move(first, ALONG_Z_THEN))
        first_then, first_core = move(first, ALONG_XY_THEN), move(first, CORE)
        first_came = move(first, ALONG_XY_FIRST)
        first_last, came_core = move(first_came, ALONG_XY_THEN), move(first_came, CORE)
        first_then, first_last, second = after(first_then, first_last, second)
        first = [first, first_came, first_then, first_last]
        first += [first_core, came_core, move(first_then, CORE), move(first_last, CORE)]
        second_came, second_then, second_core = move(second, ALONG_XY_FIRST), move(second, ALONG_XY_THEN), move(second, CORE)
        meta = tuple((at, other) for other in (False, True) for at in range(0, CHIPS, 4))
    else:
        place = jnp.zeros((2,), jnp.int32)
        first, second = gather_plain(shards)
        meta = ((0, False), (0, True))
    qkv, attended, stats, weights, vectors = attend(place, lengths, inputs, first, meta)
    prob = probs(0, lengths, qkv, stats)
    if fast:
        second_came, prob = after(second_came, prob)
        second_last, came_core = move(second_came, ALONG_XY_THEN), move(second_came, CORE)
    prob, normed, rstd, hid, inputs_t, attended_t, hid_t = window(
        1, lengths, inputs, qkv, attended, stats, weights, vectors, prob
    )
    bias_at = PROJ_BLOCK + QKV_HALF
    inner_bias = weights[::SLAB, bias_at : bias_at + 4 * SLAB].reshape(1, FF).astype(f32)
    if fast:
        second_then, second_last, normed, inner_bias = after(second_then, second_last, normed, inner_bias)
        second = [second, second_came, second_then, second_last]
        second += [second_core, came_core, move(second_then, CORE), move(second_last, CORE)]
    output, first_back, back, inner_back, branch, small, db1, down_keep, down_send = feed_forward(
        place, normed, rstd, hid, cotangent, vectors, inner_bias, weights, second, meta
    )
    inner_keep, inner_send = inner_grads(place, hid_t, inner_back, attended_t, branch)
    pairs = lengths.shape[0] * (H // 2)
    third = pairs // 3
    deps = []
    if fast:
        down = Sums(down_keep, move(down_send, CORE))
        inner_send, *deps = add_and_send(place, down, passed=[inner_send], deps=[inner_keep])
        inner = Sums(inner_keep, move(inner_send, CORE))
    grads = attend_back(0, third, qkv, back, prob, deps=deps)
    if fast:
        deps = add_and_send(place, inner, deps=grads[:1])
    grads = attend_back(third, third, qkv, back, prob, grads, deps=deps)
    if fast:
        deps = add_and_send(place, down, deps=grads[:1])
    grads = attend_back(2 * third, pairs - 2 * third, qkv, back, prob, grads, deps=deps)
    if fast:
        deps = add_and_send(place, inner, down, deps=grads[:1])
    proj_keep, proj_send = proj_grads(place, inputs_t, small, db1, grads, deps=deps)
    blocks = inputs.shape[0] // BLOCK
    early = blocks // 2
    if fast:
        proj_send, *deps = add_and_send(place, inner, down, passed=[proj_send], deps=[proj_keep])
        proj = Sums(proj_keep, move(proj_send, CORE))
        grad_input, *deps = input_back(0, early, first_back, grads, weights, deps=deps)
        down_grad, *deps = add_and_send(place, proj, down, deps=deps)
        grad_input, *deps = input_back(early, blocks - early, first_back, grads, weights, [grad_input], deps=deps)
        deps = add_and_send(place, proj, inner, deps=deps, vmem=LITTLE)
        mine, other, *deps = add_and_send(place, proj, inner, deps=deps, vmem=LITTLE)
        out_grad, inner_grad, *deps = finish_inner(place, mine, move(other, CORE))
        add_and_send(place, proj, deps=deps, vmem=LITTLE)
        mine, other, _ = add_and_send(place, proj, vmem=LITTLE)
        *square, bias, v0, v1, v2, v3, v4, v5, v6, v7 = finish_proj(place, mine, move(other, CORE))
        vectors = [v0, v1, v2, v3, v4, v5, v6, v7]
    else:
        grad_input, _ = input_back(0, blocks, first_back, grads, weights)
        shard = lambda *v: lax.psum_scatter(jnp.concatenate(v, axis=1), AXES, scatter_dimension=0, tiled=True)
        by_chip = lambda pair: [v[np.argsort(np.array(SLOT_CHIPS[c]))].astype(f32) for c, v in enumerate(pair)]
        low, high = (v.reshape(D, -1) for v in by_chip((inner_keep, inner_send)))
        out_grad, inner_grad = shard(low[:, :OUT_HALF], high[:, :OUT_HALF]), shard(low[:, OUT_HALF:], high[:, OUT_HALF:])
        parts = [jnp.stack([v[:, :, :D], v[:, :, D:]], axis=1) for v in by_chip((down_keep, down_send))]
        down_grad = shard(jnp.stack(parts, axis=1).reshape(FF, D))
        low, high = (v.reshape(D, -1) for v in by_chip((proj_keep, proj_send)))
        half = D // 2
        square = shard(low[:, :D]), shard(low[:, D:QKV_HALF], high[:, :half]), shard(high[:, half:QKV_HALF])
        columns = shard(low[:, QKV_HALF:])
        vectors = [columns[:, i] for i in range(8)]
        bias = shard(high[::SLAB, QKV_HALF : QKV_HALF + 4 * SLAB].reshape(FF, 1))[:, 0]
    return (
        output,
        grad_input,
        *square,
        out_grad,
        *vectors[:5],
        inner_grad,
        bias,
        down_grad,
        *vectors[5:],
    )


def solution(mesh):
    rows, flat = P(AXES, None), P(AXES)
    params = (rows,) * 4 + (flat,) * 5 + (rows, flat, rows, flat, flat, flat)
    return jax.shard_map(
        functools.partial(local, dict(mesh.shape) == FAST_SHAPE),
        mesh=mesh,
        in_specs=(rows, flat) + params + (rows,),
        out_specs=(rows, rows) + params,
        check_vma=False,
    )
```

```python
import functools
import math

import jax
import jax.numpy as jnp
import numpy as np
from jax import lax
from jax.experimental import pallas as pl
from jax.experimental.pallas import tpu as pltpu
from jax.sharding import PartitionSpec as P

D = 768
H = 12
DH = 64
FF = 3072
SLABS = 32
SLAB = D // SLABS
CHIPS = SLABS // 2
PAIR_ROWS = 2 * SLAB
NORM_EPSILON = 1e-12
MASKED_SCORE = -1000000000.0
GAUSS_DENSITY = 0.3989422804014327
LOG2E = 1.4426950408889634
MIB = 1 << 20
VMEM = 62 * MIB
ALL_VMEM = 127 * MIB // 2
LITTLE = 16 * MIB

QKV_HALF = 3 * D // 2
QKV_BLOCK = QKV_HALF + 128
OUT_HALF = D // 2
PROJ_BLOCK = QKV_BLOCK + OUT_HALF
INNER_HALF = FF // 2
INNER_BLOCK = OUT_HALF + INNER_HALF
DOWN_BLOCK = 2 * D

SLOT_BITS = ((8, 4, 1, 2), (4, 8, 2, 1))
SLOT_CHIPS = tuple(
    tuple(sum(bit for i, bit in enumerate(bits) if slot >> i & 1) for slot in range(CHIPS)) for bits in SLOT_BITS
)

bf16 = jnp.bfloat16
f32 = jnp.float32
ANY = pl.BlockSpec(memory_space=pl.ANY)
SMEM = pl.BlockSpec(memory_space=pltpu.SMEM)


def dot(a, b):
    return lax.dot_general(a, b, (((1,), (0,)), ((), ())), preferred_element_type=f32)


def dot_t(a, b):
    return lax.dot_general(a, b, (((1,), (1,)), ((), ())), preferred_element_type=f32)


def dot_l(a, b):
    return lax.dot_general(a, b, (((0,), (0,)), ((), ())), preferred_element_type=f32)


def call(kernel, operands, deps, in_specs, **options):
    count = len(operands)

    def body(*refs):
        kernel(*refs[:count], *refs[count + len(deps) :])

    in_specs = in_specs + [whole(8, 128) if v.shape == (8, 128) else ANY for v in deps]
    return pl.pallas_call(body, in_specs=in_specs, **options)(*operands, *deps)


def aligned(start, size, unit):
    return pl.ds(pl.multiple_of(start, unit), size)


def chip_of(slot, half):
    return jnp.where(half == 0, SLOT_CHIPS[0][slot], SLOT_CHIPS[1][slot])


def slot_of(chip, half):
    bits = SLOT_BITS[half]
    return sum(jnp.where((chip & bit) != 0, 1 << i, 0) for i, bit in enumerate(bits))


def blocks_of(place, pieces):
    for ref, (first, other) in pieces:
        half = 1 - place[1] if other else place[1]
        for i in range(ref.shape[0]):
            yield ref, i, place[0] ^ chip_of(first + i, half), half


def proj_blocks(place, pieces, weights, sem):
    for ref, i, chip, half in blocks_of(place, pieces):
        rows = aligned(chip * PAIR_ROWS, PAIR_ROWS, 16)
        yield pltpu.make_async_copy(ref.at[i], weights.at[rows, aligned(half * PROJ_BLOCK, PROJ_BLOCK, 128)], sem)


def inner_blocks(place, pieces, inner_w, sem):
    for ref, i, chip, half in blocks_of(place, pieces):
        rows = aligned(chip * PAIR_ROWS, PAIR_ROWS, 16)
        yield pltpu.make_async_copy(
            ref.at[i, :, pl.ds(0, INNER_HALF)],
            inner_w.at[rows, aligned(half * INNER_HALF, INNER_HALF, 128)],
            sem,
        )


def down_blocks(place, pieces, down_w, sem):
    for ref, i, chip, half in blocks_of(place, pieces):
        for k in range(2):
            at = (chip * 2 + half) * (2 * PAIR_ROWS) + k * PAIR_ROWS
            yield pltpu.make_async_copy(
                ref.at[i, :, pl.ds(INNER_HALF + k * D, D)], down_w.at[aligned(at, PAIR_ROWS, 16), :], sem
            )


def start_all(copies):
    for c in copies:
        c.start()


def whole(*shape):
    return pl.BlockSpec(shape, lambda *s: (0,) * len(shape))


def fold_rows(v):
    return jnp.sum(v.reshape(v.shape[0] // 8, 8, v.shape[1]), axis=0)


def hand_over(place, chip, half, keep, send, pairs, sem):
    slot = slot_of(chip ^ place[0], half)
    for mine, out in ((True, keep), (False, send)):

        @pl.when((place[1] == half) == mine)
        def _():
            for source, lanes in pairs:
                pltpu.make_async_copy(source, out.at[slot, :, lanes], sem).start()


def wait_whole(ref, sem):
    pltpu.make_async_copy(ref, ref, sem).wait()


def lane_masks():
    low = (lax.broadcasted_iota(jnp.int32, (1, 128), 1) < DH).astype(f32)
    return low.astype(bf16), (1.0 - low).astype(bf16)


def attend_kernel(meta, n_pieces, place, lengths, x_ref, *refs):
    piece_refs = refs[:n_pieces]
    qkv_ref, att_ref, stat_ref, weights, vectors = refs[n_pieces : n_pieces + 5]
    sem = refs[-1]
    seq = pl.program_id(0)
    rows = x_ref.shape[0]

    @pl.when(seq == 0)
    def _():
        start_all(proj_blocks(place, zip(piece_refs, meta), weights, sem))
        wait_whole(weights, sem)
        small = weights[:, QKV_HALF:QKV_BLOCK].astype(f32)
        vectors[...] = small.T[0:16, :]

    lowered = x_ref[...].astype(bf16)
    first = dot(lowered, weights[:, 0:QKV_HALF])
    qkv_ref[:, 0:D] = (first[:, 0:D] + vectors[0:1, :]).astype(bf16)
    qkv_ref[:, D:QKV_HALF] = first[:, D:QKV_HALF].astype(bf16)
    second = dot(lowered, weights[:, PROJ_BLOCK : PROJ_BLOCK + QKV_HALF])
    qkv_ref[:, QKV_HALF : 2 * D] = second[:, 0 : D // 2].astype(bf16)
    qkv_ref[:, 2 * D :] = (second[:, D // 2 :] + vectors[1:2, :]).astype(bf16)

    low, high = lane_masks()
    lane = lax.broadcasted_iota(jnp.int32, (1, 128), 1)
    key_at = lax.broadcasted_iota(jnp.int32, (1, rows), 1)
    hidden_keys = jnp.where(key_at < lengths[seq], 0.0, MASKED_SCORE).astype(f32)
    chunk = 256
    ones = jnp.ones((rows, 128), bf16)
    stats = [jnp.zeros((chunk, 128), f32) for _ in range(rows // chunk)]
    for pair in range(H // 2):
        at = pair * 128
        keys = qkv_ref[:, D + at : D + at + 128]
        values = jnp.concatenate([qkv_ref[:, 2 * D + at : 2 * D + at + 128], ones], axis=1)
        keys_of = (keys * low, keys * high)
        for c in range(rows // chunk):
            span = pl.ds(c * chunk, chunk)
            queries = qkv_ref[span, at : at + 128]
            outs = []
            for i in range(2):
                scores = dot_t(queries, keys_of[i]) * (0.125 * LOG2E) + hidden_keys
                peak = jnp.max(scores, axis=-1, keepdims=True)
                weight = jnp.exp2(scores - peak).astype(bf16)
                both = dot(weight, values)
                total = both[:, 128:]
                outs.append(both[:, :128] / total)
                log_total = peak + jnp.log2(total)
                stats[c] = jnp.where(lane == 2 * pair + i, log_total, stats[c])
            att_ref[span, at : at + 128] = jnp.where(lane < DH, outs[0], outs[1]).astype(bf16)
    for c in range(rows // chunk):
        stat_ref[0, :, c * chunk : (c + 1) * chunk] = stats[c].T[0:16, :]


def attend(place, lengths, x, pieces, meta):
    rows = x.shape[0] // lengths.shape[0]
    seqs = lengths.shape[0]
    return pl.pallas_call(
        functools.partial(attend_kernel, meta, len(pieces)),
        grid=(seqs,),
        in_specs=[SMEM, SMEM, pl.BlockSpec((rows, D), lambda s: (s, 0))] + [ANY] * len(pieces),
        out_specs=[
            pl.BlockSpec((rows, 3 * D), lambda s: (s, 0)),
            pl.BlockSpec((rows, D), lambda s: (s, 0)),
            pl.BlockSpec((1, 16, rows), lambda s: (s, 0, 0)),
            whole(D, 2 * PROJ_BLOCK),
            whole(16, D),
        ],
        out_shape=[
            jax.ShapeDtypeStruct((seqs * rows, 3 * D), bf16),
            jax.ShapeDtypeStruct((seqs * rows, D), bf16),
            jax.ShapeDtypeStruct((seqs, 16, rows), f32),
            jax.ShapeDtypeStruct((D, 2 * PROJ_BLOCK), bf16),
            jax.ShapeDtypeStruct((16, D), f32),
        ],
        scratch_shapes=[pltpu.SemaphoreType.DMA],
        compiler_params=pltpu.CompilerParams(vmem_limit_bytes=VMEM),
        cost_estimate=pl.CostEstimate(flops=18_000_000_000, bytes_accessed=20 * MIB, transcendentals=0),
        name="attend",
    )(place, lengths, x, *pieces)


def gelu_parts(u):
    size = jnp.abs(u)
    bell = jnp.exp2(u * u * (-0.5 * LOG2E))
    t = 1.0 / (1.0 + (0.3275911 * math.sqrt(0.5)) * size)
    poly = t * (0.127414796 + t * (-0.142248368 + t * (0.7107068705 + t * (-0.7265760135 + t * 0.5307027145))))
    tail = poly * bell
    below = jnp.where(u < 0.0, tail, 1.0 - tail)
    return below, bell


def mean_rows(v):
    return jnp.sum(v, axis=-1, keepdims=True) * (1.0 / D)


def norm_rows(total):
    center = total - mean_rows(total)
    rstd = lax.rsqrt(mean_rows(center * center) + NORM_EPSILON)
    return center * rstd, rstd


def norm_back(upstream, normed, rstd, gain):
    scaled = upstream * gain
    return rstd * (scaled - mean_rows(scaled) - normed * mean_rows(scaled * normed))


BLOCK = 256
WIDTH = 768
DOWN_STEPS = 8


def out_weight_copies(proj_w, out_w, sem):
    for half in range(2):
        lanes = pl.ds(half * PROJ_BLOCK + QKV_BLOCK, OUT_HALF)
        yield pltpu.make_async_copy(proj_w.at[:, lanes], out_w.at[:, pl.ds(half * OUT_HALF, OUT_HALF)], sem)


def probs_kernel(seq, lengths, q_ref, k_ref, stat_ref, *refs):
    prob_ref = refs[-1]
    pair = pl.program_id(0)
    rows = q_ref.shape[0]
    chunk = 256
    key_at = lax.broadcasted_iota(jnp.int32, (rows, 1), 0)
    hidden_keys = jnp.where(key_at < lengths[seq], 0.0, MASKED_SCORE).astype(f32)
    for i, mask in enumerate(lane_masks()):
        own_keys = k_ref[...] * mask
        for c in range(rows // chunk):
            span = slice(c * chunk, (c + 1) * chunk)
            log_total = stat_ref[0, pl.ds(2 * pair + i, 1), span]
            scores = dot_t(own_keys, q_ref[span, :]) * (0.125 * LOG2E) + hidden_keys
            prob_ref[i, :, span] = jnp.exp2(scores - log_total).astype(bf16)


def probs_specs(seq, rows):
    pairs = H // 2
    lane = lambda kind: pl.BlockSpec((rows, 128), lambda s: (seq, kind * pairs + s))
    specs = [SMEM, lane(0), lane(1), pl.BlockSpec((1, 16, rows), lambda s: (seq, 0, 0))]
    return specs, pl.BlockSpec((2, rows, rows), lambda s: (seq * pairs + s, 0, 0))


def probs(seq, lengths, qkv, stats, deps=()):
    seqs, _, rows = stats.shape
    specs, out = probs_specs(seq, rows)
    return call(
        functools.partial(probs_kernel, seq),
        (lengths, qkv, qkv, stats),
        deps,
        grid=(H // 2,),
        in_specs=specs,
        out_specs=out,
        out_shape=jax.ShapeDtypeStruct((seqs * H, rows, rows), bf16),
        compiler_params=pltpu.CompilerParams(vmem_limit_bytes=VMEM),
        cost_estimate=pl.CostEstimate(flops=8_000_000_000, bytes_accessed=MIB, transcendentals=0),
        name="probs",
    )


def window_kernel(seq, blocks, lengths, q_ref, k_ref, stat_ref, _, x_ref, att_ref, vec_ref, proj_w, *refs):
    prob_ref, normed_ref, rstd_ref, hid_ref, x_t, att_t, hid_t, out_w, sem = refs
    g = pl.program_id(0)

    @pl.when(g == 0)
    def _():
        start_all(out_weight_copies(proj_w, out_w, sem))

    probs_kernel(seq, lengths, q_ref, k_ref, stat_ref, prob_ref)

    @pl.when(g == 0)
    def _():
        wait_whole(out_w, sem)

    @pl.when(g < blocks)
    def _():
        x, attended = x_ref[...], att_ref[...]
        normed, rstd = norm_rows(x + dot(attended, out_w[...]) + vec_ref[2:3, :])
        normed_ref[...] = normed
        rstd_ref[...] = jnp.broadcast_to(rstd, rstd_ref.shape)
        hidden = normed * vec_ref[3:4, :] + vec_ref[4:5, :]
        hid_ref[...] = hidden.astype(bf16)
        x_t[...] = x.T.astype(bf16)
        att_t[...] = attended.astype(f32).T.astype(bf16)
        hid_t[...] = hidden.T.astype(bf16)


def window(seq, lengths, x, qkv, attended, stats, weights, vectors, prob, deps=()):
    count = x.shape[0]
    _, _, rows = stats.shape
    blocks = count // BLOCK
    block = lambda s: jnp.minimum(s, blocks - 1)
    token = lambda width: pl.BlockSpec((BLOCK, width), lambda s: (block(s), 0))
    turned = pl.BlockSpec((D, BLOCK), lambda s: (0, block(s)))
    specs, out = probs_specs(seq, rows)
    return call(
        functools.partial(window_kernel, seq, blocks),
        (lengths, qkv, qkv, stats, prob, x, attended, vectors, weights),
        deps,
        grid=(H // 2,),
        in_specs=specs + [ANY, token(D), token(D), whole(16, D), ANY],
        out_specs=[out, token(D), token(128), token(D)] + [turned] * 3,
        out_shape=[
            jax.ShapeDtypeStruct(prob.shape, bf16),
            jax.ShapeDtypeStruct((count, D), f32),
            jax.ShapeDtypeStruct((count, 128), f32),
            jax.ShapeDtypeStruct((count, D), bf16),
        ]
        + [jax.ShapeDtypeStruct((D, count), bf16)] * 3,
        input_output_aliases={4: 0},
        scratch_shapes=[pltpu.VMEM((D, D), bf16), pltpu.SemaphoreType.DMA],
        compiler_params=pltpu.CompilerParams(vmem_limit_bytes=VMEM),
        cost_estimate=pl.CostEstimate(flops=14_000_000_000, bytes_accessed=MIB, transcendentals=0),
        name="window",
    )


def ffn_kernel(meta, pieces, blocks, place, normed_ref, rstd_ref, hid_ref, cot_ref, vec_ref, b1_ref, proj_w, *refs):
    piece_refs = refs[:pieces]
    (out_ref, fb_ref, ab_ref, ib_ref, branch_ref, small_ref, db1_ref, keep, send) = refs[pieces : pieces + 9]
    (out_w, inner_w, down_w, act, down_back, sem, wsem) = refs[pieces + 9 :]
    step = pl.program_id(0)

    @pl.when(step == 0)
    def _():
        start_all(inner_blocks(place, zip(piece_refs, meta), inner_w, sem.at[0]))
        start_all(down_blocks(place, zip(piece_refs, meta), down_w, sem.at[1]))
        start_all(out_weight_copies(proj_w, out_w, sem.at[2]))
        small_ref[...] = jnp.zeros_like(small_ref)
        db1_ref[...] = jnp.zeros_like(db1_ref)
        wait_whole(inner_w, sem.at[0])
        wait_whole(down_w, sem.at[1])
        wait_whole(out_w, sem.at[2])

    @pl.when(step < blocks)
    def _():
        rows = aligned(step * BLOCK, BLOCK, BLOCK)
        first_gain, first_shift = vec_ref[3:4, :], vec_ref[4:5, :]
        second_gain, second_shift = vec_ref[6:7, :], vec_ref[7:8, :]
        first_normed = normed_ref[...]
        hidden_low = hid_ref[...]
        total = first_normed * first_gain + first_shift + vec_ref[5:6, :]
        slopes = []
        for c in range(FF // WIDTH):
            cols = pl.ds(c * WIDTH, WIDTH)
            u = dot(hidden_low, inner_w[:, cols]) + b1_ref[:, cols]
            below, bell = gelu_parts(u)
            active = (u * below).astype(bf16)
            act[rows, cols] = active
            slopes.append(below + u * bell * GAUSS_DENSITY)
            total = total + dot(active, down_w[cols, :])
        second_normed, second_rstd = norm_rows(total)
        out_ref[...] = second_normed * second_gain + second_shift
        cot = cot_ref[...]
        second_back = norm_back(cot, second_normed, second_rstd, second_gain)
        back_low = second_back.astype(bf16)
        down_back[rows, :] = back_low
        hidden_back = second_back
        for c in range(FF // WIDTH):
            cols = pl.ds(c * WIDTH, WIDTH)
            ib = (dot_t(back_low, down_w[cols, :]) * slopes[c]).astype(bf16)
            ib_ref[:, cols] = ib
            db1_ref[:, cols] += fold_rows(ib.astype(f32))
            hidden_back = hidden_back + dot_t(ib, inner_w[:, cols])
        first_back = norm_back(hidden_back, first_normed, rstd_ref[:, 0:1], first_gain)
        fb_ref[...] = first_back
        branch_low = first_back.astype(bf16)
        branch_ref[...] = branch_low
        ab_ref[...] = dot_t(branch_low, out_w[...]).astype(bf16)
        sums = (
            branch_low.astype(f32),
            hidden_back * first_normed,
            hidden_back,
            back_low.astype(f32),
            cot * second_normed,
            cot,
        )
        for i, v in enumerate(sums):
            small_ref[i] += fold_rows(v)

    @pl.when(step >= blocks)
    def _():
        chunk = step - blocks
        width = FF // DOWN_STEPS
        rows = aligned(chunk * width, width, 128)
        down_w[rows, :] = dot_l(act[:, rows], down_back[...]).astype(bf16)
        for i in range(CHIPS // DOWN_STEPS):
            chip = chunk * (CHIPS // DOWN_STEPS) + i
            for half in range(2):
                at = (chip * 2 + half) * (2 * PAIR_ROWS)
                pairs = [
                    (down_w.at[aligned(at + k * PAIR_ROWS, PAIR_ROWS, 16)], pl.ds(k * D, D)) for k in range(2)
                ]
                hand_over(place, chip, half, keep, send, pairs, wsem)

    @pl.when(step == blocks + DOWN_STEPS - 1)
    def _():
        wait_whole(keep, wsem)
        wait_whole(send, wsem)


def feed_forward(place, normed, rstd, hid, cotangent, vectors, inner_bias, weights, pieces, meta):
    count = normed.shape[0]
    blocks = count // BLOCK
    token = lambda width: pl.BlockSpec((BLOCK, width), lambda s: (jnp.minimum(s, blocks - 1), 0))
    return pl.pallas_call(
        functools.partial(ffn_kernel, meta, len(pieces), blocks),
        grid=(blocks + DOWN_STEPS,),
        in_specs=[SMEM, token(D), token(128), token(D), token(D), whole(16, D), whole(1, FF), ANY]
        + [ANY] * len(pieces),
        out_specs=[token(D), token(D), token(D), token(FF), token(D), whole(6, 8, D), whole(8, FF), ANY, ANY],
        out_shape=[
            jax.ShapeDtypeStruct((count, D), f32),
            jax.ShapeDtypeStruct((count, D), f32),
            jax.ShapeDtypeStruct((count, D), bf16),
            jax.ShapeDtypeStruct((count, FF), bf16),
            jax.ShapeDtypeStruct((count, D), bf16),
            jax.ShapeDtypeStruct((6, 8, D), f32),
            jax.ShapeDtypeStruct((8, FF), f32),
            jax.ShapeDtypeStruct((CHIPS, PAIR_ROWS, DOWN_BLOCK), bf16),
            jax.ShapeDtypeStruct((CHIPS, PAIR_ROWS, DOWN_BLOCK), bf16),
        ],
        scratch_shapes=[
            pltpu.VMEM((D, D), bf16),
            pltpu.VMEM((D, FF), bf16),
            pltpu.VMEM((FF, D), bf16),
            pltpu.VMEM((count, FF), bf16),
            pltpu.VMEM((count, D), bf16),
            pltpu.SemaphoreType.DMA((3,)),
            pltpu.SemaphoreType.DMA,
        ],
        compiler_params=pltpu.CompilerParams(vmem_limit_bytes=ALL_VMEM),
        cost_estimate=pl.CostEstimate(flops=52_000_000_000, bytes_accessed=40 * MIB, transcendentals=0),
        name="feed_forward",
    )(place, normed, rstd, hid, cotangent, vectors, inner_bias, weights, *pieces)


def inner_grads_kernel(hid_t, ib_ref, place, att_in, branch_in, keep, send, att_t, branch, out_g, inner_g, sem, wsem):
    step = pl.program_id(0)
    steps = FF // D
    later = [pltpu.make_async_copy(att_in, att_t, sem.at[0]), pltpu.make_async_copy(branch_in, branch, sem.at[1])]

    @pl.when(step == 0)
    def _():
        start_all(later)

    def give(grads, half, width, lane):
        for chip in range(CHIPS):
            block = grads.at[pl.ds(chip * PAIR_ROWS, PAIR_ROWS), pl.ds(half * width, width)]
            hand_over(place, chip, half, keep, send, [(block, pl.ds(lane, width))], wsem)

    @pl.when(step < steps)
    def _():
        cols = aligned(step * D, D, 128)
        inner_g[:, cols] = dot(hid_t[...], ib_ref[...]).astype(bf16)
        for half in range(2):

            @pl.when(step == (half + 1) * (steps // 2) - 1)
            def _():
                give(inner_g, half, INNER_HALF, OUT_HALF)

    @pl.when(step == steps)
    def _():
        for copy in later:
            copy.wait()
        out_g[...] = dot(att_t[...], branch[...]).astype(bf16)
        for half in range(2):
            give(out_g, half, OUT_HALF, 0)
        wait_whole(keep, wsem)
        wait_whole(send, wsem)


def inner_grads(place, hid_t, inner_back, att_t, branch):
    count = hid_t.shape[1]
    steps = FF // D
    return pl.pallas_call(
        inner_grads_kernel,
        grid=(steps + 1,),
        in_specs=[
            whole(D, count),
            pl.BlockSpec((count, D), lambda s: (0, jnp.minimum(s, steps - 1))),
            SMEM,
            ANY,
            ANY,
        ],
        out_specs=[ANY, ANY],
        out_shape=[jax.ShapeDtypeStruct((CHIPS, PAIR_ROWS, INNER_BLOCK), bf16)] * 2,
        scratch_shapes=[
            pltpu.VMEM((D, count), bf16),
            pltpu.VMEM((count, D), bf16),
            pltpu.VMEM((D, D), bf16),
            pltpu.VMEM((D, FF), bf16),
            pltpu.SemaphoreType.DMA((2,)),
            pltpu.SemaphoreType.DMA,
        ],
        compiler_params=pltpu.CompilerParams(vmem_limit_bytes=ALL_VMEM),
        cost_estimate=pl.CostEstimate(flops=4_000_000_000, bytes_accessed=MIB, transcendentals=0),
        name="inner_grads",
    )(hid_t, inner_back, place, att_t, branch)


def attend_back_pair(queries, keys, values, upstream, prob_ref, dq_ref, dk_ref, dv_ref):
    lows, backs = [], []
    masks = lane_masks()
    for i, mask in enumerate(masks):
        low = prob_ref[i]
        weight = low.astype(f32)
        weight_back = dot_t(values * mask, upstream)
        mean = jnp.sum(weight * weight_back, axis=0, keepdims=True)
        lows.append(low)
        backs.append((weight * (weight_back - mean)).astype(bf16))
    each = lambda v: jnp.concatenate([v * mask for mask in masks], axis=0)
    dv_ref[...] = dot(jnp.concatenate(lows, axis=1), each(upstream)).astype(bf16)
    dk_ref[...] = (dot(jnp.concatenate(backs, axis=1), each(queries)) * 0.125).astype(bf16)
    dq_ref[...] = (dot_l(jnp.concatenate(backs, axis=0), each(keys)) * 0.125).astype(bf16)


def attend_back_kernel(q_ref, k_ref, v_ref, up_ref, prob_ref, *refs):
    attend_back_pair(q_ref[...], k_ref[...], v_ref[...], up_ref[...], prob_ref, *refs[-3:])


def pair_specs(rows, first, last):
    pairs = H // 2
    pair = lambda s: jnp.minimum(first + s, last)
    lane = lambda kind: pl.BlockSpec((rows, 128), lambda s: (pair(s) // pairs, kind * pairs + pair(s) % pairs))
    return [lane(0), lane(1), lane(2), lane(0), pl.BlockSpec((2, rows, rows), lambda s: (pair(s), 0, 0))]


def attend_back(first, count, qkv, back, prob, grads=(), deps=()):
    specs = pair_specs(prob.shape[1], first, first + count - 1)
    return call(
        attend_back_kernel,
        (qkv, qkv, qkv, back, prob, *grads),
        deps,
        grid=(count,),
        in_specs=specs + [ANY] * len(grads),
        out_specs=[specs[0]] * 3,
        out_shape=[jax.ShapeDtypeStruct(back.shape, bf16)] * 3,
        input_output_aliases={5 + i: i for i in range(len(grads))},
        compiler_params=pltpu.CompilerParams(vmem_limit_bytes=ALL_VMEM),
        cost_estimate=pl.CostEstimate(flops=3_000_000_000, bytes_accessed=MIB, transcendentals=0),
        name=f"attend_back_{first}",
    )


def proj_grads_kernel(place, turned, small_ref, db1_ref, dq, dk, dv, keep, send, grads, packed, bias, sem, wsem):
    step = pl.program_id(0)
    copies = [pltpu.make_async_copy(v, grads.at[i], sem.at[i]) for i, v in enumerate((dq, dk, dv))]

    @pl.when(step == 0)
    def _():
        start_all([copies[1], copies[2], copies[0]])

    for turn, which in enumerate((1, 2, 0)):

        @pl.when(step == turn)
        def _():
            copies[which].wait()
            g = dot(turned[...], grads[which]).astype(bf16)
            if which == 1:
                packed[:, D:QKV_HALF] = g[:, : D // 2]
                packed[:, QKV_BLOCK : QKV_BLOCK + D // 2] = g[:, D // 2 :]
            else:
                at = 0 if which == 0 else QKV_BLOCK + D // 2
                packed[:, at : at + D] = g
                bias[which // 2] = fold_rows(grads[which].astype(f32))

    @pl.when(step == 0)
    def _():
        owner = lax.broadcasted_iota(jnp.int32, (SLABS, FF), 1) // (4 * SLAB)
        one = lax.broadcasted_iota(jnp.int32, (SLABS, FF), 0)
        mine = jnp.where(owner == one, jnp.sum(db1_ref[...], axis=0, keepdims=True), 0.0)
        place_of = lax.broadcasted_iota(jnp.int32, (FF, 128), 0) % (4 * SLAB)
        pick = (place_of == lax.broadcasted_iota(jnp.int32, (FF, 128), 1)).astype(f32)
        table = lax.dot_general(
            mine, pick, (((1,), (0,)), ((), ())), precision=lax.Precision.HIGHEST, preferred_element_type=f32
        )
        spread = jnp.broadcast_to(table[:, None, :], (SLABS, SLAB, 128)).reshape(D, 128)
        packed[:, QKV_BLOCK + QKV_HALF :] = spread.astype(bf16)

    def give(half):
        for chip in range(CHIPS):
            block = packed.at[pl.ds(chip * PAIR_ROWS, PAIR_ROWS), pl.ds(half * QKV_BLOCK, QKV_BLOCK)]
            hand_over(place, chip, half, keep, send, [(block, pl.ds(0, QKV_BLOCK))], wsem)

    @pl.when(step == 1)
    def _():
        give(1)

    @pl.when(step == 2)
    def _():
        rows_of = [bias[...], small_ref[...], jnp.zeros((120, 8, D), f32)]
        packed[:, QKV_HALF:QKV_BLOCK] = jnp.sum(jnp.concatenate(rows_of, axis=0), axis=1).T.astype(bf16)
        give(0)
        wait_whole(keep, wsem)
        wait_whole(send, wsem)


def proj_grads(place, turned, small, inner_bias_grad, grads, deps=()):
    count = turned.shape[1]
    return call(
        proj_grads_kernel,
        (place, turned, small, inner_bias_grad, *grads),
        deps,
        grid=(3,),
        in_specs=[SMEM, whole(D, count), whole(6, 8, D), whole(8, FF), ANY, ANY, ANY],
        out_specs=[ANY, ANY],
        out_shape=[jax.ShapeDtypeStruct((CHIPS, PAIR_ROWS, QKV_BLOCK), bf16)] * 2,
        scratch_shapes=[
            pltpu.VMEM((3, count, D), bf16),
            pltpu.VMEM((D, 2 * QKV_BLOCK), bf16),
            pltpu.VMEM((2, 8, D), f32),
            pltpu.SemaphoreType.DMA((3,)),
            pltpu.SemaphoreType.DMA,
        ],
        compiler_params=pltpu.CompilerParams(vmem_limit_bytes=ALL_VMEM),
        cost_estimate=pl.CostEstimate(flops=4_000_000_000, bytes_accessed=MIB, transcendentals=0),
        name="proj_grads",
    )


def input_back_kernel(fb_ref, dq_ref, dk_ref, dv_ref, w_ref, *refs):
    half = D // 2
    total = fb_ref[...] + dot_t(dq_ref[...], w_ref[:, 0:D])
    total = total + dot_t(dk_ref[:, :half], w_ref[:, D:QKV_HALF])
    total = total + dot_t(dk_ref[:, half:], w_ref[:, PROJ_BLOCK : PROJ_BLOCK + half])
    out_ref, small_ref = refs[-2:]
    small_ref[...] = total[0:8, 0:128]
    out_ref[...] = total + dot_t(dv_ref[...], w_ref[:, PROJ_BLOCK + half : PROJ_BLOCK + QKV_HALF])


def input_back(first, blocks, first_back, grads, weights, given=(), deps=()):
    token = pl.BlockSpec((BLOCK, D), lambda s: (first + s, 0))
    return call(
        input_back_kernel,
        (first_back, *grads, weights, *given),
        deps,
        grid=(blocks,),
        in_specs=[token] * 4 + [whole(D, 2 * PROJ_BLOCK)] + [ANY] * len(given),
        out_specs=[token, whole(8, 128)],
        out_shape=[jax.ShapeDtypeStruct(first_back.shape, f32), jax.ShapeDtypeStruct((8, 128), f32)],
        input_output_aliases={5: 0} if given else {},
        compiler_params=pltpu.CompilerParams(vmem_limit_bytes=ALL_VMEM),
        cost_estimate=pl.CostEstimate(flops=10_000_000_000, bytes_accessed=MIB, transcendentals=0),
        name=f"input_back_{first}",
    )


def add_up_kernel(jobs, passed, place, *refs):
    refs[len(refs) - 1][...] = refs[0][0, 0:8, 0:128].astype(f32)
    first, out = 0, sum(count for count, _ in jobs) + passed
    for count, kind in jobs:
        terms = refs[first : first + count]
        first += count

        def total(slot):
            return sum((ref[slot].astype(f32) for ref in terms[1:]), terms[0][slot].astype(f32))

        slots = terms[0].shape[0]
        if kind == "upper":

            def one(i, _, total=total, ready=refs[out]):
                ready[i] = total(i).astype(bf16)
                return 0

            lax.fori_loop(0, slots, one, 0)
            out += 1
        elif kind == "both":
            half = slots // 2

            def one(i, _, total=total, ready=refs[out], rest=refs[out + 1], half=half):
                rest[i] = total(i)
                ready[i] = total(half + i).astype(bf16)
                return 0

            lax.fori_loop(0, half, one, 0)
            out += 2
        elif kind == "down":
            whole_sum = total(0)
            refs[out][0:PAIR_ROWS, :] = whole_sum[:, :D]
            refs[out][PAIR_ROWS:, :] = whole_sum[:, D:]
            out += 1
        else:
            whole_sum = total(0)
            low_core = place[1] == 0
            low, high = whole_sum[:SLAB], whole_sum[SLAB:]
            refs[out][...] = jnp.where(low_core, low, high)
            refs[out + 1][...] = jnp.where(low_core, high, low)
            out += 2


def add_up(place, *groups, passed=(), deps=(), vmem=ALL_VMEM):
    operands, specs, out_specs, shapes, jobs = [], [], [], [], []
    steps = 3 if any(size == CHIPS for size, _ in groups) else 1
    one_step = all(size > 1 for size, _ in groups)
    steps = steps if one_step else 1
    for size, terms in groups:
        _, rows, lanes = terms[0].shape
        half, block = size // 2, rows // steps
        kind = "upper" if size == CHIPS else "both" if size > 1 else "down" if lanes == DOWN_BLOCK else "halves"
        operands += terms
        take = (half, 1) if kind == "upper" else (size, 0)
        specs += [pl.BlockSpec((take[0], block, lanes), lambda s, at=take[1]: (at, s, 0))] * len(terms)
        if size > 1:
            kinds = [bf16] if kind == "upper" else [bf16, f32]
            out_specs += [pl.BlockSpec((half, block, lanes), lambda s: (0, s, 0))] * len(kinds)
            shapes += [jax.ShapeDtypeStruct((half, rows, lanes), dtype) for dtype in kinds]
        else:
            ends = [(2 * PAIR_ROWS, D)] if kind == "down" else [(SLAB, lanes)] * 2
            out_specs += [whole(*end) for end in ends]
            shapes += [jax.ShapeDtypeStruct(end, f32) for end in ends]
        jobs.append((len(terms), kind))
    return call(
        lambda *refs: add_up_kernel(jobs, len(passed), refs[0], *refs[1:]),
        [place] + operands + list(passed),
        deps,
        grid=(steps,),
        in_specs=[SMEM] + specs + [ANY] * len(passed),
        out_specs=out_specs + [ANY] * len(passed) + [whole(8, 128)],
        out_shape=shapes
        + [jax.ShapeDtypeStruct(v.shape, v.dtype) for v in passed]
        + [jax.ShapeDtypeStruct((8, 128), f32)],
        input_output_aliases={1 + len(operands) + i: len(shapes) + i for i in range(len(passed))},
        compiler_params=pltpu.CompilerParams(vmem_limit_bytes=vmem),
        cost_estimate=pl.CostEstimate(flops=1000, bytes_accessed=1000, transcendentals=0),
        name="add_up",
    )


def finish_inner_kernel(place, mine, other, out_g, inner_g, small):
    low_core = place[1] == 0
    low = jnp.where(low_core, mine[...], other[...])
    high = jnp.where(low_core, other[...], mine[...])
    out_g[:, :OUT_HALF], out_g[:, OUT_HALF:] = low[:, :OUT_HALF], high[:, :OUT_HALF]
    inner_g[:, :INNER_HALF], inner_g[:, INNER_HALF:] = low[:, OUT_HALF:], high[:, OUT_HALF:]
    small[...] = low[0:8, 0:128]


def finish_proj_kernel(place, mine, other, dq, dk, dv, bias, *vectors):
    low_core = place[1] == 0
    low = jnp.where(low_core, mine[...], other[...])
    high = jnp.where(low_core, other[...], mine[...])
    half = D // 2
    dq[...] = low[:, :D]
    dk[:, :half], dk[:, half:] = low[:, D:QKV_HALF], high[:, :half]
    dv[...] = high[:, half:QKV_HALF]
    bias[...] = high[0, QKV_HALF : QKV_HALF + 4 * SLAB]
    rows = low[:, QKV_HALF:].T
    for i, out in enumerate(vectors):
        out[...] = rows[i, 0:SLAB]


def finish(kernel, place, mine, other, shapes, name, deps=()):
    at = lambda shape: pl.BlockSpec(shape, lambda s: (0,) * len(shape))
    return call(
        kernel,
        (place, mine, other),
        deps,
        grid=(1,),
        in_specs=[SMEM, at(mine.shape), at(mine.shape)],
        out_specs=[at(shape) for shape in shapes],
        out_shape=[jax.ShapeDtypeStruct(shape, f32) for shape in shapes],
        compiler_params=pltpu.CompilerParams(vmem_limit_bytes=LITTLE),
        cost_estimate=pl.CostEstimate(flops=1000, bytes_accessed=1000, transcendentals=0),
        name=name,
    )


def finish_inner(place, mine, other):
    return finish(finish_inner_kernel, place, mine, other, [(SLAB, D), (SLAB, FF), (8, 128)], "finish_inner")


def finish_proj(place, mine, other, deps=()):
    shapes = [(SLAB, D)] * 3 + [(4 * SLAB,)] + [(SLAB,)] * 8
    return finish(finish_proj_kernel, place, mine, other, shapes, "finish_proj", deps)


AXES = ("dp", "fsdp")


CORE = (1, 1)
ALONG_Z_FIRST, ALONG_Z_THEN, ALONG_Z_BOTH, ALONG_XY_FIRST, ALONG_XY_THEN = (16, 8), (8, 16), (24, 24), (2, 4), (4, 2)
FAST_SHAPE = {"dp": 4, "fsdp": 8}


def move(v, masks):
    return lax.ppermute(v, AXES, [(i, i ^ masks[i & 1]) for i in range(SLABS)])


SUM_STEPS = (ALONG_XY_THEN, ALONG_XY_FIRST, ALONG_Z_THEN, ALONG_Z_FIRST)


def after(*values):
    return lax.optimization_barrier(values)


class Sums:
    def __init__(self, keep, got):
        self.size, self.terms, self.step = CHIPS, [keep, got], 0

    def job(self):
        return self.size, self.terms

    def send(self, outs):
        ready = outs.pop(0)
        if self.size < CHIPS:
            self.terms = [outs.pop(0)]
        self.size //= 2
        self.terms = self.terms + [move(ready, SUM_STEPS[self.step])]
        self.step += 1


def add_and_send(place, *groups, **options):
    outs = list(add_up(place, *[g.job() for g in groups], **options))
    for g in groups:
        if g.size > 1:
            g.send(outs)
    return outs


def fast_blocks(shards, core):
    (qw, kw, vw, ow, qb, vb, ob, fg, fs, iw, ib, dw, db, sg, ss) = shards
    vectors = jnp.pad(jnp.stack([qb, vb, ob, fg, fs, db, sg, ss], axis=1), ((0, 0), (0, 120)))
    inner_bias = jnp.pad(ib.reshape(1, 4 * SLAB), ((0, SLAB - 1), (0, 128 - 4 * SLAB)))
    half = D // 2
    halves = [
        jnp.concatenate([qw, kw[:, :half], vectors, ow[:, :half], iw[:, :INNER_HALF]], axis=1),
        jnp.concatenate([kw[:, half:], vw, inner_bias, ow[:, half:], iw[:, INNER_HALF:]], axis=1),
    ]
    low_core = core == 0
    own = jnp.where(low_core, halves[0], halves[1])
    other = move(jnp.where(low_core, halves[1], halves[0]), CORE)
    rows = jnp.concatenate([jnp.where(low_core, own, other), jnp.where(low_core, other, own)], axis=0)
    return rows[:, :PROJ_BLOCK], rows[:, PROJ_BLOCK:], jnp.concatenate([dw[:PAIR_ROWS], dw[PAIR_ROWS:]], axis=1)


def gather_plain(shards):
    (qw, kw, vw, ow, qb, vb, ob, fg, fs, iw, ib, dw, db, sg, ss) = [
        lax.all_gather(v, AXES, axis=0, tiled=True) for v in shards
    ]
    vectors = jnp.pad(jnp.stack([qb, vb, ob, fg, fs, db, sg, ss], axis=1), ((0, 0), (0, 120)))
    inner_bias = jnp.pad(ib.reshape(SLABS, 1, 4 * SLAB), ((0, 0), (0, SLAB - 1), (0, 128 - 4 * SLAB))).reshape(D, 128)
    half = D // 2
    chips = lambda v: v.reshape(CHIPS, PAIR_ROWS, -1)
    down = dw.reshape(CHIPS, 2, 2, PAIR_ROWS, D)
    first = [
        chips(jnp.concatenate([qw, kw[:, :half], vectors, ow[:, :half]], axis=1)),
        chips(jnp.concatenate([kw[:, half:], vw, inner_bias, ow[:, half:]], axis=1)),
    ]
    second = [
        jnp.concatenate([chips(iw[:, c * INNER_HALF : (c + 1) * INNER_HALF]), down[:, c, 0], down[:, c, 1]], axis=2)
        for c in range(2)
    ]
    slots = lambda halves: [v[np.array(SLOT_CHIPS[c])] for c, v in enumerate(halves)]
    return slots(first), slots(second)


def local(fast, inputs, lengths, *rest):
    shards, cotangent = rest[:15], rest[15]
    both = lambda v, came: jnp.concatenate([v, came])
    if fast:
        linear = lax.axis_index(AXES)
        core = linear & 1
        place = jnp.stack([linear >> 1, core]).astype(jnp.int32)
        first, inner, down = fast_blocks(shards, core)
        first = first[None]
        first = both(first, move(first, ALONG_Z_FIRST))
        first, second = after(first, jnp.concatenate([inner, down], axis=1)[None])
        second = jnp.concatenate([second] + [move(second, steps) for steps in (ALONG_Z_FIRST, ALONG_Z_THEN, ALONG_Z_BOTH)])
        first = both(first, move(first, ALONG_Z_THEN))
        first_then, first_core = move(first, ALONG_XY_THEN), move(first, CORE)
        first_came = move(first, ALONG_XY_FIRST)
        first_last, came_core = move(first_came, ALONG_XY_THEN), move(first_came, CORE)
        first_then, first_last, second = after(first_then, first_last, second)
        first = [first, first_came, first_then, first_last]
        first += [first_core, came_core, move(first_then, CORE), move(first_last, CORE)]
        second_came, second_then, second_core = move(second, ALONG_XY_FIRST), move(second, ALONG_XY_THEN), move(second, CORE)
        meta = tuple((at, other) for other in (False, True) for at in range(0, CHIPS, 4))
    else:
        place = jnp.zeros((2,), jnp.int32)
        first, second = gather_plain(shards)
        meta = ((0, False), (0, True))
    qkv, attended, stats, weights, vectors = attend(place, lengths, inputs, first, meta)
    prob = probs(0, lengths, qkv, stats)
    if fast:
        second_came, prob = after(second_came, prob)
        second_last, came_core = move(second_came, ALONG_XY_THEN), move(second_came, CORE)
    prob, normed, rstd, hid, inputs_t, attended_t, hid_t = window(
        1, lengths, inputs, qkv, attended, stats, weights, vectors, prob
    )
    bias_at = PROJ_BLOCK + QKV_HALF
    inner_bias = weights[::SLAB, bias_at : bias_at + 4 * SLAB].reshape(1, FF).astype(f32)
    if fast:
        second_then, second_last, normed, inner_bias = after(second_then, second_last, normed, inner_bias)
        second = [second, second_came, second_then, second_last]
        second += [second_core, came_core, move(second_then, CORE), move(second_last, CORE)]
    output, first_back, back, inner_back, branch, small, db1, down_keep, down_send = feed_forward(
        place, normed, rstd, hid, cotangent, vectors, inner_bias, weights, second, meta
    )
    inner_keep, inner_send = inner_grads(place, hid_t, inner_back, attended_t, branch)
    pairs = lengths.shape[0] * (H // 2)
    third = pairs // 3
    deps = []
    if fast:
        down = Sums(down_keep, move(down_send, CORE))
        inner_send, *deps = add_and_send(place, down, passed=[inner_send], deps=[inner_keep])
        inner = Sums(inner_keep, move(inner_send, CORE))
    grads = attend_back(0, third, qkv, back, prob, deps=deps)
    if fast:
        deps = add_and_send(place, inner, deps=grads[:1])
    grads = attend_back(third, third, qkv, back, prob, grads, deps=deps)
    if fast:
        deps = add_and_send(place, down, deps=grads[:1])
    grads = attend_back(2 * third, pairs - 2 * third, qkv, back, prob, grads, deps=deps)
    if fast:
        deps = add_and_send(place, inner, down, deps=grads[:1])
    proj_keep, proj_send = proj_grads(place, inputs_t, small, db1, grads, deps=deps)
    blocks = inputs.shape[0] // BLOCK
    early = 1
    if fast:
        proj_send, *deps = add_and_send(place, inner, down, passed=[proj_send], deps=[proj_keep])
        proj = Sums(proj_keep, move(proj_send, CORE))
        grad_input, *deps = input_back(0, early, first_back, grads, weights, deps=deps)
        down_grad, *deps = add_and_send(place, proj, down, deps=deps)
        grad_input, *deps = input_back(early, blocks - early, first_back, grads, weights, [grad_input], deps=deps)
        deps = add_and_send(place, proj, inner, deps=deps, vmem=LITTLE)
        mine, other, *deps = add_and_send(place, proj, inner, deps=deps, vmem=LITTLE)
        out_grad, inner_grad, *deps = finish_inner(place, mine, move(other, CORE))
        add_and_send(place, proj, deps=deps, vmem=LITTLE)
        mine, other, _ = add_and_send(place, proj, vmem=LITTLE)
        *square, bias, v0, v1, v2, v3, v4, v5, v6, v7 = finish_proj(place, mine, move(other, CORE))
        vectors = [v0, v1, v2, v3, v4, v5, v6, v7]
    else:
        grad_input, _ = input_back(0, blocks, first_back, grads, weights)
        shard = lambda *v: lax.psum_scatter(jnp.concatenate(v, axis=1), AXES, scatter_dimension=0, tiled=True)
        by_chip = lambda pair: [v[np.argsort(np.array(SLOT_CHIPS[c]))].astype(f32) for c, v in enumerate(pair)]
        low, high = (v.reshape(D, -1) for v in by_chip((inner_keep, inner_send)))
        out_grad, inner_grad = shard(low[:, :OUT_HALF], high[:, :OUT_HALF]), shard(low[:, OUT_HALF:], high[:, OUT_HALF:])
        parts = [jnp.stack([v[:, :, :D], v[:, :, D:]], axis=1) for v in by_chip((down_keep, down_send))]
        down_grad = shard(jnp.stack(parts, axis=1).reshape(FF, D))
        low, high = (v.reshape(D, -1) for v in by_chip((proj_keep, proj_send)))
        half = D // 2
        square = shard(low[:, :D]), shard(low[:, D:QKV_HALF], high[:, :half]), shard(high[:, half:QKV_HALF])
        columns = shard(low[:, QKV_HALF:])
        vectors = [columns[:, i] for i in range(8)]
        bias = shard(high[::SLAB, QKV_HALF : QKV_HALF + 4 * SLAB].reshape(FF, 1))[:, 0]
    return (
        output,
        grad_input,
        *square,
        out_grad,
        *vectors[:5],
        inner_grad,
        bias,
        down_grad,
        *vectors[5:],
    )


def solution(mesh):
    rows, flat = P(AXES, None), P(AXES)
    params = (rows,) * 4 + (flat,) * 5 + (rows, flat, rows, flat, flat, flat)
    return jax.shard_map(
        functools.partial(local, dict(mesh.shape) == FAST_SHAPE),
        mesh=mesh,
        in_specs=(rows, flat) + params + (rows,),
        out_specs=(rows, rows) + params,
        check_vma=False,
    )
```

```python
import functools
import math

import jax
import jax.numpy as jnp
import numpy as np
from jax import lax
from jax.experimental import pallas as pl
from jax.experimental.pallas import tpu as pltpu
from jax.sharding import PartitionSpec as P

D = 768
H = 12
DH = 64
FF = 3072
SLABS = 32
SLAB = D // SLABS
CHIPS = SLABS // 2
PAIR_ROWS = 2 * SLAB
NORM_EPSILON = 1e-12
MASKED_SCORE = -1000000000.0
GAUSS_DENSITY = 0.3989422804014327
LOG2E = 1.4426950408889634
MIB = 1 << 20
VMEM = 62 * MIB
ALL_VMEM = 127 * MIB // 2
LITTLE = 16 * MIB

QKV_HALF = 3 * D // 2
QKV_BLOCK = QKV_HALF + 128
OUT_HALF = D // 2
PROJ_BLOCK = QKV_BLOCK + OUT_HALF
INNER_HALF = FF // 2
INNER_BLOCK = OUT_HALF + INNER_HALF
DOWN_BLOCK = 2 * D

SLOT_BITS = ((8, 4, 1, 2), (4, 8, 2, 1))
SLOT_CHIPS = tuple(
    tuple(sum(bit for i, bit in enumerate(bits) if slot >> i & 1) for slot in range(CHIPS)) for bits in SLOT_BITS
)

bf16 = jnp.bfloat16
f32 = jnp.float32
ANY = pl.BlockSpec(memory_space=pl.ANY)
SMEM = pl.BlockSpec(memory_space=pltpu.SMEM)


def dot(a, b):
    return lax.dot_general(a, b, (((1,), (0,)), ((), ())), preferred_element_type=f32)


def dot_t(a, b):
    return lax.dot_general(a, b, (((1,), (1,)), ((), ())), preferred_element_type=f32)


def dot_l(a, b):
    return lax.dot_general(a, b, (((0,), (0,)), ((), ())), preferred_element_type=f32)


def call(kernel, operands, deps, in_specs, **options):
    count = len(operands)

    def body(*refs):
        kernel(*refs[:count], *refs[count + len(deps) :])

    in_specs = in_specs + [whole(8, 128) if v.shape == (8, 128) else ANY for v in deps]
    return pl.pallas_call(body, in_specs=in_specs, **options)(*operands, *deps)


def aligned(start, size, unit):
    return pl.ds(pl.multiple_of(start, unit), size)


def chip_of(slot, half):
    return jnp.where(half == 0, SLOT_CHIPS[0][slot], SLOT_CHIPS[1][slot])


def slot_of(chip, half):
    bits = SLOT_BITS[half]
    return sum(jnp.where((chip & bit) != 0, 1 << i, 0) for i, bit in enumerate(bits))


def blocks_of(place, pieces):
    for ref, (first, other) in pieces:
        half = 1 - place[1] if other else place[1]
        for i in range(ref.shape[0]):
            yield ref, i, place[0] ^ chip_of(first + i, half), half


def proj_blocks(place, pieces, weights, sem):
    for ref, i, chip, half in blocks_of(place, pieces):
        rows = aligned(chip * PAIR_ROWS, PAIR_ROWS, 16)
        yield pltpu.make_async_copy(ref.at[i], weights.at[rows, aligned(half * PROJ_BLOCK, PROJ_BLOCK, 128)], sem)


def inner_blocks(place, pieces, inner_w, sem):
    for ref, i, chip, half in blocks_of(place, pieces):
        rows = aligned(chip * PAIR_ROWS, PAIR_ROWS, 16)
        yield pltpu.make_async_copy(
            ref.at[i, :, pl.ds(0, INNER_HALF)],
            inner_w.at[rows, aligned(half * INNER_HALF, INNER_HALF, 128)],
            sem,
        )


def down_blocks(place, pieces, down_w, sem):
    for ref, i, chip, half in blocks_of(place, pieces):
        for k in range(2):
            at = (chip * 2 + half) * (2 * PAIR_ROWS) + k * PAIR_ROWS
            yield pltpu.make_async_copy(
                ref.at[i, :, pl.ds(INNER_HALF + k * D, D)], down_w.at[aligned(at, PAIR_ROWS, 16), :], sem
            )


def start_all(copies):
    for c in copies:
        c.start()


def whole(*shape):
    return pl.BlockSpec(shape, lambda *s: (0,) * len(shape))


def fold_rows(v):
    return jnp.sum(v.reshape(v.shape[0] // 8, 8, v.shape[1]), axis=0)


def hand_over(place, chip, half, keep, send, pairs, sem):
    slot = slot_of(chip ^ place[0], half)
    for mine, out in ((True, keep), (False, send)):

        @pl.when((place[1] == half) == mine)
        def _():
            for source, lanes in pairs:
                pltpu.make_async_copy(source, out.at[slot, :, lanes], sem).start()


def wait_whole(ref, sem):
    pltpu.make_async_copy(ref, ref, sem).wait()


def lane_masks():
    low = (lax.broadcasted_iota(jnp.int32, (1, 128), 1) < DH).astype(f32)
    return low.astype(bf16), (1.0 - low).astype(bf16)


def attend_kernel(meta, n_pieces, place, lengths, x_ref, *refs):
    piece_refs = refs[:n_pieces]
    qkv_ref, att_ref, stat_ref, weights, vectors = refs[n_pieces : n_pieces + 5]
    sem = refs[-1]
    seq = pl.program_id(0)
    rows = x_ref.shape[0]

    @pl.when(seq == 0)
    def _():
        start_all(proj_blocks(place, zip(piece_refs, meta), weights, sem))
        wait_whole(weights, sem)
        small = weights[:, QKV_HALF:QKV_BLOCK].astype(f32)
        vectors[...] = small.T[0:16, :]

    lowered = x_ref[...].astype(bf16)
    first = dot(lowered, weights[:, 0:QKV_HALF])
    qkv_ref[:, 0:D] = (first[:, 0:D] + vectors[0:1, :]).astype(bf16)
    qkv_ref[:, D:QKV_HALF] = first[:, D:QKV_HALF].astype(bf16)
    second = dot(lowered, weights[:, PROJ_BLOCK : PROJ_BLOCK + QKV_HALF])
    qkv_ref[:, QKV_HALF : 2 * D] = second[:, 0 : D // 2].astype(bf16)
    qkv_ref[:, 2 * D :] = (second[:, D // 2 :] + vectors[1:2, :]).astype(bf16)

    low, high = lane_masks()
    lane = lax.broadcasted_iota(jnp.int32, (1, 128), 1)
    key_at = lax.broadcasted_iota(jnp.int32, (1, rows), 1)
    hidden_keys = jnp.where(key_at < lengths[seq], 0.0, MASKED_SCORE).astype(f32)
    chunk = 256
    ones = jnp.ones((rows, 128), bf16)
    stats = [jnp.zeros((chunk, 128), f32) for _ in range(rows // chunk)]
    for pair in range(H // 2):
        at = pair * 128
        keys = qkv_ref[:, D + at : D + at + 128]
        values = jnp.concatenate([qkv_ref[:, 2 * D + at : 2 * D + at + 128], ones], axis=1)
        keys_of = (keys * low, keys * high)
        for c in range(rows // chunk):
            span = pl.ds(c * chunk, chunk)
            queries = qkv_ref[span, at : at + 128]
            outs = []
            for i in range(2):
                scores = dot_t(queries, keys_of[i]) * (0.125 * LOG2E) + hidden_keys
                peak = jnp.max(scores, axis=-1, keepdims=True)
                weight = jnp.exp2(scores - peak).astype(bf16)
                both = dot(weight, values)
                total = both[:, 128:]
                outs.append(both[:, :128] / total)
                log_total = peak + jnp.log2(total)
                stats[c] = jnp.where(lane == 2 * pair + i, log_total, stats[c])
            att_ref[span, at : at + 128] = jnp.where(lane < DH, outs[0], outs[1]).astype(bf16)
    for c in range(rows // chunk):
        stat_ref[0, :, c * chunk : (c + 1) * chunk] = stats[c].T[0:16, :]


def attend(place, lengths, x, pieces, meta):
    rows = x.shape[0] // lengths.shape[0]
    seqs = lengths.shape[0]
    return pl.pallas_call(
        functools.partial(attend_kernel, meta, len(pieces)),
        grid=(seqs,),
        in_specs=[SMEM, SMEM, pl.BlockSpec((rows, D), lambda s: (s, 0))] + [ANY] * len(pieces),
        out_specs=[
            pl.BlockSpec((rows, 3 * D), lambda s: (s, 0)),
            pl.BlockSpec((rows, D), lambda s: (s, 0)),
            pl.BlockSpec((1, 16, rows), lambda s: (s, 0, 0)),
            whole(D, 2 * PROJ_BLOCK),
            whole(16, D),
        ],
        out_shape=[
            jax.ShapeDtypeStruct((seqs * rows, 3 * D), bf16),
            jax.ShapeDtypeStruct((seqs * rows, D), bf16),
            jax.ShapeDtypeStruct((seqs, 16, rows), f32),
            jax.ShapeDtypeStruct((D, 2 * PROJ_BLOCK), bf16),
            jax.ShapeDtypeStruct((16, D), f32),
        ],
        scratch_shapes=[pltpu.SemaphoreType.DMA],
        compiler_params=pltpu.CompilerParams(vmem_limit_bytes=VMEM),
        cost_estimate=pl.CostEstimate(flops=18_000_000_000, bytes_accessed=20 * MIB, transcendentals=0),
        name="attend",
    )(place, lengths, x, *pieces)


def gelu_parts(u):
    size = jnp.abs(u)
    bell = jnp.exp2(u * u * (-0.5 * LOG2E))
    t = 1.0 / (1.0 + (0.3275911 * math.sqrt(0.5)) * size)
    poly = t * (0.127414796 + t * (-0.142248368 + t * (0.7107068705 + t * (-0.7265760135 + t * 0.5307027145))))
    tail = poly * bell
    below = jnp.where(u < 0.0, tail, 1.0 - tail)
    return below, bell


def mean_rows(v):
    return jnp.sum(v, axis=-1, keepdims=True) * (1.0 / D)


def norm_rows(total):
    center = total - mean_rows(total)
    rstd = lax.rsqrt(mean_rows(center * center) + NORM_EPSILON)
    return center * rstd, rstd


def norm_back(upstream, normed, rstd, gain):
    scaled = upstream * gain
    return rstd * (scaled - mean_rows(scaled) - normed * mean_rows(scaled * normed))


BLOCK = 256
WIDTH = 768
DOWN_STEPS = 8


def out_weight_copies(proj_w, out_w, sem):
    for half in range(2):
        lanes = pl.ds(half * PROJ_BLOCK + QKV_BLOCK, OUT_HALF)
        yield pltpu.make_async_copy(proj_w.at[:, lanes], out_w.at[:, pl.ds(half * OUT_HALF, OUT_HALF)], sem)


def probs_kernel(seq, lengths, q_ref, k_ref, stat_ref, *refs):
    prob_ref = refs[-1]
    pair = pl.program_id(0)
    rows = q_ref.shape[0]
    chunk = 256
    key_at = lax.broadcasted_iota(jnp.int32, (rows, 1), 0)
    hidden_keys = jnp.where(key_at < lengths[seq], 0.0, MASKED_SCORE).astype(f32)
    for i, mask in enumerate(lane_masks()):
        own_keys = k_ref[...] * mask
        for c in range(rows // chunk):
            span = slice(c * chunk, (c + 1) * chunk)
            log_total = stat_ref[0, pl.ds(2 * pair + i, 1), span]
            scores = dot_t(own_keys, q_ref[span, :]) * (0.125 * LOG2E) + hidden_keys
            prob_ref[i, :, span] = jnp.exp2(scores - log_total).astype(bf16)


def probs_specs(seq, rows):
    pairs = H // 2
    lane = lambda kind: pl.BlockSpec((rows, 128), lambda s: (seq, kind * pairs + s))
    specs = [SMEM, lane(0), lane(1), pl.BlockSpec((1, 16, rows), lambda s: (seq, 0, 0))]
    return specs, pl.BlockSpec((2, rows, rows), lambda s: (seq * pairs + s, 0, 0))


def probs(seq, lengths, qkv, stats, deps=()):
    seqs, _, rows = stats.shape
    specs, out = probs_specs(seq, rows)
    return call(
        functools.partial(probs_kernel, seq),
        (lengths, qkv, qkv, stats),
        deps,
        grid=(H // 2,),
        in_specs=specs,
        out_specs=out,
        out_shape=jax.ShapeDtypeStruct((seqs * H, rows, rows), bf16),
        compiler_params=pltpu.CompilerParams(vmem_limit_bytes=VMEM),
        cost_estimate=pl.CostEstimate(flops=8_000_000_000, bytes_accessed=MIB, transcendentals=0),
        name="probs",
    )


def window_kernel(seq, blocks, lengths, q_ref, k_ref, stat_ref, _, x_ref, att_ref, vec_ref, proj_w, *refs):
    prob_ref, normed_ref, rstd_ref, hid_ref, x_t, att_t, hid_t, out_w, sem = refs
    g = pl.program_id(0)

    @pl.when(g == 0)
    def _():
        start_all(out_weight_copies(proj_w, out_w, sem))

    probs_kernel(seq, lengths, q_ref, k_ref, stat_ref, prob_ref)

    @pl.when(g == 0)
    def _():
        wait_whole(out_w, sem)

    @pl.when(g < blocks)
    def _():
        x, attended = x_ref[...], att_ref[...]
        normed, rstd = norm_rows(x + dot(attended, out_w[...]) + vec_ref[2:3, :])
        normed_ref[...] = normed
        rstd_ref[...] = jnp.broadcast_to(rstd, rstd_ref.shape)
        hidden = normed * vec_ref[3:4, :] + vec_ref[4:5, :]
        hid_ref[...] = hidden.astype(bf16)
        x_t[...] = x.T.astype(bf16)
        att_t[...] = attended.astype(f32).T.astype(bf16)
        hid_t[...] = hidden.T.astype(bf16)


def window(seq, lengths, x, qkv, attended, stats, weights, vectors, prob, deps=()):
    count = x.shape[0]
    _, _, rows = stats.shape
    blocks = count // BLOCK
    block = lambda s: jnp.minimum(s, blocks - 1)
    token = lambda width: pl.BlockSpec((BLOCK, width), lambda s: (block(s), 0))
    turned = pl.BlockSpec((D, BLOCK), lambda s: (0, block(s)))
    specs, out = probs_specs(seq, rows)
    return call(
        functools.partial(window_kernel, seq, blocks),
        (lengths, qkv, qkv, stats, prob, x, attended, vectors, weights),
        deps,
        grid=(H // 2,),
        in_specs=specs + [ANY, token(D), token(D), whole(16, D), ANY],
        out_specs=[out, token(D), token(128), token(D)] + [turned] * 3,
        out_shape=[
            jax.ShapeDtypeStruct(prob.shape, bf16),
            jax.ShapeDtypeStruct((count, D), f32),
            jax.ShapeDtypeStruct((count, 128), f32),
            jax.ShapeDtypeStruct((count, D), bf16),
        ]
        + [jax.ShapeDtypeStruct((D, count), bf16)] * 3,
        input_output_aliases={4: 0},
        scratch_shapes=[pltpu.VMEM((D, D), bf16), pltpu.SemaphoreType.DMA],
        compiler_params=pltpu.CompilerParams(vmem_limit_bytes=VMEM),
        cost_estimate=pl.CostEstimate(flops=14_000_000_000, bytes_accessed=MIB, transcendentals=0),
        name="window",
    )


def ffn_kernel(meta, pieces, blocks, place, normed_ref, rstd_ref, hid_ref, cot_ref, vec_ref, b1_ref, proj_w, *refs):
    piece_refs = refs[:pieces]
    (out_ref, fb_ref, ab_ref, ib_ref, branch_ref, small_ref, db1_ref, keep, send) = refs[pieces : pieces + 9]
    (out_w, inner_w, down_w, act, down_back, sem, wsem) = refs[pieces + 9 :]
    step = pl.program_id(0)

    @pl.when(step == 0)
    def _():
        start_all(inner_blocks(place, zip(piece_refs, meta), inner_w, sem.at[0]))
        start_all(down_blocks(place, zip(piece_refs, meta), down_w, sem.at[1]))
        start_all(out_weight_copies(proj_w, out_w, sem.at[2]))
        small_ref[...] = jnp.zeros_like(small_ref)
        db1_ref[...] = jnp.zeros_like(db1_ref)
        wait_whole(inner_w, sem.at[0])
        wait_whole(down_w, sem.at[1])
        wait_whole(out_w, sem.at[2])

    @pl.when(step < blocks)
    def _():
        rows = aligned(step * BLOCK, BLOCK, BLOCK)
        first_gain, first_shift = vec_ref[3:4, :], vec_ref[4:5, :]
        second_gain, second_shift = vec_ref[6:7, :], vec_ref[7:8, :]
        first_normed = normed_ref[...]
        hidden_low = hid_ref[...]
        total = first_normed * first_gain + first_shift + vec_ref[5:6, :]
        slopes = []
        for c in range(FF // WIDTH):
            cols = pl.ds(c * WIDTH, WIDTH)
            u = dot(hidden_low, inner_w[:, cols]) + b1_ref[:, cols]
            below, bell = gelu_parts(u)
            active = (u * below).astype(bf16)
            act[rows, cols] = active
            slopes.append(below + u * bell * GAUSS_DENSITY)
            total = total + dot(active, down_w[cols, :])
        second_normed, second_rstd = norm_rows(total)
        out_ref[...] = second_normed * second_gain + second_shift
        cot = cot_ref[...]
        second_back = norm_back(cot, second_normed, second_rstd, second_gain)
        back_low = second_back.astype(bf16)
        down_back[rows, :] = back_low
        hidden_back = second_back
        for c in range(FF // WIDTH):
            cols = pl.ds(c * WIDTH, WIDTH)
            ib = (dot_t(back_low, down_w[cols, :]) * slopes[c]).astype(bf16)
            ib_ref[:, cols] = ib
            db1_ref[:, cols] += fold_rows(ib.astype(f32))
            hidden_back = hidden_back + dot_t(ib, inner_w[:, cols])
        first_back = norm_back(hidden_back, first_normed, rstd_ref[:, 0:1], first_gain)
        fb_ref[...] = first_back
        branch_low = first_back.astype(bf16)
        branch_ref[...] = branch_low
        ab_ref[...] = dot_t(branch_low, out_w[...]).astype(bf16)
        sums = (
            branch_low.astype(f32),
            hidden_back * first_normed,
            hidden_back,
            back_low.astype(f32),
            cot * second_normed,
            cot,
        )
        for i, v in enumerate(sums):
            small_ref[i] += fold_rows(v)

    @pl.when(step >= blocks)
    def _():
        chunk = step - blocks
        width = FF // DOWN_STEPS
        rows = aligned(chunk * width, width, 128)
        down_w[rows, :] = dot_l(act[:, rows], down_back[...]).astype(bf16)
        for i in range(CHIPS // DOWN_STEPS):
            chip = chunk * (CHIPS // DOWN_STEPS) + i
            for half in range(2):
                at = (chip * 2 + half) * (2 * PAIR_ROWS)
                pairs = [
                    (down_w.at[aligned(at + k * PAIR_ROWS, PAIR_ROWS, 16)], pl.ds(k * D, D)) for k in range(2)
                ]
                hand_over(place, chip, half, keep, send, pairs, wsem)

    @pl.when(step == blocks + DOWN_STEPS - 1)
    def _():
        wait_whole(keep, wsem)
        wait_whole(send, wsem)


def feed_forward(place, normed, rstd, hid, cotangent, vectors, inner_bias, weights, pieces, meta):
    count = normed.shape[0]
    blocks = count // BLOCK
    token = lambda width: pl.BlockSpec((BLOCK, width), lambda s: (jnp.minimum(s, blocks - 1), 0))
    return pl.pallas_call(
        functools.partial(ffn_kernel, meta, len(pieces), blocks),
        grid=(blocks + DOWN_STEPS,),
        in_specs=[SMEM, token(D), token(128), token(D), token(D), whole(16, D), whole(1, FF), ANY]
        + [ANY] * len(pieces),
        out_specs=[token(D), token(D), token(D), token(FF), token(D), whole(6, 8, D), whole(8, FF), ANY, ANY],
        out_shape=[
            jax.ShapeDtypeStruct((count, D), f32),
            jax.ShapeDtypeStruct((count, D), f32),
            jax.ShapeDtypeStruct((count, D), bf16),
            jax.ShapeDtypeStruct((count, FF), bf16),
            jax.ShapeDtypeStruct((count, D), bf16),
            jax.ShapeDtypeStruct((6, 8, D), f32),
            jax.ShapeDtypeStruct((8, FF), f32),
            jax.ShapeDtypeStruct((CHIPS, PAIR_ROWS, DOWN_BLOCK), bf16),
            jax.ShapeDtypeStruct((CHIPS, PAIR_ROWS, DOWN_BLOCK), bf16),
        ],
        scratch_shapes=[
            pltpu.VMEM((D, D), bf16),
            pltpu.VMEM((D, FF), bf16),
            pltpu.VMEM((FF, D), bf16),
            pltpu.VMEM((count, FF), bf16),
            pltpu.VMEM((count, D), bf16),
            pltpu.SemaphoreType.DMA((3,)),
            pltpu.SemaphoreType.DMA,
        ],
        compiler_params=pltpu.CompilerParams(vmem_limit_bytes=ALL_VMEM),
        cost_estimate=pl.CostEstimate(flops=52_000_000_000, bytes_accessed=40 * MIB, transcendentals=0),
        name="feed_forward",
    )(place, normed, rstd, hid, cotangent, vectors, inner_bias, weights, *pieces)


def inner_grads_kernel(hid_t, ib_ref, place, att_in, branch_in, keep, send, att_t, branch, out_g, inner_g, sem, wsem):
    step = pl.program_id(0)
    steps = FF // D
    later = [pltpu.make_async_copy(att_in, att_t, sem.at[0]), pltpu.make_async_copy(branch_in, branch, sem.at[1])]

    @pl.when(step == 0)
    def _():
        start_all(later)

    def give(grads, half, width, lane):
        for chip in range(CHIPS):
            block = grads.at[pl.ds(chip * PAIR_ROWS, PAIR_ROWS), pl.ds(half * width, width)]
            hand_over(place, chip, half, keep, send, [(block, pl.ds(lane, width))], wsem)

    @pl.when(step < steps)
    def _():
        cols = aligned(step * D, D, 128)
        inner_g[:, cols] = dot(hid_t[...], ib_ref[...]).astype(bf16)
        for half in range(2):

            @pl.when(step == (half + 1) * (steps // 2) - 1)
            def _():
                give(inner_g, half, INNER_HALF, OUT_HALF)

    @pl.when(step == steps)
    def _():
        for copy in later:
            copy.wait()
        out_g[...] = dot(att_t[...], branch[...]).astype(bf16)
        for half in range(2):
            give(out_g, half, OUT_HALF, 0)
        wait_whole(keep, wsem)
        wait_whole(send, wsem)


def inner_grads(place, hid_t, inner_back, att_t, branch):
    count = hid_t.shape[1]
    steps = FF // D
    return pl.pallas_call(
        inner_grads_kernel,
        grid=(steps + 1,),
        in_specs=[
            whole(D, count),
            pl.BlockSpec((count, D), lambda s: (0, jnp.minimum(s, steps - 1))),
            SMEM,
            ANY,
            ANY,
        ],
        out_specs=[ANY, ANY],
        out_shape=[jax.ShapeDtypeStruct((CHIPS, PAIR_ROWS, INNER_BLOCK), bf16)] * 2,
        scratch_shapes=[
            pltpu.VMEM((D, count), bf16),
            pltpu.VMEM((count, D), bf16),
            pltpu.VMEM((D, D), bf16),
            pltpu.VMEM((D, FF), bf16),
            pltpu.SemaphoreType.DMA((2,)),
            pltpu.SemaphoreType.DMA,
        ],
        compiler_params=pltpu.CompilerParams(vmem_limit_bytes=ALL_VMEM),
        cost_estimate=pl.CostEstimate(flops=4_000_000_000, bytes_accessed=MIB, transcendentals=0),
        name="inner_grads",
    )(hid_t, inner_back, place, att_t, branch)


def attend_back_pair(queries, keys, values, upstream, prob_ref, dq_ref, dk_ref, dv_ref):
    lows, backs = [], []
    masks = lane_masks()
    for i, mask in enumerate(masks):
        low = prob_ref[i]
        weight = low.astype(f32)
        weight_back = dot_t(values * mask, upstream)
        mean = jnp.sum(weight * weight_back, axis=0, keepdims=True)
        lows.append(low)
        backs.append((weight * (weight_back - mean)).astype(bf16))
    each = lambda v: jnp.concatenate([v * mask for mask in masks], axis=0)
    dv_ref[...] = dot(jnp.concatenate(lows, axis=1), each(upstream)).astype(bf16)
    dk_ref[...] = (dot(jnp.concatenate(backs, axis=1), each(queries)) * 0.125).astype(bf16)
    dq_ref[...] = (dot_l(jnp.concatenate(backs, axis=0), each(keys)) * 0.125).astype(bf16)


def attend_back_kernel(q_ref, k_ref, v_ref, up_ref, prob_ref, *refs):
    attend_back_pair(q_ref[...], k_ref[...], v_ref[...], up_ref[...], prob_ref, *refs[-3:])


def pair_specs(rows, first, last):
    pairs = H // 2
    pair = lambda s: jnp.minimum(first + s, last)
    lane = lambda kind: pl.BlockSpec((rows, 128), lambda s: (pair(s) // pairs, kind * pairs + pair(s) % pairs))
    return [lane(0), lane(1), lane(2), lane(0), pl.BlockSpec((2, rows, rows), lambda s: (pair(s), 0, 0))]


def attend_back(first, count, qkv, back, prob, grads=(), deps=()):
    specs = pair_specs(prob.shape[1], first, first + count - 1)
    return call(
        attend_back_kernel,
        (qkv, qkv, qkv, back, prob, *grads),
        deps,
        grid=(count,),
        in_specs=specs + [ANY] * len(grads),
        out_specs=[specs[0]] * 3,
        out_shape=[jax.ShapeDtypeStruct(back.shape, bf16)] * 3,
        input_output_aliases={5 + i: i for i in range(len(grads))},
        compiler_params=pltpu.CompilerParams(vmem_limit_bytes=ALL_VMEM),
        cost_estimate=pl.CostEstimate(flops=3_000_000_000, bytes_accessed=MIB, transcendentals=0),
        name=f"attend_back_{first}",
    )


def proj_grads_kernel(place, turned, small_ref, db1_ref, dq, dk, dv, keep, send, grads, packed, bias, sem, wsem):
    step = pl.program_id(0)
    copies = [pltpu.make_async_copy(v, grads.at[i], sem.at[i]) for i, v in enumerate((dq, dk, dv))]

    @pl.when(step == 0)
    def _():
        start_all([copies[1], copies[2], copies[0]])

    for turn, which in enumerate((1, 2, 0)):

        @pl.when(step == turn)
        def _():
            copies[which].wait()
            g = dot(turned[...], grads[which]).astype(bf16)
            if which == 1:
                packed[:, D:QKV_HALF] = g[:, : D // 2]
                packed[:, QKV_BLOCK : QKV_BLOCK + D // 2] = g[:, D // 2 :]
            else:
                at = 0 if which == 0 else QKV_BLOCK + D // 2
                packed[:, at : at + D] = g
                bias[which // 2] = fold_rows(grads[which].astype(f32))

    @pl.when(step == 0)
    def _():
        owner = lax.broadcasted_iota(jnp.int32, (SLABS, FF), 1) // (4 * SLAB)
        one = lax.broadcasted_iota(jnp.int32, (SLABS, FF), 0)
        mine = jnp.where(owner == one, jnp.sum(db1_ref[...], axis=0, keepdims=True), 0.0)
        place_of = lax.broadcasted_iota(jnp.int32, (FF, 128), 0) % (4 * SLAB)
        pick = (place_of == lax.broadcasted_iota(jnp.int32, (FF, 128), 1)).astype(f32)
        table = lax.dot_general(
            mine, pick, (((1,), (0,)), ((), ())), precision=lax.Precision.HIGHEST, preferred_element_type=f32
        )
        spread = jnp.broadcast_to(table[:, None, :], (SLABS, SLAB, 128)).reshape(D, 128)
        packed[:, QKV_BLOCK + QKV_HALF :] = spread.astype(bf16)

    def give(half):
        for chip in range(CHIPS):
            block = packed.at[pl.ds(chip * PAIR_ROWS, PAIR_ROWS), pl.ds(half * QKV_BLOCK, QKV_BLOCK)]
            hand_over(place, chip, half, keep, send, [(block, pl.ds(0, QKV_BLOCK))], wsem)

    @pl.when(step == 1)
    def _():
        give(1)

    @pl.when(step == 2)
    def _():
        rows_of = [bias[...], small_ref[...], jnp.zeros((120, 8, D), f32)]
        packed[:, QKV_HALF:QKV_BLOCK] = jnp.sum(jnp.concatenate(rows_of, axis=0), axis=1).T.astype(bf16)
        give(0)
        wait_whole(keep, wsem)
        wait_whole(send, wsem)


def proj_grads(place, turned, small, inner_bias_grad, grads, deps=()):
    count = turned.shape[1]
    return call(
        proj_grads_kernel,
        (place, turned, small, inner_bias_grad, *grads),
        deps,
        grid=(3,),
        in_specs=[SMEM, whole(D, count), whole(6, 8, D), whole(8, FF), ANY, ANY, ANY],
        out_specs=[ANY, ANY],
        out_shape=[jax.ShapeDtypeStruct((CHIPS, PAIR_ROWS, QKV_BLOCK), bf16)] * 2,
        scratch_shapes=[
            pltpu.VMEM((3, count, D), bf16),
            pltpu.VMEM((D, 2 * QKV_BLOCK), bf16),
            pltpu.VMEM((2, 8, D), f32),
            pltpu.SemaphoreType.DMA((3,)),
            pltpu.SemaphoreType.DMA,
        ],
        compiler_params=pltpu.CompilerParams(vmem_limit_bytes=ALL_VMEM),
        cost_estimate=pl.CostEstimate(flops=4_000_000_000, bytes_accessed=MIB, transcendentals=0),
        name="proj_grads",
    )


def input_back_kernel(fb_ref, dq_ref, dk_ref, dv_ref, w_ref, *refs):
    half = D // 2
    total = fb_ref[...] + dot_t(dq_ref[...], w_ref[:, 0:D])
    total = total + dot_t(dk_ref[:, :half], w_ref[:, D:QKV_HALF])
    total = total + dot_t(dk_ref[:, half:], w_ref[:, PROJ_BLOCK : PROJ_BLOCK + half])
    out_ref, small_ref = refs[-2:]
    small_ref[...] = total[0:8, 0:128]
    out_ref[...] = total + dot_t(dv_ref[...], w_ref[:, PROJ_BLOCK + half : PROJ_BLOCK + QKV_HALF])


def input_back(first, blocks, first_back, grads, weights, given=(), deps=()):
    token = pl.BlockSpec((BLOCK, D), lambda s: (first + s, 0))
    return call(
        input_back_kernel,
        (first_back, *grads, weights, *given),
        deps,
        grid=(blocks,),
        in_specs=[token] * 4 + [whole(D, 2 * PROJ_BLOCK)] + [ANY] * len(given),
        out_specs=[token, whole(8, 128)],
        out_shape=[jax.ShapeDtypeStruct(first_back.shape, f32), jax.ShapeDtypeStruct((8, 128), f32)],
        input_output_aliases={5: 0} if given else {},
        compiler_params=pltpu.CompilerParams(vmem_limit_bytes=ALL_VMEM),
        cost_estimate=pl.CostEstimate(flops=10_000_000_000, bytes_accessed=MIB, transcendentals=0),
        name=f"input_back_{first}",
    )


def add_up_kernel(jobs, passed, place, *refs):
    refs[len(refs) - 1][...] = refs[0][0, 0:8, 0:128].astype(f32)
    first, out = 0, sum(count for count, _ in jobs) + passed
    for count, kind in jobs:
        terms = refs[first : first + count]
        first += count

        def total(slot):
            return sum((ref[slot].astype(f32) for ref in terms[1:]), terms[0][slot].astype(f32))

        slots = terms[0].shape[0]
        if kind == "upper":

            def one(i, _, total=total, ready=refs[out]):
                ready[i] = total(i).astype(bf16)
                return 0

            lax.fori_loop(0, slots, one, 0)
            out += 1
        elif kind == "both":
            half = slots // 2

            def one(i, _, total=total, ready=refs[out], rest=refs[out + 1], half=half):
                rest[i] = total(i)
                ready[i] = total(half + i).astype(bf16)
                return 0

            lax.fori_loop(0, half, one, 0)
            out += 2
        elif kind == "down":
            whole_sum = total(0)
            refs[out][0:PAIR_ROWS, :] = whole_sum[:, :D]
            refs[out][PAIR_ROWS:, :] = whole_sum[:, D:]
            out += 1
        else:
            whole_sum = total(0)
            low_core = place[1] == 0
            low, high = whole_sum[:SLAB], whole_sum[SLAB:]
            refs[out][...] = jnp.where(low_core, low, high)
            refs[out + 1][...] = jnp.where(low_core, high, low)
            out += 2


def add_up(place, *groups, passed=(), deps=(), vmem=ALL_VMEM):
    operands, specs, out_specs, shapes, jobs = [], [], [], [], []
    for size, terms, lazy in groups:
        _, rows, lanes = terms[0].shape
        half = size // 2
        kind = "upper" if lazy else "both" if size > 1 else "down" if lanes == DOWN_BLOCK else "halves"
        operands += terms
        take = (half, 1) if kind == "upper" else (size, 0)
        specs += [pl.BlockSpec((take[0], rows, lanes), lambda s, at=take[1]: (at, 0, 0))] * len(terms)
        if size > 1:
            kinds = [bf16] if kind == "upper" else [bf16, f32]
            out_specs += [whole(half, rows, lanes)] * len(kinds)
            shapes += [jax.ShapeDtypeStruct((half, rows, lanes), dtype) for dtype in kinds]
        else:
            ends = [(2 * PAIR_ROWS, D)] if kind == "down" else [(SLAB, lanes)] * 2
            out_specs += [whole(*end) for end in ends]
            shapes += [jax.ShapeDtypeStruct(end, f32) for end in ends]
        jobs.append((len(terms), kind))
    return call(
        lambda *refs: add_up_kernel(jobs, len(passed), refs[0], *refs[1:]),
        [place] + operands + list(passed),
        deps,
        grid=(1,),
        in_specs=[SMEM] + specs + [ANY] * len(passed),
        out_specs=out_specs + [ANY] * len(passed) + [whole(8, 128)],
        out_shape=shapes
        + [jax.ShapeDtypeStruct(v.shape, v.dtype) for v in passed]
        + [jax.ShapeDtypeStruct((8, 128), f32)],
        input_output_aliases={1 + len(operands) + i: len(shapes) + i for i in range(len(passed))},
        compiler_params=pltpu.CompilerParams(vmem_limit_bytes=vmem),
        cost_estimate=pl.CostEstimate(flops=1000, bytes_accessed=1000, transcendentals=0),
        name="add_up",
    )


def finish_inner_kernel(place, mine, other, out_g, inner_g, small):
    low_core = place[1] == 0
    low = jnp.where(low_core, mine[...], other[...])
    high = jnp.where(low_core, other[...], mine[...])
    out_g[:, :OUT_HALF], out_g[:, OUT_HALF:] = low[:, :OUT_HALF], high[:, :OUT_HALF]
    inner_g[:, :INNER_HALF], inner_g[:, INNER_HALF:] = low[:, OUT_HALF:], high[:, OUT_HALF:]
    small[...] = low[0:8, 0:128]


def finish_proj_kernel(place, mine, other, dq, dk, dv, bias, *vectors):
    low_core = place[1] == 0
    low = jnp.where(low_core, mine[...], other[...])
    high = jnp.where(low_core, other[...], mine[...])
    half = D // 2
    dq[...] = low[:, :D]
    dk[:, :half], dk[:, half:] = low[:, D:QKV_HALF], high[:, :half]
    dv[...] = high[:, half:QKV_HALF]
    bias[...] = high[0, QKV_HALF : QKV_HALF + 4 * SLAB]
    rows = low[:, QKV_HALF:].T
    for i, out in enumerate(vectors):
        out[...] = rows[i, 0:SLAB]


def finish(kernel, place, mine, other, shapes, name, deps=()):
    at = lambda shape: pl.BlockSpec(shape, lambda s: (0,) * len(shape))
    return call(
        kernel,
        (place, mine, other),
        deps,
        grid=(1,),
        in_specs=[SMEM, at(mine.shape), at(mine.shape)],
        out_specs=[at(shape) for shape in shapes],
        out_shape=[jax.ShapeDtypeStruct(shape, f32) for shape in shapes],
        compiler_params=pltpu.CompilerParams(vmem_limit_bytes=LITTLE),
        cost_estimate=pl.CostEstimate(flops=1000, bytes_accessed=1000, transcendentals=0),
        name=name,
    )


def finish_inner(place, mine, other):
    return finish(finish_inner_kernel, place, mine, other, [(SLAB, D), (SLAB, FF), (8, 128)], "finish_inner")


def finish_proj(place, mine, other, deps=()):
    shapes = [(SLAB, D)] * 3 + [(4 * SLAB,)] + [(SLAB,)] * 8
    return finish(finish_proj_kernel, place, mine, other, shapes, "finish_proj", deps)


AXES = ("dp", "fsdp")


CORE = (1, 1)
ALONG_Z_FIRST, ALONG_Z_THEN, ALONG_Z_BOTH, ALONG_XY_FIRST, ALONG_XY_THEN = (16, 8), (8, 16), (24, 24), (2, 4), (4, 2)
FAST_SHAPE = {"dp": 4, "fsdp": 8}


def move(v, masks):
    return lax.ppermute(v, AXES, [(i, i ^ masks[i & 1]) for i in range(SLABS)])


SUM_STEPS = (ALONG_XY_THEN, ALONG_XY_FIRST, ALONG_Z_THEN, ALONG_Z_FIRST)


def after(*values):
    return lax.optimization_barrier(values)


class Sums:
    def __init__(self, keep, got):
        self.size, self.terms, self.step = CHIPS, [keep, got], 0

    def send(self, outs, lazy):
        ready = outs.pop(0)
        if not lazy:
            self.terms = [outs.pop(0)]
        self.size //= 2
        self.terms = self.terms + [move(ready, SUM_STEPS[self.step])]
        self.step += 1


def add_and_send(place, *groups, lazy=False, **options):
    outs = list(add_up(place, *[(g.size, g.terms, lazy) for g in groups], **options))
    for g in groups:
        if g.size > 1:
            g.send(outs, lazy)
    return outs


def fast_blocks(shards, core):
    (qw, kw, vw, ow, qb, vb, ob, fg, fs, iw, ib, dw, db, sg, ss) = shards
    vectors = jnp.pad(jnp.stack([qb, vb, ob, fg, fs, db, sg, ss], axis=1), ((0, 0), (0, 120)))
    inner_bias = jnp.pad(ib.reshape(1, 4 * SLAB), ((0, SLAB - 1), (0, 128 - 4 * SLAB)))
    half = D // 2
    halves = [
        jnp.concatenate([qw, kw[:, :half], vectors, ow[:, :half], iw[:, :INNER_HALF]], axis=1),
        jnp.concatenate([kw[:, half:], vw, inner_bias, ow[:, half:], iw[:, INNER_HALF:]], axis=1),
    ]
    low_core = core == 0
    own = jnp.where(low_core, halves[0], halves[1])
    other = move(jnp.where(low_core, halves[1], halves[0]), CORE)
    rows = jnp.concatenate([jnp.where(low_core, own, other), jnp.where(low_core, other, own)], axis=0)
    return rows[:, :PROJ_BLOCK], rows[:, PROJ_BLOCK:], jnp.concatenate([dw[:PAIR_ROWS], dw[PAIR_ROWS:]], axis=1)


def gather_plain(shards):
    (qw, kw, vw, ow, qb, vb, ob, fg, fs, iw, ib, dw, db, sg, ss) = [
        lax.all_gather(v, AXES, axis=0, tiled=True) for v in shards
    ]
    vectors = jnp.pad(jnp.stack([qb, vb, ob, fg, fs, db, sg, ss], axis=1), ((0, 0), (0, 120)))
    inner_bias = jnp.pad(ib.reshape(SLABS, 1, 4 * SLAB), ((0, 0), (0, SLAB - 1), (0, 128 - 4 * SLAB))).reshape(D, 128)
    half = D // 2
    chips = lambda v: v.reshape(CHIPS, PAIR_ROWS, -1)
    down = dw.reshape(CHIPS, 2, 2, PAIR_ROWS, D)
    first = [
        chips(jnp.concatenate([qw, kw[:, :half], vectors, ow[:, :half]], axis=1)),
        chips(jnp.concatenate([kw[:, half:], vw, inner_bias, ow[:, half:]], axis=1)),
    ]
    second = [
        jnp.concatenate([chips(iw[:, c * INNER_HALF : (c + 1) * INNER_HALF]), down[:, c, 0], down[:, c, 1]], axis=2)
        for c in range(2)
    ]
    slots = lambda halves: [v[np.array(SLOT_CHIPS[c])] for c, v in enumerate(halves)]
    return slots(first), slots(second)


def local(fast, inputs, lengths, *rest):
    shards, cotangent = rest[:15], rest[15]
    both = lambda v, came: jnp.concatenate([v, came])
    if fast:
        linear = lax.axis_index(AXES)
        core = linear & 1
        place = jnp.stack([linear >> 1, core]).astype(jnp.int32)
        first, inner, down = fast_blocks(shards, core)
        first = first[None]
        first = both(first, move(first, ALONG_Z_FIRST))
        first, second = after(first, jnp.concatenate([inner, down], axis=1)[None])
        second = jnp.concatenate([second] + [move(second, steps) for steps in (ALONG_Z_FIRST, ALONG_Z_THEN, ALONG_Z_BOTH)])
        first = both(first, move(first, ALONG_Z_THEN))
        first_then, first_core = move(first, ALONG_XY_THEN), move(first, CORE)
        first_came = move(first, ALONG_XY_FIRST)
        first_last, came_core = move(first_came, ALONG_XY_THEN), move(first_came, CORE)
        first_then, first_last, second = after(first_then, first_last, second)
        first = [first, first_came, first_then, first_last]
        first += [first_core, came_core, move(first_then, CORE), move(first_last, CORE)]
        second_came, second_then, second_core = move(second, ALONG_XY_FIRST), move(second, ALONG_XY_THEN), move(second, CORE)
        meta = tuple((at, other) for other in (False, True) for at in range(0, CHIPS, 4))
    else:
        place = jnp.zeros((2,), jnp.int32)
        first, second = gather_plain(shards)
        meta = ((0, False), (0, True))
    qkv, attended, stats, weights, vectors = attend(place, lengths, inputs, first, meta)
    prob = probs(0, lengths, qkv, stats)
    if fast:
        second_came, prob = after(second_came, prob)
        second_last, came_core = move(second_came, ALONG_XY_THEN), move(second_came, CORE)
    prob, normed, rstd, hid, inputs_t, attended_t, hid_t = window(
        1, lengths, inputs, qkv, attended, stats, weights, vectors, prob
    )
    bias_at = PROJ_BLOCK + QKV_HALF
    inner_bias = weights[::SLAB, bias_at : bias_at + 4 * SLAB].reshape(1, FF).astype(f32)
    if fast:
        second_then, second_last, normed, inner_bias = after(second_then, second_last, normed, inner_bias)
        second = [second, second_came, second_then, second_last]
        second += [second_core, came_core, move(second_then, CORE), move(second_last, CORE)]
    output, first_back, back, inner_back, branch, small, db1, down_keep, down_send = feed_forward(
        place, normed, rstd, hid, cotangent, vectors, inner_bias, weights, second, meta
    )
    inner_keep, inner_send = inner_grads(place, hid_t, inner_back, attended_t, branch)
    pairs = lengths.shape[0] * (H // 2)
    third = pairs // 3
    deps = []
    if fast:
        down = Sums(down_keep, move(down_send, CORE))
        inner_send, *deps = add_and_send(place, down, lazy=True, passed=[inner_send], deps=[inner_keep])
        inner = Sums(inner_keep, move(inner_send, CORE))
    grads = attend_back(0, third, qkv, back, prob, deps=deps)
    if fast:
        deps = add_and_send(place, inner, lazy=True, deps=grads[:1])
    grads = attend_back(third, third, qkv, back, prob, grads, deps=deps)
    if fast:
        deps = add_and_send(place, down, lazy=True, deps=grads[:1])
    grads = attend_back(2 * third, pairs - 2 * third, qkv, back, prob, grads, deps=deps)
    if fast:
        deps = add_and_send(place, inner, down, lazy=True, deps=grads[:1])
    proj_keep, proj_send = proj_grads(place, inputs_t, small, db1, grads, deps=deps)
    blocks = inputs.shape[0] // BLOCK
    if fast:
        proj_send, *deps = add_and_send(place, inner, down, passed=[proj_send], deps=[proj_keep])
        proj = Sums(proj_keep, move(proj_send, CORE))
        deps = add_and_send(place, proj, lazy=True, deps=deps)
        grad_input, *deps = input_back(0, blocks, first_back, grads, weights, deps=deps)
        down_grad, *deps = add_and_send(place, proj, inner, down, deps=deps, vmem=LITTLE)
        mine, other, *deps = add_and_send(place, proj, inner, deps=deps, vmem=LITTLE)
        out_grad, inner_grad, *deps = finish_inner(place, mine, move(other, CORE))
        deps = add_and_send(place, proj, deps=deps, vmem=LITTLE)
        mine, other, _ = add_and_send(place, proj, deps=deps, vmem=LITTLE)
        *square, bias, v0, v1, v2, v3, v4, v5, v6, v7 = finish_proj(place, mine, move(other, CORE))
        vectors = [v0, v1, v2, v3, v4, v5, v6, v7]
    else:
        grad_input, _ = input_back(0, blocks, first_back, grads, weights)
        shard = lambda *v: lax.psum_scatter(jnp.concatenate(v, axis=1), AXES, scatter_dimension=0, tiled=True)
        by_chip = lambda pair: [v[np.argsort(np.array(SLOT_CHIPS[c]))].astype(f32) for c, v in enumerate(pair)]
        low, high = (v.reshape(D, -1) for v in by_chip((inner_keep, inner_send)))
        out_grad, inner_grad = shard(low[:, :OUT_HALF], high[:, :OUT_HALF]), shard(low[:, OUT_HALF:], high[:, OUT_HALF:])
        parts = [jnp.stack([v[:, :, :D], v[:, :, D:]], axis=1) for v in by_chip((down_keep, down_send))]
        down_grad = shard(jnp.stack(parts, axis=1).reshape(FF, D))
        low, high = (v.reshape(D, -1) for v in by_chip((proj_keep, proj_send)))
        half = D // 2
        square = shard(low[:, :D]), shard(low[:, D:QKV_HALF], high[:, :half]), shard(high[:, half:QKV_HALF])
        columns = shard(low[:, QKV_HALF:])
        vectors = [columns[:, i] for i in range(8)]
        bias = shard(high[::SLAB, QKV_HALF : QKV_HALF + 4 * SLAB].reshape(FF, 1))[:, 0]
    return (
        output,
        grad_input,
        *square,
        out_grad,
        *vectors[:5],
        inner_grad,
        bias,
        down_grad,
        *vectors[5:],
    )


def solution(mesh):
    rows, flat = P(AXES, None), P(AXES)
    params = (rows,) * 4 + (flat,) * 5 + (rows, flat, rows, flat, flat, flat)
    return jax.shard_map(
        functools.partial(local, dict(mesh.shape) == FAST_SHAPE),
        mesh=mesh,
        in_specs=(rows, flat) + params + (rows,),
        out_specs=(rows, rows) + params,
        check_vma=False,
    )
```

```python
import functools
import math

import jax
import jax.numpy as jnp
import numpy as np
from jax import lax
from jax.experimental import pallas as pl
from jax.experimental.pallas import tpu as pltpu
from jax.sharding import PartitionSpec as P

D = 768
H = 12
DH = 64
FF = 3072
SLABS = 32
SLAB = D // SLABS
CHIPS = SLABS // 2
PAIR_ROWS = 2 * SLAB
NORM_EPSILON = 1e-12
MASKED_SCORE = -1000000000.0
GAUSS_DENSITY = 0.3989422804014327
LOG2E = 1.4426950408889634
MIB = 1 << 20
VMEM = 62 * MIB
ALL_VMEM = 127 * MIB // 2
LITTLE = 16 * MIB

QKV_HALF = 3 * D // 2
QKV_BLOCK = QKV_HALF + 128
OUT_HALF = D // 2
PROJ_BLOCK = QKV_BLOCK + OUT_HALF
INNER_HALF = FF // 2
INNER_BLOCK = OUT_HALF + INNER_HALF
DOWN_BLOCK = 2 * D

SLOT_BITS = ((8, 4, 1, 2), (4, 8, 2, 1))
SLOT_CHIPS = tuple(
    tuple(sum(bit for i, bit in enumerate(bits) if slot >> i & 1) for slot in range(CHIPS)) for bits in SLOT_BITS
)

bf16 = jnp.bfloat16
f32 = jnp.float32
ANY = pl.BlockSpec(memory_space=pl.ANY)
SMEM = pl.BlockSpec(memory_space=pltpu.SMEM)


def dot(a, b):
    return lax.dot_general(a, b, (((1,), (0,)), ((), ())), preferred_element_type=f32)


def dot_t(a, b):
    return lax.dot_general(a, b, (((1,), (1,)), ((), ())), preferred_element_type=f32)


def dot_l(a, b):
    return lax.dot_general(a, b, (((0,), (0,)), ((), ())), preferred_element_type=f32)


def call(kernel, operands, deps, in_specs, **options):
    count = len(operands)

    def body(*refs):
        kernel(*refs[:count], *refs[count + len(deps) :])

    in_specs = in_specs + [whole(8, 128) if v.shape == (8, 128) else ANY for v in deps]
    return pl.pallas_call(body, in_specs=in_specs, **options)(*operands, *deps)


def aligned(start, size, unit):
    return pl.ds(pl.multiple_of(start, unit), size)


def chip_of(slot, half):
    return jnp.where(half == 0, SLOT_CHIPS[0][slot], SLOT_CHIPS[1][slot])


def slot_of(chip, half):
    bits = SLOT_BITS[half]
    return sum(jnp.where((chip & bit) != 0, 1 << i, 0) for i, bit in enumerate(bits))


def blocks_of(place, pieces):
    for ref, (first, other) in pieces:
        half = 1 - place[1] if other else place[1]
        for i in range(ref.shape[0]):
            yield ref, i, place[0] ^ chip_of(first + i, half), half


def proj_blocks(place, pieces, weights, sem):
    for ref, i, chip, half in blocks_of(place, pieces):
        rows = aligned(chip * PAIR_ROWS, PAIR_ROWS, 16)
        yield pltpu.make_async_copy(ref.at[i], weights.at[rows, aligned(half * PROJ_BLOCK, PROJ_BLOCK, 128)], sem)


def inner_blocks(place, pieces, inner_w, sem):
    for ref, i, chip, half in blocks_of(place, pieces):
        rows = aligned(chip * PAIR_ROWS, PAIR_ROWS, 16)
        yield pltpu.make_async_copy(
            ref.at[i, :, pl.ds(0, INNER_HALF)],
            inner_w.at[rows, aligned(half * INNER_HALF, INNER_HALF, 128)],
            sem,
        )


def down_blocks(place, pieces, down_w, sem):
    for ref, i, chip, half in blocks_of(place, pieces):
        for k in range(2):
            at = (chip * 2 + half) * (2 * PAIR_ROWS) + k * PAIR_ROWS
            yield pltpu.make_async_copy(
                ref.at[i, :, pl.ds(INNER_HALF + k * D, D)], down_w.at[aligned(at, PAIR_ROWS, 16), :], sem
            )


def start_all(copies):
    for c in copies:
        c.start()


def whole(*shape):
    return pl.BlockSpec(shape, lambda *s: (0,) * len(shape))


def fold_rows(v):
    return jnp.sum(v.reshape(v.shape[0] // 8, 8, v.shape[1]), axis=0)


def hand_over(place, chip, half, keep, send, pairs, sem):
    slot = slot_of(chip ^ place[0], half)
    for mine, out in ((True, keep), (False, send)):

        @pl.when((place[1] == half) == mine)
        def _():
            for source, lanes in pairs:
                pltpu.make_async_copy(source, out.at[slot, :, lanes], sem).start()


def wait_whole(ref, sem):
    pltpu.make_async_copy(ref, ref, sem).wait()


def lane_masks():
    low = (lax.broadcasted_iota(jnp.int32, (1, 128), 1) < DH).astype(f32)
    return low.astype(bf16), (1.0 - low).astype(bf16)


def attend_kernel(meta, n_pieces, place, lengths, x_ref, *refs):
    piece_refs = refs[:n_pieces]
    qkv_ref, att_ref, stat_ref, weights, vectors = refs[n_pieces : n_pieces + 5]
    sem = refs[-1]
    seq = pl.program_id(0)
    rows = x_ref.shape[0]

    @pl.when(seq == 0)
    def _():
        start_all(proj_blocks(place, zip(piece_refs, meta), weights, sem))
        wait_whole(weights, sem)
        small = weights[:, QKV_HALF:QKV_BLOCK].astype(f32)
        vectors[...] = small.T[0:16, :]

    lowered = x_ref[...].astype(bf16)
    first = dot(lowered, weights[:, 0:QKV_HALF])
    qkv_ref[:, 0:D] = (first[:, 0:D] + vectors[0:1, :]).astype(bf16)
    qkv_ref[:, D:QKV_HALF] = first[:, D:QKV_HALF].astype(bf16)
    second = dot(lowered, weights[:, PROJ_BLOCK : PROJ_BLOCK + QKV_HALF])
    qkv_ref[:, QKV_HALF : 2 * D] = second[:, 0 : D // 2].astype(bf16)
    qkv_ref[:, 2 * D :] = (second[:, D // 2 :] + vectors[1:2, :]).astype(bf16)

    low, high = lane_masks()
    lane = lax.broadcasted_iota(jnp.int32, (1, 128), 1)
    key_at = lax.broadcasted_iota(jnp.int32, (1, rows), 1)
    hidden_keys = jnp.where(key_at < lengths[seq], 0.0, MASKED_SCORE).astype(f32)
    chunk = 256
    ones = jnp.ones((rows, 128), bf16)
    stats = [jnp.zeros((chunk, 128), f32) for _ in range(rows // chunk)]
    for pair in range(H // 2):
        at = pair * 128
        keys = qkv_ref[:, D + at : D + at + 128]
        values = jnp.concatenate([qkv_ref[:, 2 * D + at : 2 * D + at + 128], ones], axis=1)
        keys_of = (keys * low, keys * high)
        for c in range(rows // chunk):
            span = pl.ds(c * chunk, chunk)
            queries = qkv_ref[span, at : at + 128]
            outs = []
            for i in range(2):
                scores = dot_t(queries, keys_of[i]) * (0.125 * LOG2E) + hidden_keys
                peak = jnp.max(scores, axis=-1, keepdims=True)
                weight = jnp.exp2(scores - peak).astype(bf16)
                both = dot(weight, values)
                total = both[:, 128:]
                outs.append(both[:, :128] / total)
                log_total = peak + jnp.log2(total)
                stats[c] = jnp.where(lane == 2 * pair + i, log_total, stats[c])
            att_ref[span, at : at + 128] = jnp.where(lane < DH, outs[0], outs[1]).astype(bf16)
    for c in range(rows // chunk):
        stat_ref[0, :, c * chunk : (c + 1) * chunk] = stats[c].T[0:16, :]


def attend(place, lengths, x, pieces, meta):
    rows = x.shape[0] // lengths.shape[0]
    seqs = lengths.shape[0]
    return pl.pallas_call(
        functools.partial(attend_kernel, meta, len(pieces)),
        grid=(seqs,),
        in_specs=[SMEM, SMEM, pl.BlockSpec((rows, D), lambda s: (s, 0))] + [ANY] * len(pieces),
        out_specs=[
            pl.BlockSpec((rows, 3 * D), lambda s: (s, 0)),
            pl.BlockSpec((rows, D), lambda s: (s, 0)),
            pl.BlockSpec((1, 16, rows), lambda s: (s, 0, 0)),
            whole(D, 2 * PROJ_BLOCK),
            whole(16, D),
        ],
        out_shape=[
            jax.ShapeDtypeStruct((seqs * rows, 3 * D), bf16),
            jax.ShapeDtypeStruct((seqs * rows, D), bf16),
            jax.ShapeDtypeStruct((seqs, 16, rows), f32),
            jax.ShapeDtypeStruct((D, 2 * PROJ_BLOCK), bf16),
            jax.ShapeDtypeStruct((16, D), f32),
        ],
        scratch_shapes=[pltpu.SemaphoreType.DMA],
        compiler_params=pltpu.CompilerParams(vmem_limit_bytes=VMEM),
        cost_estimate=pl.CostEstimate(flops=18_000_000_000, bytes_accessed=20 * MIB, transcendentals=0),
        name="attend",
    )(place, lengths, x, *pieces)


def gelu_parts(u):
    size = jnp.abs(u)
    bell = jnp.exp2(u * u * (-0.5 * LOG2E))
    t = 1.0 / (1.0 + (0.3275911 * math.sqrt(0.5)) * size)
    poly = t * (0.127414796 + t * (-0.142248368 + t * (0.7107068705 + t * (-0.7265760135 + t * 0.5307027145))))
    tail = poly * bell
    below = jnp.where(u < 0.0, tail, 1.0 - tail)
    return below, bell


def mean_rows(v):
    return jnp.sum(v, axis=-1, keepdims=True) * (1.0 / D)


def norm_rows(total):
    center = total - mean_rows(total)
    rstd = lax.rsqrt(mean_rows(center * center) + NORM_EPSILON)
    return center * rstd, rstd


def norm_back(upstream, normed, rstd, gain):
    scaled = upstream * gain
    return rstd * (scaled - mean_rows(scaled) - normed * mean_rows(scaled * normed))


BLOCK = 256
WIDTH = 768
DOWN_STEPS = 8


def out_weight_copies(proj_w, out_w, sem):
    for half in range(2):
        lanes = pl.ds(half * PROJ_BLOCK + QKV_BLOCK, OUT_HALF)
        yield pltpu.make_async_copy(proj_w.at[:, lanes], out_w.at[:, pl.ds(half * OUT_HALF, OUT_HALF)], sem)


def probs_kernel(seq, lengths, q_ref, k_ref, stat_ref, *refs):
    prob_ref = refs[-1]
    pair = pl.program_id(0)
    rows = q_ref.shape[0]
    chunk = 256
    key_at = lax.broadcasted_iota(jnp.int32, (rows, 1), 0)
    hidden_keys = jnp.where(key_at < lengths[seq], 0.0, MASKED_SCORE).astype(f32)
    for i, mask in enumerate(lane_masks()):
        own_keys = k_ref[...] * mask
        for c in range(rows // chunk):
            span = slice(c * chunk, (c + 1) * chunk)
            log_total = stat_ref[0, pl.ds(2 * pair + i, 1), span]
            scores = dot_t(own_keys, q_ref[span, :]) * (0.125 * LOG2E) + hidden_keys
            prob_ref[i, :, span] = jnp.exp2(scores - log_total).astype(bf16)


def probs_specs(seq, rows):
    pairs = H // 2
    lane = lambda kind: pl.BlockSpec((rows, 128), lambda s: (seq, kind * pairs + s))
    specs = [SMEM, lane(0), lane(1), pl.BlockSpec((1, 16, rows), lambda s: (seq, 0, 0))]
    return specs, pl.BlockSpec((2, rows, rows), lambda s: (seq * pairs + s, 0, 0))


def probs(seq, lengths, qkv, stats, deps=()):
    seqs, _, rows = stats.shape
    specs, out = probs_specs(seq, rows)
    return call(
        functools.partial(probs_kernel, seq),
        (lengths, qkv, qkv, stats),
        deps,
        grid=(H // 2,),
        in_specs=specs,
        out_specs=out,
        out_shape=jax.ShapeDtypeStruct((seqs * H, rows, rows), bf16),
        compiler_params=pltpu.CompilerParams(vmem_limit_bytes=VMEM),
        cost_estimate=pl.CostEstimate(flops=8_000_000_000, bytes_accessed=MIB, transcendentals=0),
        name="probs",
    )


def window_kernel(seq, blocks, lengths, q_ref, k_ref, stat_ref, _, x_ref, att_ref, vec_ref, proj_w, *refs):
    prob_ref, normed_ref, rstd_ref, hid_ref, x_t, att_t, hid_t, out_w, sem = refs
    g = pl.program_id(0)

    @pl.when(g == 0)
    def _():
        start_all(out_weight_copies(proj_w, out_w, sem))

    probs_kernel(seq, lengths, q_ref, k_ref, stat_ref, prob_ref)

    @pl.when(g == 0)
    def _():
        wait_whole(out_w, sem)

    @pl.when(g < blocks)
    def _():
        x, attended = x_ref[...], att_ref[...]
        normed, rstd = norm_rows(x + dot(attended, out_w[...]) + vec_ref[2:3, :])
        normed_ref[...] = normed
        rstd_ref[...] = jnp.broadcast_to(rstd, rstd_ref.shape)
        hidden = normed * vec_ref[3:4, :] + vec_ref[4:5, :]
        hid_ref[...] = hidden.astype(bf16)
        x_t[...] = x.T.astype(bf16)
        att_t[...] = attended.astype(f32).T.astype(bf16)
        hid_t[...] = hidden.T.astype(bf16)


def window(seq, lengths, x, qkv, attended, stats, weights, vectors, prob, deps=()):
    count = x.shape[0]
    _, _, rows = stats.shape
    blocks = count // BLOCK
    block = lambda s: jnp.minimum(s, blocks - 1)
    token = lambda width: pl.BlockSpec((BLOCK, width), lambda s: (block(s), 0))
    turned = pl.BlockSpec((D, BLOCK), lambda s: (0, block(s)))
    specs, out = probs_specs(seq, rows)
    return call(
        functools.partial(window_kernel, seq, blocks),
        (lengths, qkv, qkv, stats, prob, x, attended, vectors, weights),
        deps,
        grid=(H // 2,),
        in_specs=specs + [ANY, token(D), token(D), whole(16, D), ANY],
        out_specs=[out, token(D), token(128), token(D)] + [turned] * 3,
        out_shape=[
            jax.ShapeDtypeStruct(prob.shape, bf16),
            jax.ShapeDtypeStruct((count, D), f32),
            jax.ShapeDtypeStruct((count, 128), f32),
            jax.ShapeDtypeStruct((count, D), bf16),
        ]
        + [jax.ShapeDtypeStruct((D, count), bf16)] * 3,
        input_output_aliases={4: 0},
        scratch_shapes=[pltpu.VMEM((D, D), bf16), pltpu.SemaphoreType.DMA],
        compiler_params=pltpu.CompilerParams(vmem_limit_bytes=VMEM),
        cost_estimate=pl.CostEstimate(flops=14_000_000_000, bytes_accessed=MIB, transcendentals=0),
        name="window",
    )


def ffn_kernel(meta, pieces, blocks, place, normed_ref, rstd_ref, hid_ref, cot_ref, vec_ref, b1_ref, proj_w, *refs):
    piece_refs = refs[:pieces]
    (out_ref, fb_ref, ab_ref, ib_ref, branch_ref, small_ref, db1_ref, keep, send) = refs[pieces : pieces + 9]
    (out_w, inner_w, down_w, act, down_back, sem, wsem) = refs[pieces + 9 :]
    step = pl.program_id(0)

    @pl.when(step == 0)
    def _():
        start_all(inner_blocks(place, zip(piece_refs, meta), inner_w, sem.at[0]))
        start_all(down_blocks(place, zip(piece_refs, meta), down_w, sem.at[1]))
        start_all(out_weight_copies(proj_w, out_w, sem.at[2]))
        small_ref[...] = jnp.zeros_like(small_ref)
        db1_ref[...] = jnp.zeros_like(db1_ref)
        wait_whole(inner_w, sem.at[0])
        wait_whole(down_w, sem.at[1])
        wait_whole(out_w, sem.at[2])

    @pl.when(step < blocks)
    def _():
        rows = aligned(step * BLOCK, BLOCK, BLOCK)
        first_gain, first_shift = vec_ref[3:4, :], vec_ref[4:5, :]
        second_gain, second_shift = vec_ref[6:7, :], vec_ref[7:8, :]
        first_normed = normed_ref[...]
        hidden_low = hid_ref[...]
        total = first_normed * first_gain + first_shift + vec_ref[5:6, :]
        slopes = []
        for c in range(FF // WIDTH):
            cols = pl.ds(c * WIDTH, WIDTH)
            u = dot(hidden_low, inner_w[:, cols]) + b1_ref[:, cols]
            below, bell = gelu_parts(u)
            active = (u * below).astype(bf16)
            act[rows, cols] = active
            slopes.append(below + u * bell * GAUSS_DENSITY)
            total = total + dot(active, down_w[cols, :])
        second_normed, second_rstd = norm_rows(total)
        out_ref[...] = second_normed * second_gain + second_shift
        cot = cot_ref[...]
        second_back = norm_back(cot, second_normed, second_rstd, second_gain)
        back_low = second_back.astype(bf16)
        down_back[rows, :] = back_low
        hidden_back = second_back
        for c in range(FF // WIDTH):
            cols = pl.ds(c * WIDTH, WIDTH)
            ib = (dot_t(back_low, down_w[cols, :]) * slopes[c]).astype(bf16)
            ib_ref[:, cols] = ib
            db1_ref[:, cols] += fold_rows(ib.astype(f32))
            hidden_back = hidden_back + dot_t(ib, inner_w[:, cols])
        first_back = norm_back(hidden_back, first_normed, rstd_ref[:, 0:1], first_gain)
        fb_ref[...] = first_back
        branch_low = first_back.astype(bf16)
        branch_ref[...] = branch_low
        ab_ref[...] = dot_t(branch_low, out_w[...]).astype(bf16)
        sums = (
            branch_low.astype(f32),
            hidden_back * first_normed,
            hidden_back,
            back_low.astype(f32),
            cot * second_normed,
            cot,
        )
        for i, v in enumerate(sums):
            small_ref[i] += fold_rows(v)

    @pl.when(step >= blocks)
    def _():
        chunk = step - blocks
        width = FF // DOWN_STEPS
        rows = aligned(chunk * width, width, 128)
        down_w[rows, :] = dot_l(act[:, rows], down_back[...]).astype(bf16)
        for i in range(CHIPS // DOWN_STEPS):
            chip = chunk * (CHIPS // DOWN_STEPS) + i
            for half in range(2):
                at = (chip * 2 + half) * (2 * PAIR_ROWS)
                pairs = [
                    (down_w.at[aligned(at + k * PAIR_ROWS, PAIR_ROWS, 16)], pl.ds(k * D, D)) for k in range(2)
                ]
                hand_over(place, chip, half, keep, send, pairs, wsem)

    @pl.when(step == blocks + DOWN_STEPS - 1)
    def _():
        wait_whole(keep, wsem)
        wait_whole(send, wsem)


def feed_forward(place, normed, rstd, hid, cotangent, vectors, inner_bias, weights, pieces, meta):
    count = normed.shape[0]
    blocks = count // BLOCK
    token = lambda width: pl.BlockSpec((BLOCK, width), lambda s: (jnp.minimum(s, blocks - 1), 0))
    return pl.pallas_call(
        functools.partial(ffn_kernel, meta, len(pieces), blocks),
        grid=(blocks + DOWN_STEPS,),
        in_specs=[SMEM, token(D), token(128), token(D), token(D), whole(16, D), whole(1, FF), ANY]
        + [ANY] * len(pieces),
        out_specs=[token(D), token(D), token(D), token(FF), token(D), whole(6, 8, D), whole(8, FF), ANY, ANY],
        out_shape=[
            jax.ShapeDtypeStruct((count, D), f32),
            jax.ShapeDtypeStruct((count, D), f32),
            jax.ShapeDtypeStruct((count, D), bf16),
            jax.ShapeDtypeStruct((count, FF), bf16),
            jax.ShapeDtypeStruct((count, D), bf16),
            jax.ShapeDtypeStruct((6, 8, D), f32),
            jax.ShapeDtypeStruct((8, FF), f32),
            jax.ShapeDtypeStruct((CHIPS, PAIR_ROWS, DOWN_BLOCK), bf16),
            jax.ShapeDtypeStruct((CHIPS, PAIR_ROWS, DOWN_BLOCK), bf16),
        ],
        scratch_shapes=[
            pltpu.VMEM((D, D), bf16),
            pltpu.VMEM((D, FF), bf16),
            pltpu.VMEM((FF, D), bf16),
            pltpu.VMEM((count, FF), bf16),
            pltpu.VMEM((count, D), bf16),
            pltpu.SemaphoreType.DMA((3,)),
            pltpu.SemaphoreType.DMA,
        ],
        compiler_params=pltpu.CompilerParams(vmem_limit_bytes=ALL_VMEM),
        cost_estimate=pl.CostEstimate(flops=52_000_000_000, bytes_accessed=40 * MIB, transcendentals=0),
        name="feed_forward",
    )(place, normed, rstd, hid, cotangent, vectors, inner_bias, weights, *pieces)


def inner_grads_kernel(hid_t, ib_ref, place, att_in, branch_in, keep, send, att_t, branch, out_g, inner_g, sem, wsem):
    step = pl.program_id(0)
    steps = FF // D
    later = [pltpu.make_async_copy(att_in, att_t, sem.at[0]), pltpu.make_async_copy(branch_in, branch, sem.at[1])]

    @pl.when(step == 0)
    def _():
        start_all(later)

    def give(grads, half, width, lane):
        for chip in range(CHIPS):
            block = grads.at[pl.ds(chip * PAIR_ROWS, PAIR_ROWS), pl.ds(half * width, width)]
            hand_over(place, chip, half, keep, send, [(block, pl.ds(lane, width))], wsem)

    @pl.when(step < steps)
    def _():
        cols = aligned(step * D, D, 128)
        inner_g[:, cols] = dot(hid_t[...], ib_ref[...]).astype(bf16)
        for half in range(2):

            @pl.when(step == (half + 1) * (steps // 2) - 1)
            def _():
                give(inner_g, half, INNER_HALF, OUT_HALF)

    @pl.when(step == steps)
    def _():
        for copy in later:
            copy.wait()
        out_g[...] = dot(att_t[...], branch[...]).astype(bf16)
        for half in range(2):
            give(out_g, half, OUT_HALF, 0)
        wait_whole(keep, wsem)
        wait_whole(send, wsem)


def inner_grads(place, hid_t, inner_back, att_t, branch):
    count = hid_t.shape[1]
    steps = FF // D
    return pl.pallas_call(
        inner_grads_kernel,
        grid=(steps + 1,),
        in_specs=[
            whole(D, count),
            pl.BlockSpec((count, D), lambda s: (0, jnp.minimum(s, steps - 1))),
            SMEM,
            ANY,
            ANY,
        ],
        out_specs=[ANY, ANY],
        out_shape=[jax.ShapeDtypeStruct((CHIPS, PAIR_ROWS, INNER_BLOCK), bf16)] * 2,
        scratch_shapes=[
            pltpu.VMEM((D, count), bf16),
            pltpu.VMEM((count, D), bf16),
            pltpu.VMEM((D, D), bf16),
            pltpu.VMEM((D, FF), bf16),
            pltpu.SemaphoreType.DMA((2,)),
            pltpu.SemaphoreType.DMA,
        ],
        compiler_params=pltpu.CompilerParams(vmem_limit_bytes=ALL_VMEM),
        cost_estimate=pl.CostEstimate(flops=4_000_000_000, bytes_accessed=MIB, transcendentals=0),
        name="inner_grads",
    )(hid_t, inner_back, place, att_t, branch)


def attend_back_pair(queries, keys, values, upstream, prob_ref, dq_ref, dk_ref, dv_ref):
    lows, backs = [], []
    masks = lane_masks()
    for i, mask in enumerate(masks):
        low = prob_ref[i]
        weight = low.astype(f32)
        weight_back = dot_t(values * mask, upstream)
        mean = jnp.sum(weight * weight_back, axis=0, keepdims=True)
        lows.append(low)
        backs.append((weight * (weight_back - mean)).astype(bf16))
    each = lambda v: jnp.concatenate([v * mask for mask in masks], axis=0)
    dv_ref[...] = dot(jnp.concatenate(lows, axis=1), each(upstream)).astype(bf16)
    dk_ref[...] = (dot(jnp.concatenate(backs, axis=1), each(queries)) * 0.125).astype(bf16)
    dq_ref[...] = (dot_l(jnp.concatenate(backs, axis=0), each(keys)) * 0.125).astype(bf16)


def attend_back_kernel(q_ref, k_ref, v_ref, up_ref, prob_ref, *refs):
    attend_back_pair(q_ref[...], k_ref[...], v_ref[...], up_ref[...], prob_ref, *refs[-3:])


def pair_specs(rows, first, last):
    pairs = H // 2
    pair = lambda s: jnp.minimum(first + s, last)
    lane = lambda kind: pl.BlockSpec((rows, 128), lambda s: (pair(s) // pairs, kind * pairs + pair(s) % pairs))
    return [lane(0), lane(1), lane(2), lane(0), pl.BlockSpec((2, rows, rows), lambda s: (pair(s), 0, 0))]


def attend_back(first, count, qkv, back, prob, grads=(), deps=()):
    specs = pair_specs(prob.shape[1], first, first + count - 1)
    return call(
        attend_back_kernel,
        (qkv, qkv, qkv, back, prob, *grads),
        deps,
        grid=(count,),
        in_specs=specs + [ANY] * len(grads),
        out_specs=[specs[0]] * 3,
        out_shape=[jax.ShapeDtypeStruct(back.shape, bf16)] * 3,
        input_output_aliases={5 + i: i for i in range(len(grads))},
        compiler_params=pltpu.CompilerParams(vmem_limit_bytes=ALL_VMEM),
        cost_estimate=pl.CostEstimate(flops=3_000_000_000, bytes_accessed=MIB, transcendentals=0),
        name=f"attend_back_{first}",
    )


def proj_grads_kernel(place, turned, small_ref, db1_ref, dq, dk, dv, keep, send, grads, packed, bias, sem, wsem):
    step = pl.program_id(0)
    copies = [pltpu.make_async_copy(v, grads.at[i], sem.at[i]) for i, v in enumerate((dq, dk, dv))]

    @pl.when(step == 0)
    def _():
        start_all([copies[1], copies[2], copies[0]])

    for turn, which in enumerate((1, 2, 0)):

        @pl.when(step == turn)
        def _():
            copies[which].wait()
            g = dot(turned[...], grads[which]).astype(bf16)
            if which == 1:
                packed[:, D:QKV_HALF] = g[:, : D // 2]
                packed[:, QKV_BLOCK : QKV_BLOCK + D // 2] = g[:, D // 2 :]
            else:
                at = 0 if which == 0 else QKV_BLOCK + D // 2
                packed[:, at : at + D] = g
                bias[which // 2] = fold_rows(grads[which].astype(f32))

    @pl.when(step == 0)
    def _():
        owner = lax.broadcasted_iota(jnp.int32, (SLABS, FF), 1) // (4 * SLAB)
        one = lax.broadcasted_iota(jnp.int32, (SLABS, FF), 0)
        mine = jnp.where(owner == one, jnp.sum(db1_ref[...], axis=0, keepdims=True), 0.0)
        place_of = lax.broadcasted_iota(jnp.int32, (FF, 128), 0) % (4 * SLAB)
        pick = place_of == lax.broadcasted_iota(jnp.int32, (FF, 128), 1)
        table = dot(mine.astype(bf16), pick.astype(bf16))
        spread = jnp.broadcast_to(table[:, None, :], (SLABS, SLAB, 128)).reshape(D, 128)
        packed[:, QKV_BLOCK + QKV_HALF :] = spread.astype(bf16)

    def give(half):
        for chip in range(CHIPS):
            block = packed.at[pl.ds(chip * PAIR_ROWS, PAIR_ROWS), pl.ds(half * QKV_BLOCK, QKV_BLOCK)]
            hand_over(place, chip, half, keep, send, [(block, pl.ds(0, QKV_BLOCK))], wsem)

    @pl.when(step == 1)
    def _():
        give(1)

    @pl.when(step == 2)
    def _():
        rows_of = [bias[...], small_ref[...], jnp.zeros((120, 8, D), f32)]
        packed[:, QKV_HALF:QKV_BLOCK] = jnp.sum(jnp.concatenate(rows_of, axis=0), axis=1).T.astype(bf16)
        give(0)
        wait_whole(keep, wsem)
        wait_whole(send, wsem)


def proj_grads(place, turned, small, inner_bias_grad, grads, deps=()):
    count = turned.shape[1]
    return call(
        proj_grads_kernel,
        (place, turned, small, inner_bias_grad, *grads),
        deps,
        grid=(3,),
        in_specs=[SMEM, whole(D, count), whole(6, 8, D), whole(8, FF), ANY, ANY, ANY],
        out_specs=[ANY, ANY],
        out_shape=[jax.ShapeDtypeStruct((CHIPS, PAIR_ROWS, QKV_BLOCK), bf16)] * 2,
        scratch_shapes=[
            pltpu.VMEM((3, count, D), bf16),
            pltpu.VMEM((D, 2 * QKV_BLOCK), bf16),
            pltpu.VMEM((2, 8, D), f32),
            pltpu.SemaphoreType.DMA((3,)),
            pltpu.SemaphoreType.DMA,
        ],
        compiler_params=pltpu.CompilerParams(vmem_limit_bytes=ALL_VMEM),
        cost_estimate=pl.CostEstimate(flops=4_000_000_000, bytes_accessed=MIB, transcendentals=0),
        name="proj_grads",
    )


def input_back_kernel(fb_ref, dq_ref, dk_ref, dv_ref, w_ref, *refs):
    half = D // 2
    total = fb_ref[...] + dot_t(dq_ref[...], w_ref[:, 0:D])
    total = total + dot_t(dk_ref[:, :half], w_ref[:, D:QKV_HALF])
    total = total + dot_t(dk_ref[:, half:], w_ref[:, PROJ_BLOCK : PROJ_BLOCK + half])
    out_ref, small_ref = refs[-2:]
    small_ref[...] = total[0:16, 0:128]
    out_ref[...] = total + dot_t(dv_ref[...], w_ref[:, PROJ_BLOCK + half : PROJ_BLOCK + QKV_HALF])


def input_back(first, blocks, first_back, grads, weights, given=(), deps=()):
    token = pl.BlockSpec((BLOCK, D), lambda s: (first + s, 0))
    return call(
        input_back_kernel,
        (first_back, *grads, weights, *given),
        deps,
        grid=(blocks,),
        in_specs=[token] * 4 + [whole(D, 2 * PROJ_BLOCK)] + [ANY] * len(given),
        out_specs=[token, whole(16, 128)],
        out_shape=[jax.ShapeDtypeStruct(first_back.shape, f32), jax.ShapeDtypeStruct((16, 128), f32)],
        input_output_aliases={5: 0} if given else {},
        compiler_params=pltpu.CompilerParams(vmem_limit_bytes=ALL_VMEM),
        cost_estimate=pl.CostEstimate(flops=10_000_000_000, bytes_accessed=MIB, transcendentals=0),
        name=f"input_back_{first}",
    )


def add_up_kernel(jobs, passed, place, *refs):
    refs[len(refs) - 1][...] = refs[0][0, 0:8, 0:128].astype(f32)
    first, out = 0, sum(count for count, _ in jobs) + passed
    for count, kind in jobs:
        terms = refs[first : first + count]
        first += count

        def total(slot):
            return sum((ref[slot].astype(f32) for ref in terms[1:]), terms[0][slot].astype(f32))

        slots = terms[0].shape[0]
        if kind == "upper":

            def one(i, _, total=total, ready=refs[out]):
                ready[i] = total(i).astype(bf16)
                return 0

            lax.fori_loop(0, slots, one, 0)
            out += 1
        elif kind == "both":
            half = slots // 2

            def one(i, _, total=total, ready=refs[out], rest=refs[out + 1], half=half):
                rest[i] = total(i)
                ready[i] = total(half + i).astype(bf16)
                return 0

            lax.fori_loop(0, half, one, 0)
            out += 2
        elif kind == "down":
            whole_sum = total(0)
            refs[out][0:PAIR_ROWS, :] = whole_sum[:, :D]
            refs[out][PAIR_ROWS:, :] = whole_sum[:, D:]
            out += 1
        else:
            whole_sum = total(0)
            low_core = place[1] == 0
            low, high = whole_sum[:SLAB], whole_sum[SLAB:]
            refs[out][...] = jnp.where(low_core, low, high)
            refs[out + 1][...] = jnp.where(low_core, high, low)
            out += 2


def add_up(place, *groups, passed=(), deps=(), vmem=ALL_VMEM):
    operands, specs, out_specs, shapes, jobs = [], [], [], [], []
    for size, terms, lazy in groups:
        _, rows, lanes = terms[0].shape
        half = size // 2
        kind = "upper" if lazy else "both" if size > 1 else "down" if lanes == DOWN_BLOCK else "halves"
        operands += terms
        take = (half, 1) if kind == "upper" else (size, 0)
        specs += [pl.BlockSpec((take[0], rows, lanes), lambda s, at=take[1]: (at, 0, 0))] * len(terms)
        if size > 1:
            kinds = [bf16] if kind == "upper" else [bf16, f32]
            out_specs += [whole(half, rows, lanes)] * len(kinds)
            shapes += [jax.ShapeDtypeStruct((half, rows, lanes), dtype) for dtype in kinds]
        else:
            ends = [(2 * PAIR_ROWS, D)] if kind == "down" else [(SLAB, lanes)] * 2
            out_specs += [whole(*end) for end in ends]
            shapes += [jax.ShapeDtypeStruct(end, f32) for end in ends]
        jobs.append((len(terms), kind))
    return call(
        lambda *refs: add_up_kernel(jobs, len(passed), refs[0], *refs[1:]),
        [place] + operands + list(passed),
        deps,
        grid=(1,),
        in_specs=[SMEM] + specs + [ANY] * len(passed),
        out_specs=out_specs + [ANY] * len(passed) + [whole(8, 128)],
        out_shape=shapes
        + [jax.ShapeDtypeStruct(v.shape, v.dtype) for v in passed]
        + [jax.ShapeDtypeStruct((8, 128), f32)],
        input_output_aliases={1 + len(operands) + i: len(shapes) + i for i in range(len(passed))},
        compiler_params=pltpu.CompilerParams(vmem_limit_bytes=vmem),
        cost_estimate=pl.CostEstimate(flops=1000, bytes_accessed=1000, transcendentals=0),
        name="add_up",
    )


def gate(value, deps, vmem=ALL_VMEM):
    return call(
        lambda value_ref, out_ref: None,
        [value],
        deps,
        grid=(1,),
        in_specs=[ANY],
        out_specs=ANY,
        out_shape=jax.ShapeDtypeStruct(value.shape, value.dtype),
        input_output_aliases={0: 0},
        compiler_params=pltpu.CompilerParams(vmem_limit_bytes=vmem),
        cost_estimate=pl.CostEstimate(flops=1000, bytes_accessed=1000, transcendentals=0),
        name="gate",
    )


def finish_inner_kernel(place, mine, other, out_g, inner_g, small):
    low_core = place[1] == 0
    low = jnp.where(low_core, mine[...], other[...])
    high = jnp.where(low_core, other[...], mine[...])
    out_g[:, :OUT_HALF], out_g[:, OUT_HALF:] = low[:, :OUT_HALF], high[:, :OUT_HALF]
    inner_g[:, :INNER_HALF], inner_g[:, INNER_HALF:] = low[:, OUT_HALF:], high[:, OUT_HALF:]
    small[...] = low[0:8, 0:128]


def finish_proj_kernel(place, mine, other, dq, dk, dv, bias, *vectors):
    low_core = place[1] == 0
    low = jnp.where(low_core, mine[...], other[...])
    high = jnp.where(low_core, other[...], mine[...])
    half = D // 2
    dq[...] = low[:, :D]
    dk[:, :half], dk[:, half:] = low[:, D:QKV_HALF], high[:, :half]
    dv[...] = high[:, half:QKV_HALF]
    bias[...] = high[0, QKV_HALF : QKV_HALF + 4 * SLAB]
    rows = low[:, QKV_HALF:].T
    for i, out in enumerate(vectors):
        out[...] = rows[i, 0:SLAB]


def finish(kernel, place, mine, other, shapes, name, deps=()):
    at = lambda shape: pl.BlockSpec(shape, lambda s: (0,) * len(shape))
    return call(
        kernel,
        (place, mine, other),
        deps,
        grid=(1,),
        in_specs=[SMEM, at(mine.shape), at(mine.shape)],
        out_specs=[at(shape) for shape in shapes],
        out_shape=[jax.ShapeDtypeStruct(shape, f32) for shape in shapes],
        compiler_params=pltpu.CompilerParams(vmem_limit_bytes=LITTLE),
        cost_estimate=pl.CostEstimate(flops=1000, bytes_accessed=1000, transcendentals=0),
        name=name,
    )


def finish_inner(place, mine, other):
    return finish(finish_inner_kernel, place, mine, other, [(SLAB, D), (SLAB, FF), (8, 128)], "finish_inner")


def finish_proj(place, mine, other, deps=()):
    shapes = [(SLAB, D)] * 3 + [(4 * SLAB,)] + [(SLAB,)] * 8
    return finish(finish_proj_kernel, place, mine, other, shapes, "finish_proj", deps)


AXES = ("dp", "fsdp")


CORE = (1, 1)
ALONG_Z_FIRST, ALONG_Z_THEN, ALONG_Z_BOTH, ALONG_XY_FIRST, ALONG_XY_THEN = (16, 8), (8, 16), (24, 24), (2, 4), (4, 2)
FAST_SHAPE = {"dp": 4, "fsdp": 8}


def move(v, masks):
    return lax.ppermute(v, AXES, [(i, i ^ masks[i & 1]) for i in range(SLABS)])


SUM_STEPS = (ALONG_XY_THEN, ALONG_XY_FIRST, ALONG_Z_THEN, ALONG_Z_FIRST)


def after(*values):
    return lax.optimization_barrier(values)


class Sums:
    def __init__(self, keep, got):
        self.size, self.terms, self.step = CHIPS, [keep, got], 0

    def send(self, outs, lazy):
        ready = outs.pop(0)
        if not lazy:
            self.terms = [outs.pop(0)]
        self.size //= 2
        self.terms = self.terms + [move(ready, SUM_STEPS[self.step])]
        self.step += 1


def add_and_send(place, *groups, lazy=False, **options):
    outs = list(add_up(place, *[(g.size, g.terms, lazy) for g in groups], **options))
    for g in groups:
        if g.size > 1:
            g.send(outs, lazy)
    return outs


def fast_blocks(shards, core):
    (qw, kw, vw, ow, qb, vb, ob, fg, fs, iw, ib, dw, db, sg, ss) = shards
    vectors = jnp.pad(jnp.stack([qb, vb, ob, fg, fs, db, sg, ss], axis=1), ((0, 0), (0, 120)))
    inner_bias = jnp.pad(ib.reshape(1, 4 * SLAB), ((0, SLAB - 1), (0, 128 - 4 * SLAB)))
    half = D // 2
    halves = [
        jnp.concatenate([qw, kw[:, :half], vectors, ow[:, :half], iw[:, :INNER_HALF]], axis=1),
        jnp.concatenate([kw[:, half:], vw, inner_bias, ow[:, half:], iw[:, INNER_HALF:]], axis=1),
    ]
    low_core = core == 0
    own = jnp.where(low_core, halves[0], halves[1])
    other = move(jnp.where(low_core, halves[1], halves[0]), CORE)
    rows = jnp.concatenate([jnp.where(low_core, own, other), jnp.where(low_core, other, own)], axis=0)
    return rows[:, :PROJ_BLOCK], rows[:, PROJ_BLOCK:], jnp.concatenate([dw[:PAIR_ROWS], dw[PAIR_ROWS:]], axis=1)


def gather_plain(shards):
    (qw, kw, vw, ow, qb, vb, ob, fg, fs, iw, ib, dw, db, sg, ss) = [
        lax.all_gather(v, AXES, axis=0, tiled=True) for v in shards
    ]
    vectors = jnp.pad(jnp.stack([qb, vb, ob, fg, fs, db, sg, ss], axis=1), ((0, 0), (0, 120)))
    inner_bias = jnp.pad(ib.reshape(SLABS, 1, 4 * SLAB), ((0, 0), (0, SLAB - 1), (0, 128 - 4 * SLAB))).reshape(D, 128)
    half = D // 2
    chips = lambda v: v.reshape(CHIPS, PAIR_ROWS, -1)
    down = dw.reshape(CHIPS, 2, 2, PAIR_ROWS, D)
    first = [
        chips(jnp.concatenate([qw, kw[:, :half], vectors, ow[:, :half]], axis=1)),
        chips(jnp.concatenate([kw[:, half:], vw, inner_bias, ow[:, half:]], axis=1)),
    ]
    second = [
        jnp.concatenate([chips(iw[:, c * INNER_HALF : (c + 1) * INNER_HALF]), down[:, c, 0], down[:, c, 1]], axis=2)
        for c in range(2)
    ]
    slots = lambda halves: [v[np.array(SLOT_CHIPS[c])] for c, v in enumerate(halves)]
    return slots(first), slots(second)


def local(fast, inputs, lengths, *rest):
    shards, cotangent = rest[:15], rest[15]
    both = lambda v, came: jnp.concatenate([v, came])
    if fast:
        linear = lax.axis_index(AXES)
        core = linear & 1
        place = jnp.stack([linear >> 1, core]).astype(jnp.int32)
        first, inner, down = fast_blocks(shards, core)
        first = first[None]
        first = both(first, move(first, ALONG_Z_FIRST))
        first, second = after(first, jnp.concatenate([inner, down], axis=1)[None])
        second = jnp.concatenate([second] + [move(second, steps) for steps in (ALONG_Z_FIRST, ALONG_Z_THEN, ALONG_Z_BOTH)])
        first = both(first, move(first, ALONG_Z_THEN))
        first_then, first_core = move(first, ALONG_XY_THEN), move(first, CORE)
        first_came = move(first, ALONG_XY_FIRST)
        first_last, came_core = move(first_came, ALONG_XY_THEN), move(first_came, CORE)
        first_then, first_last, second = after(first_then, first_last, second)
        first = [first, first_came, first_then, first_last]
        first += [first_core, came_core, move(first_then, CORE), move(first_last, CORE)]
        second_came, second_then, second_core = move(second, ALONG_XY_FIRST), move(second, ALONG_XY_THEN), move(second, CORE)
        meta = tuple((at, other) for other in (False, True) for at in range(0, CHIPS, 4))
    else:
        place = jnp.zeros((2,), jnp.int32)
        first, second = gather_plain(shards)
        meta = ((0, False), (0, True))
    qkv, attended, stats, weights, vectors = attend(place, lengths, inputs, first, meta)
    prob = probs(0, lengths, qkv, stats)
    if fast:
        second_came, second_then, prob = after(second_came, second_then, prob)
        second_last, came_core, then_core = move(second_came, ALONG_XY_THEN), move(second_came, CORE), move(second_then, CORE)
    prob, normed, rstd, hid, inputs_t, attended_t, hid_t = window(
        1, lengths, inputs, qkv, attended, stats, weights, vectors, prob
    )
    bias_at = PROJ_BLOCK + QKV_HALF
    inner_bias = weights[::SLAB, bias_at : bias_at + 4 * SLAB].reshape(1, FF).astype(f32)
    if fast:
        second_last, normed, inner_bias = after(second_last, normed, inner_bias)
        second = [second, second_came, second_then, second_last]
        second += [second_core, came_core, then_core, move(second_last, CORE)]
    output, first_back, back, inner_back, branch, small, db1, down_keep, down_send = feed_forward(
        place, normed, rstd, hid, cotangent, vectors, inner_bias, weights, second, meta
    )
    inner_keep, inner_send = inner_grads(place, hid_t, inner_back, attended_t, branch)
    pairs = lengths.shape[0] * (H // 2)
    third = pairs // 3
    deps = []
    if fast:
        down = Sums(down_keep, move(down_send, CORE))
        inner_send, *deps = add_and_send(place, down, lazy=True, passed=[inner_send], deps=[inner_keep])
        inner = Sums(inner_keep, move(inner_send, CORE))
    grads = attend_back(0, third, qkv, back, prob, deps=deps)
    if fast:
        deps = add_and_send(place, inner, lazy=True, deps=grads[:1])
    grads = attend_back(third, third, qkv, back, prob, grads, deps=deps)
    if fast:
        deps = add_and_send(place, down, lazy=True, deps=grads[:1])
    grads = attend_back(2 * third, pairs - 2 * third, qkv, back, prob, grads, deps=deps)
    if fast:
        deps = add_and_send(place, inner, down, lazy=True, deps=grads[:1])
    proj_keep, proj_send = proj_grads(place, inputs_t, small, db1, grads, deps=deps)
    blocks = inputs.shape[0] // BLOCK
    if fast:
        proj_send = gate(proj_send, [inner.terms[-1], down.terms[-1]])
        proj = Sums(proj_keep, move(proj_send, CORE))
        deps = add_and_send(place, inner, down, deps=[proj_keep])
        deps = add_and_send(place, proj, lazy=True, deps=deps)
        grad_input, came = input_back(0, blocks, first_back, grads, weights, deps=deps)
        proj.terms[-1] = gate(proj.terms[-1], [inner.terms[-1], down.terms[-1], came], MIB)
        deps = add_and_send(place, proj, vmem=LITTLE)
        down_grad, *deps = add_and_send(place, inner, down, deps=deps, vmem=LITTLE)
        proj.terms[-1] = gate(proj.terms[-1], [inner.terms[-1]], MIB)
        deps = add_and_send(place, proj, deps=deps, vmem=LITTLE)
        mine, other, *deps = add_and_send(place, proj, inner, deps=deps, vmem=LITTLE)
        out_grad, inner_grad, *deps = finish_inner(place, mine, move(other, CORE))
        mine, other, _ = add_and_send(place, proj, deps=deps, vmem=LITTLE)
        *square, bias, v0, v1, v2, v3, v4, v5, v6, v7 = finish_proj(place, mine, move(other, CORE))
        vectors = [v0, v1, v2, v3, v4, v5, v6, v7]
    else:
        grad_input, _ = input_back(0, blocks, first_back, grads, weights)
        shard = lambda *v: lax.psum_scatter(jnp.concatenate(v, axis=1), AXES, scatter_dimension=0, tiled=True)
        by_chip = lambda pair: [v[np.argsort(np.array(SLOT_CHIPS[c]))].astype(f32) for c, v in enumerate(pair)]
        low, high = (v.reshape(D, -1) for v in by_chip((inner_keep, inner_send)))
        out_grad, inner_grad = shard(low[:, :OUT_HALF], high[:, :OUT_HALF]), shard(low[:, OUT_HALF:], high[:, OUT_HALF:])
        parts = [jnp.stack([v[:, :, :D], v[:, :, D:]], axis=1) for v in by_chip((down_keep, down_send))]
        down_grad = shard(jnp.stack(parts, axis=1).reshape(FF, D))
        low, high = (v.reshape(D, -1) for v in by_chip((proj_keep, proj_send)))
        half = D // 2
        square = shard(low[:, :D]), shard(low[:, D:QKV_HALF], high[:, :half]), shard(high[:, half:QKV_HALF])
        columns = shard(low[:, QKV_HALF:])
        vectors = [columns[:, i] for i in range(8)]
        bias = shard(high[::SLAB, QKV_HALF : QKV_HALF + 4 * SLAB].reshape(FF, 1))[:, 0]
    return (
        output,
        grad_input,
        *square,
        out_grad,
        *vectors[:5],
        inner_grad,
        bias,
        down_grad,
        *vectors[5:],
    )


def solution(mesh):
    rows, flat = P(AXES, None), P(AXES)
    params = (rows,) * 4 + (flat,) * 5 + (rows, flat, rows, flat, flat, flat)
    return jax.shard_map(
        functools.partial(local, dict(mesh.shape) == FAST_SHAPE),
        mesh=mesh,
        in_specs=(rows, flat) + params + (rows,),
        out_specs=(rows, rows) + params,
        check_vma=False,
    )
```

```python
import functools
import math

import jax
import jax.numpy as jnp
import numpy as np
from jax import lax
from jax.experimental import pallas as pl
from jax.experimental.pallas import tpu as pltpu
from jax.sharding import PartitionSpec as P

D = 768
H = 12
DH = 64
FF = 3072
SLABS = 32
SLAB = D // SLABS
CHIPS = SLABS // 2
PAIR_ROWS = 2 * SLAB
NORM_EPSILON = 1e-12
MASKED_SCORE = -1000000000.0
GAUSS_DENSITY = 0.3989422804014327
LOG2E = 1.4426950408889634
MIB = 1 << 20
VMEM = 62 * MIB
ALL_VMEM = 127 * MIB // 2
LITTLE = 16 * MIB

QKV_HALF = 3 * D // 2
QKV_BLOCK = QKV_HALF + 128
OUT_HALF = D // 2
PROJ_BLOCK = QKV_BLOCK + OUT_HALF
INNER_HALF = FF // 2
INNER_BLOCK = OUT_HALF + INNER_HALF
DOWN_BLOCK = 2 * D

SLOT_BITS = ((8, 4, 1, 2), (4, 8, 2, 1))
SLOT_CHIPS = tuple(
    tuple(sum(bit for i, bit in enumerate(bits) if slot >> i & 1) for slot in range(CHIPS)) for bits in SLOT_BITS
)

bf16 = jnp.bfloat16
f32 = jnp.float32
ANY = pl.BlockSpec(memory_space=pl.ANY)
SMEM = pl.BlockSpec(memory_space=pltpu.SMEM)


def dot(a, b):
    return lax.dot_general(a, b, (((1,), (0,)), ((), ())), preferred_element_type=f32)


def dot_t(a, b):
    return lax.dot_general(a, b, (((1,), (1,)), ((), ())), preferred_element_type=f32)


def dot_l(a, b):
    return lax.dot_general(a, b, (((0,), (0,)), ((), ())), preferred_element_type=f32)


def call(kernel, operands, deps, in_specs, **options):
    count = len(operands)

    def body(*refs):
        kernel(*refs[:count], *refs[count + len(deps) :])

    in_specs = in_specs + [whole(8, 128) if v.shape == (8, 128) else ANY for v in deps]
    return pl.pallas_call(body, in_specs=in_specs, **options)(*operands, *deps)


def aligned(start, size, unit):
    return pl.ds(pl.multiple_of(start, unit), size)


def chip_of(slot, half):
    return jnp.where(half == 0, SLOT_CHIPS[0][slot], SLOT_CHIPS[1][slot])


def slot_of(chip, half):
    bits = SLOT_BITS[half]
    return sum(jnp.where((chip & bit) != 0, 1 << i, 0) for i, bit in enumerate(bits))


def blocks_of(place, pieces):
    for ref, (first, other) in pieces:
        half = 1 - place[1] if other else place[1]
        for i in range(ref.shape[0]):
            yield ref, i, place[0] ^ chip_of(first + i, half), half


def proj_blocks(place, pieces, weights, sem):
    for ref, i, chip, half in blocks_of(place, pieces):
        rows = aligned(chip * PAIR_ROWS, PAIR_ROWS, 16)
        yield pltpu.make_async_copy(ref.at[i], weights.at[rows, aligned(half * PROJ_BLOCK, PROJ_BLOCK, 128)], sem)


def inner_blocks(place, pieces, inner_w, sem):
    for ref, i, chip, half in blocks_of(place, pieces):
        rows = aligned(chip * PAIR_ROWS, PAIR_ROWS, 16)
        yield pltpu.make_async_copy(
            ref.at[i, :, pl.ds(0, INNER_HALF)],
            inner_w.at[rows, aligned(half * INNER_HALF, INNER_HALF, 128)],
            sem,
        )


def down_blocks(place, pieces, down_w, sem):
    for ref, i, chip, half in blocks_of(place, pieces):
        for k in range(2):
            at = (chip * 2 + half) * (2 * PAIR_ROWS) + k * PAIR_ROWS
            yield pltpu.make_async_copy(
                ref.at[i, :, pl.ds(INNER_HALF + k * D, D)], down_w.at[aligned(at, PAIR_ROWS, 16), :], sem
            )


def start_all(copies):
    for c in copies:
        c.start()


def whole(*shape):
    return pl.BlockSpec(shape, lambda *s: (0,) * len(shape))


def fold_rows(v):
    return jnp.sum(v.reshape(v.shape[0] // 8, 8, v.shape[1]), axis=0)


def hand_over(place, chip, half, keep, send, pairs, sem):
    slot = slot_of(chip ^ place[0], half)
    for mine, out in ((True, keep), (False, send)):

        @pl.when((place[1] == half) == mine)
        def _():
            for source, lanes in pairs:
                pltpu.make_async_copy(source, out.at[slot, :, lanes], sem).start()


def wait_whole(ref, sem):
    pltpu.make_async_copy(ref, ref, sem).wait()


def lane_masks():
    low = (lax.broadcasted_iota(jnp.int32, (1, 128), 1) < DH).astype(f32)
    return low.astype(bf16), (1.0 - low).astype(bf16)


def attend_kernel(meta, n_pieces, place, lengths, x_ref, *refs):
    piece_refs = refs[:n_pieces]
    qkv_ref, att_ref, stat_ref, weights, vectors = refs[n_pieces : n_pieces + 5]
    sem = refs[-1]
    seq = pl.program_id(0)
    rows = x_ref.shape[0]

    @pl.when(seq == 0)
    def _():
        start_all(proj_blocks(place, zip(piece_refs, meta), weights, sem))
        wait_whole(weights, sem)
        small = weights[:, QKV_HALF:QKV_BLOCK].astype(f32)
        vectors[...] = small.T[0:16, :]

    lowered = x_ref[...].astype(bf16)
    first = dot(lowered, weights[:, 0:QKV_HALF])
    qkv_ref[:, 0:D] = (first[:, 0:D] + vectors[0:1, :]).astype(bf16)
    qkv_ref[:, D:QKV_HALF] = first[:, D:QKV_HALF].astype(bf16)
    second = dot(lowered, weights[:, PROJ_BLOCK : PROJ_BLOCK + QKV_HALF])
    qkv_ref[:, QKV_HALF : 2 * D] = second[:, 0 : D // 2].astype(bf16)
    qkv_ref[:, 2 * D :] = (second[:, D // 2 :] + vectors[1:2, :]).astype(bf16)

    low, high = lane_masks()
    lane = lax.broadcasted_iota(jnp.int32, (1, 128), 1)
    key_at = lax.broadcasted_iota(jnp.int32, (1, rows), 1)
    hidden_keys = jnp.where(key_at < lengths[seq], 0.0, MASKED_SCORE).astype(f32)
    chunk = 256
    ones = jnp.ones((rows, 128), bf16)
    stats = [jnp.zeros((chunk, 128), f32) for _ in range(rows // chunk)]
    for pair in range(H // 2):
        at = pair * 128
        keys = qkv_ref[:, D + at : D + at + 128]
        values = jnp.concatenate([qkv_ref[:, 2 * D + at : 2 * D + at + 128], ones], axis=1)
        keys_of = (keys * low, keys * high)
        for c in range(rows // chunk):
            span = pl.ds(c * chunk, chunk)
            queries = qkv_ref[span, at : at + 128]
            outs = []
            for i in range(2):
                scores = dot_t(queries, keys_of[i]) * (0.125 * LOG2E) + hidden_keys
                peak = jnp.max(scores, axis=-1, keepdims=True)
                weight = jnp.exp2(scores - peak).astype(bf16)
                both = dot(weight, values)
                total = both[:, 128:]
                outs.append(both[:, :128] / total)
                log_total = peak + jnp.log2(total)
                stats[c] = jnp.where(lane == 2 * pair + i, log_total, stats[c])
            att_ref[span, at : at + 128] = jnp.where(lane < DH, outs[0], outs[1]).astype(bf16)
    for c in range(rows // chunk):
        stat_ref[0, :, c * chunk : (c + 1) * chunk] = stats[c].T[0:16, :]


def attend(place, lengths, x, pieces, meta):
    rows = x.shape[0] // lengths.shape[0]
    seqs = lengths.shape[0]
    return pl.pallas_call(
        functools.partial(attend_kernel, meta, len(pieces)),
        grid=(seqs,),
        in_specs=[SMEM, SMEM, pl.BlockSpec((rows, D), lambda s: (s, 0))] + [ANY] * len(pieces),
        out_specs=[
            pl.BlockSpec((rows, 3 * D), lambda s: (s, 0)),
            pl.BlockSpec((rows, D), lambda s: (s, 0)),
            pl.BlockSpec((1, 16, rows), lambda s: (s, 0, 0)),
            whole(D, 2 * PROJ_BLOCK),
            whole(16, D),
        ],
        out_shape=[
            jax.ShapeDtypeStruct((seqs * rows, 3 * D), bf16),
            jax.ShapeDtypeStruct((seqs * rows, D), bf16),
            jax.ShapeDtypeStruct((seqs, 16, rows), f32),
            jax.ShapeDtypeStruct((D, 2 * PROJ_BLOCK), bf16),
            jax.ShapeDtypeStruct((16, D), f32),
        ],
        scratch_shapes=[pltpu.SemaphoreType.DMA],
        compiler_params=pltpu.CompilerParams(vmem_limit_bytes=VMEM),
        cost_estimate=pl.CostEstimate(flops=18_000_000_000, bytes_accessed=20 * MIB, transcendentals=0),
        name="attend",
    )(place, lengths, x, *pieces)


def gelu_parts(u):
    size = jnp.abs(u)
    bell = jnp.exp2(u * u * (-0.5 * LOG2E))
    t = 1.0 / (1.0 + (0.3275911 * math.sqrt(0.5)) * size)
    poly = t * (0.127414796 + t * (-0.142248368 + t * (0.7107068705 + t * (-0.7265760135 + t * 0.5307027145))))
    tail = poly * bell
    below = jnp.where(u < 0.0, tail, 1.0 - tail)
    return below, bell


def mean_rows(v):
    return jnp.sum(v, axis=-1, keepdims=True) * (1.0 / D)


def norm_rows(total):
    center = total - mean_rows(total)
    rstd = lax.rsqrt(mean_rows(center * center) + NORM_EPSILON)
    return center * rstd, rstd


def norm_back(upstream, normed, rstd, gain):
    scaled = upstream * gain
    return rstd * (scaled - mean_rows(scaled) - normed * mean_rows(scaled * normed))


BLOCK = 256
WIDTH = 768
DOWN_STEPS = 4


def out_weight_copies(proj_w, out_w, sem):
    for half in range(2):
        lanes = pl.ds(half * PROJ_BLOCK + QKV_BLOCK, OUT_HALF)
        yield pltpu.make_async_copy(proj_w.at[:, lanes], out_w.at[:, pl.ds(half * OUT_HALF, OUT_HALF)], sem)


def probs_kernel(seq, lengths, q_ref, k_ref, stat_ref, *refs):
    prob_ref = refs[-1]
    pair = pl.program_id(0)
    rows = q_ref.shape[0]
    chunk = 256
    key_at = lax.broadcasted_iota(jnp.int32, (rows, 1), 0)
    hidden_keys = jnp.where(key_at < lengths[seq], 0.0, MASKED_SCORE).astype(f32)
    for i, mask in enumerate(lane_masks()):
        own_keys = k_ref[...] * mask
        for c in range(rows // chunk):
            span = slice(c * chunk, (c + 1) * chunk)
            log_total = stat_ref[0, pl.ds(2 * pair + i, 1), span]
            scores = dot_t(own_keys, q_ref[span, :]) * (0.125 * LOG2E) + hidden_keys
            prob_ref[i, :, span] = jnp.exp2(scores - log_total).astype(bf16)


def probs_specs(seq, rows):
    pairs = H // 2
    lane = lambda kind: pl.BlockSpec((rows, 128), lambda s: (seq, kind * pairs + s))
    specs = [SMEM, lane(0), lane(1), pl.BlockSpec((1, 16, rows), lambda s: (seq, 0, 0))]
    return specs, pl.BlockSpec((2, rows, rows), lambda s: (seq * pairs + s, 0, 0))


def probs(seq, lengths, qkv, stats, deps=()):
    seqs, _, rows = stats.shape
    specs, out = probs_specs(seq, rows)
    return call(
        functools.partial(probs_kernel, seq),
        (lengths, qkv, qkv, stats),
        deps,
        grid=(H // 2,),
        in_specs=specs,
        out_specs=out,
        out_shape=jax.ShapeDtypeStruct((seqs * H, rows, rows), bf16),
        compiler_params=pltpu.CompilerParams(vmem_limit_bytes=VMEM),
        cost_estimate=pl.CostEstimate(flops=8_000_000_000, bytes_accessed=MIB, transcendentals=0),
        name="probs",
    )


def window_kernel(seq, blocks, lengths, q_ref, k_ref, stat_ref, _, x_ref, att_ref, vec_ref, proj_w, *refs):
    prob_ref, normed_ref, rstd_ref, hid_ref, x_t, att_t, hid_t, out_w, sem = refs
    g = pl.program_id(0)

    @pl.when(g == 0)
    def _():
        start_all(out_weight_copies(proj_w, out_w, sem))

    probs_kernel(seq, lengths, q_ref, k_ref, stat_ref, prob_ref)

    @pl.when(g == 0)
    def _():
        wait_whole(out_w, sem)

    @pl.when(g < blocks)
    def _():
        x, attended = x_ref[...], att_ref[...]
        normed, rstd = norm_rows(x + dot(attended, out_w[...]) + vec_ref[2:3, :])
        normed_ref[...] = normed
        rstd_ref[...] = jnp.broadcast_to(rstd, rstd_ref.shape)
        hidden = normed * vec_ref[3:4, :] + vec_ref[4:5, :]
        hid_ref[...] = hidden.astype(bf16)
        x_t[...] = x.T.astype(bf16)
        att_t[...] = attended.astype(f32).T.astype(bf16)
        hid_t[...] = hidden.T.astype(bf16)


def window(seq, lengths, x, qkv, attended, stats, weights, vectors, prob, deps=()):
    count = x.shape[0]
    _, _, rows = stats.shape
    blocks = count // BLOCK
    block = lambda s: jnp.minimum(s, blocks - 1)
    token = lambda width: pl.BlockSpec((BLOCK, width), lambda s: (block(s), 0))
    turned = pl.BlockSpec((D, BLOCK), lambda s: (0, block(s)))
    specs, out = probs_specs(seq, rows)
    return call(
        functools.partial(window_kernel, seq, blocks),
        (lengths, qkv, qkv, stats, prob, x, attended, vectors, weights),
        deps,
        grid=(H // 2,),
        in_specs=specs + [ANY, token(D), token(D), whole(16, D), ANY],
        out_specs=[out, token(D), token(128), token(D)] + [turned] * 3,
        out_shape=[
            jax.ShapeDtypeStruct(prob.shape, bf16),
            jax.ShapeDtypeStruct((count, D), f32),
            jax.ShapeDtypeStruct((count, 128), f32),
            jax.ShapeDtypeStruct((count, D), bf16),
        ]
        + [jax.ShapeDtypeStruct((D, count), bf16)] * 3,
        input_output_aliases={4: 0},
        scratch_shapes=[pltpu.VMEM((D, D), bf16), pltpu.SemaphoreType.DMA],
        compiler_params=pltpu.CompilerParams(vmem_limit_bytes=VMEM),
        cost_estimate=pl.CostEstimate(flops=14_000_000_000, bytes_accessed=MIB, transcendentals=0),
        name="window",
    )


def ffn_kernel(meta, pieces, blocks, place, normed_ref, rstd_ref, hid_ref, cot_ref, vec_ref, b1_ref, proj_w, *refs):
    piece_refs = refs[:pieces]
    (out_ref, fb_ref, ab_ref, ib_ref, branch_ref, small_ref, db1_ref, keep, send) = refs[pieces : pieces + 9]
    (out_w, inner_w, down_w, act, down_back, sem, wsem) = refs[pieces + 9 :]
    step = pl.program_id(0)

    @pl.when(step == 0)
    def _():
        start_all(inner_blocks(place, zip(piece_refs, meta), inner_w, sem.at[0]))
        start_all(down_blocks(place, zip(piece_refs, meta), down_w, sem.at[1]))
        start_all(out_weight_copies(proj_w, out_w, sem.at[2]))
        small_ref[...] = jnp.zeros_like(small_ref)
        db1_ref[...] = jnp.zeros_like(db1_ref)
        wait_whole(inner_w, sem.at[0])
        wait_whole(down_w, sem.at[1])
        wait_whole(out_w, sem.at[2])

    @pl.when(step < blocks)
    def _():
        rows = aligned(step * BLOCK, BLOCK, BLOCK)
        first_gain, first_shift = vec_ref[3:4, :], vec_ref[4:5, :]
        second_gain, second_shift = vec_ref[6:7, :], vec_ref[7:8, :]
        first_normed = normed_ref[...]
        hidden_low = hid_ref[...]
        total = first_normed * first_gain + first_shift + vec_ref[5:6, :]
        slopes = []
        for c in range(FF // WIDTH):
            cols = pl.ds(c * WIDTH, WIDTH)
            u = dot(hidden_low, inner_w[:, cols]) + b1_ref[:, cols]
            below, bell = gelu_parts(u)
            active = (u * below).astype(bf16)
            act[rows, cols] = active
            slopes.append(below + u * bell * GAUSS_DENSITY)
            total = total + dot(active, down_w[cols, :])
        second_normed, second_rstd = norm_rows(total)
        out_ref[...] = second_normed * second_gain + second_shift
        cot = cot_ref[...]
        second_back = norm_back(cot, second_normed, second_rstd, second_gain)
        back_low = second_back.astype(bf16)
        down_back[rows, :] = back_low
        hidden_back = second_back
        for c in range(FF // WIDTH):
            cols = pl.ds(c * WIDTH, WIDTH)
            ib = (dot_t(back_low, down_w[cols, :]) * slopes[c]).astype(bf16)
            ib_ref[:, cols] = ib
            db1_ref[:, cols] += fold_rows(ib.astype(f32))
            hidden_back = hidden_back + dot_t(ib, inner_w[:, cols])
        first_back = norm_back(hidden_back, first_normed, rstd_ref[:, 0:1], first_gain)
        fb_ref[...] = first_back
        branch_low = first_back.astype(bf16)
        branch_ref[...] = branch_low
        ab_ref[...] = dot_t(branch_low, out_w[...]).astype(bf16)
        sums = (
            branch_low.astype(f32),
            hidden_back * first_normed,
            hidden_back,
            back_low.astype(f32),
            cot * second_normed,
            cot,
        )
        for i, v in enumerate(sums):
            small_ref[i] += fold_rows(v)

    @pl.when(step >= blocks)
    def _():
        chunk = step - blocks
        width = FF // DOWN_STEPS
        rows = aligned(chunk * width, width, 128)
        down_w[rows, :] = dot_l(act[:, rows], down_back[...]).astype(bf16)
        for i in range(CHIPS // DOWN_STEPS):
            chip = chunk * (CHIPS // DOWN_STEPS) + i
            for half in range(2):
                at = (chip * 2 + half) * (2 * PAIR_ROWS)
                pairs = [
                    (down_w.at[aligned(at + k * PAIR_ROWS, PAIR_ROWS, 16)], pl.ds(k * D, D)) for k in range(2)
                ]
                hand_over(place, chip, half, keep, send, pairs, wsem)

    @pl.when(step == blocks + DOWN_STEPS - 1)
    def _():
        wait_whole(keep, wsem)
        wait_whole(send, wsem)


def feed_forward(place, normed, rstd, hid, cotangent, vectors, inner_bias, weights, pieces, meta):
    count = normed.shape[0]
    blocks = count // BLOCK
    token = lambda width: pl.BlockSpec((BLOCK, width), lambda s: (jnp.minimum(s, blocks - 1), 0))
    return pl.pallas_call(
        functools.partial(ffn_kernel, meta, len(pieces), blocks),
        grid=(blocks + DOWN_STEPS,),
        in_specs=[SMEM, token(D), token(128), token(D), token(D), whole(16, D), whole(1, FF), ANY]
        + [ANY] * len(pieces),
        out_specs=[token(D), token(D), token(D), token(FF), token(D), whole(6, 8, D), whole(8, FF), ANY, ANY],
        out_shape=[
            jax.ShapeDtypeStruct((count, D), f32),
            jax.ShapeDtypeStruct((count, D), f32),
            jax.ShapeDtypeStruct((count, D), bf16),
            jax.ShapeDtypeStruct((count, FF), bf16),
            jax.ShapeDtypeStruct((count, D), bf16),
            jax.ShapeDtypeStruct((6, 8, D), f32),
            jax.ShapeDtypeStruct((8, FF), f32),
            jax.ShapeDtypeStruct((CHIPS, PAIR_ROWS, DOWN_BLOCK), bf16),
            jax.ShapeDtypeStruct((CHIPS, PAIR_ROWS, DOWN_BLOCK), bf16),
        ],
        scratch_shapes=[
            pltpu.VMEM((D, D), bf16),
            pltpu.VMEM((D, FF), bf16),
            pltpu.VMEM((FF, D), bf16),
            pltpu.VMEM((count, FF), bf16),
            pltpu.VMEM((count, D), bf16),
            pltpu.SemaphoreType.DMA((3,)),
            pltpu.SemaphoreType.DMA,
        ],
        compiler_params=pltpu.CompilerParams(vmem_limit_bytes=ALL_VMEM),
        cost_estimate=pl.CostEstimate(flops=52_000_000_000, bytes_accessed=40 * MIB, transcendentals=0),
        name="feed_forward",
    )(place, normed, rstd, hid, cotangent, vectors, inner_bias, weights, *pieces)


def inner_grads_kernel(hid_t, ib_ref, place, att_in, branch_in, keep, send, att_t, branch, out_g, inner_g, sem, wsem):
    step = pl.program_id(0)
    steps = FF // D
    later = [pltpu.make_async_copy(att_in, att_t, sem.at[0]), pltpu.make_async_copy(branch_in, branch, sem.at[1])]

    @pl.when(step == 0)
    def _():
        start_all(later)

    def give(grads, half, width, lane):
        for chip in range(CHIPS):
            block = grads.at[pl.ds(chip * PAIR_ROWS, PAIR_ROWS), pl.ds(half * width, width)]
            hand_over(place, chip, half, keep, send, [(block, pl.ds(lane, width))], wsem)

    @pl.when(step < steps)
    def _():
        cols = aligned(step * D, D, 128)
        inner_g[:, cols] = dot(hid_t[...], ib_ref[...]).astype(bf16)
        for half in range(2):

            @pl.when(step == (half + 1) * (steps // 2) - 1)
            def _():
                give(inner_g, half, INNER_HALF, OUT_HALF)

    @pl.when(step == steps)
    def _():
        for copy in later:
            copy.wait()
        out_g[...] = dot(att_t[...], branch[...]).astype(bf16)
        for half in range(2):
            give(out_g, half, OUT_HALF, 0)
        wait_whole(keep, wsem)
        wait_whole(send, wsem)


def inner_grads(place, hid_t, inner_back, att_t, branch):
    count = hid_t.shape[1]
    steps = FF // D
    return pl.pallas_call(
        inner_grads_kernel,
        grid=(steps + 1,),
        in_specs=[
            whole(D, count),
            pl.BlockSpec((count, D), lambda s: (0, jnp.minimum(s, steps - 1))),
            SMEM,
            ANY,
            ANY,
        ],
        out_specs=[ANY, ANY],
        out_shape=[jax.ShapeDtypeStruct((CHIPS, PAIR_ROWS, INNER_BLOCK), bf16)] * 2,
        scratch_shapes=[
            pltpu.VMEM((D, count), bf16),
            pltpu.VMEM((count, D), bf16),
            pltpu.VMEM((D, D), bf16),
            pltpu.VMEM((D, FF), bf16),
            pltpu.SemaphoreType.DMA((2,)),
            pltpu.SemaphoreType.DMA,
        ],
        compiler_params=pltpu.CompilerParams(vmem_limit_bytes=ALL_VMEM),
        cost_estimate=pl.CostEstimate(flops=4_000_000_000, bytes_accessed=MIB, transcendentals=0),
        name="inner_grads",
    )(hid_t, inner_back, place, att_t, branch)


def attend_back_pair(queries, keys, values, upstream, prob_ref, dq_ref, dk_ref, dv_ref):
    lows, backs = [], []
    masks = lane_masks()
    for i, mask in enumerate(masks):
        low = prob_ref[i]
        weight = low.astype(f32)
        weight_back = dot_t(values * mask, upstream)
        mean = jnp.sum(weight * weight_back, axis=0, keepdims=True)
        lows.append(low)
        backs.append((weight * (weight_back - mean)).astype(bf16))
    each = lambda v: jnp.concatenate([v * mask for mask in masks], axis=0)
    dv_ref[...] = dot(jnp.concatenate(lows, axis=1), each(upstream)).astype(bf16)
    dk_ref[...] = (dot(jnp.concatenate(backs, axis=1), each(queries)) * 0.125).astype(bf16)
    dq_ref[...] = (dot_l(jnp.concatenate(backs, axis=0), each(keys)) * 0.125).astype(bf16)


def attend_back_kernel(q_ref, k_ref, v_ref, up_ref, prob_ref, *refs):
    attend_back_pair(q_ref[...], k_ref[...], v_ref[...], up_ref[...], prob_ref, *refs[-3:])


def pair_specs(rows, first, last):
    pairs = H // 2
    pair = lambda s: jnp.minimum(first + s, last)
    lane = lambda kind: pl.BlockSpec((rows, 128), lambda s: (pair(s) // pairs, kind * pairs + pair(s) % pairs))
    return [lane(0), lane(1), lane(2), lane(0), pl.BlockSpec((2, rows, rows), lambda s: (pair(s), 0, 0))]


def attend_back(first, count, qkv, back, prob, grads=(), deps=()):
    specs = pair_specs(prob.shape[1], first, first + count - 1)
    return call(
        attend_back_kernel,
        (qkv, qkv, qkv, back, prob, *grads),
        deps,
        grid=(count,),
        in_specs=specs + [ANY] * len(grads),
        out_specs=[specs[0]] * 3,
        out_shape=[jax.ShapeDtypeStruct(back.shape, bf16)] * 3,
        input_output_aliases={5 + i: i for i in range(len(grads))},
        compiler_params=pltpu.CompilerParams(vmem_limit_bytes=ALL_VMEM),
        cost_estimate=pl.CostEstimate(flops=3_000_000_000, bytes_accessed=MIB, transcendentals=0),
        name=f"attend_back_{first}",
    )


def proj_grads_kernel(place, turned, small_ref, db1_ref, dq, dk, dv, keep, send, grads, packed, bias, sem, wsem):
    step = pl.program_id(0)
    copies = [pltpu.make_async_copy(v, grads.at[i], sem.at[i]) for i, v in enumerate((dq, dk, dv))]

    @pl.when(step == 0)
    def _():
        start_all([copies[1], copies[2], copies[0]])

    for turn, which in enumerate((1, 2, 0)):

        @pl.when(step == turn)
        def _():
            copies[which].wait()
            g = dot(turned[...], grads[which]).astype(bf16)
            if which == 1:
                packed[:, D:QKV_HALF] = g[:, : D // 2]
                packed[:, QKV_BLOCK : QKV_BLOCK + D // 2] = g[:, D // 2 :]
            else:
                at = 0 if which == 0 else QKV_BLOCK + D // 2
                packed[:, at : at + D] = g
                bias[which // 2] = fold_rows(grads[which].astype(f32))

    @pl.when(step == 0)
    def _():
        owner = lax.broadcasted_iota(jnp.int32, (SLABS, FF), 1) // (4 * SLAB)
        one = lax.broadcasted_iota(jnp.int32, (SLABS, FF), 0)
        mine = jnp.where(owner == one, jnp.sum(db1_ref[...], axis=0, keepdims=True), 0.0)
        place_of = lax.broadcasted_iota(jnp.int32, (FF, 128), 0) % (4 * SLAB)
        pick = place_of == lax.broadcasted_iota(jnp.int32, (FF, 128), 1)
        table = dot(mine.astype(bf16), pick.astype(bf16))
        spread = jnp.broadcast_to(table[:, None, :], (SLABS, SLAB, 128)).reshape(D, 128)
        packed[:, QKV_BLOCK + QKV_HALF :] = spread.astype(bf16)

    def give(half):
        for chip in range(CHIPS):
            block = packed.at[pl.ds(chip * PAIR_ROWS, PAIR_ROWS), pl.ds(half * QKV_BLOCK, QKV_BLOCK)]
            hand_over(place, chip, half, keep, send, [(block, pl.ds(0, QKV_BLOCK))], wsem)

    @pl.when(step == 1)
    def _():
        give(1)

    @pl.when(step == 2)
    def _():
        rows_of = [bias[...], small_ref[...], jnp.zeros((120, 8, D), f32)]
        packed[:, QKV_HALF:QKV_BLOCK] = jnp.sum(jnp.concatenate(rows_of, axis=0), axis=1).T.astype(bf16)
        give(0)
        wait_whole(keep, wsem)
        wait_whole(send, wsem)


def proj_grads(place, turned, small, inner_bias_grad, grads, deps=()):
    count = turned.shape[1]
    return call(
        proj_grads_kernel,
        (place, turned, small, inner_bias_grad, *grads),
        deps,
        grid=(3,),
        in_specs=[SMEM, whole(D, count), whole(6, 8, D), whole(8, FF), ANY, ANY, ANY],
        out_specs=[ANY, ANY],
        out_shape=[jax.ShapeDtypeStruct((CHIPS, PAIR_ROWS, QKV_BLOCK), bf16)] * 2,
        scratch_shapes=[
            pltpu.VMEM((3, count, D), bf16),
            pltpu.VMEM((D, 2 * QKV_BLOCK), bf16),
            pltpu.VMEM((2, 8, D), f32),
            pltpu.SemaphoreType.DMA((3,)),
            pltpu.SemaphoreType.DMA,
        ],
        compiler_params=pltpu.CompilerParams(vmem_limit_bytes=ALL_VMEM),
        cost_estimate=pl.CostEstimate(flops=4_000_000_000, bytes_accessed=MIB, transcendentals=0),
        name="proj_grads",
    )


def input_back_kernel(fb_ref, dq_ref, dk_ref, dv_ref, w_ref, *refs):
    half = D // 2
    total = fb_ref[...] + dot_t(dq_ref[...], w_ref[:, 0:D])
    total = total + dot_t(dk_ref[:, :half], w_ref[:, D:QKV_HALF])
    total = total + dot_t(dk_ref[:, half:], w_ref[:, PROJ_BLOCK : PROJ_BLOCK + half])
    out_ref, small_ref = refs[-2:]
    small_ref[...] = total[0:16, 0:128]
    out_ref[...] = total + dot_t(dv_ref[...], w_ref[:, PROJ_BLOCK + half : PROJ_BLOCK + QKV_HALF])


def input_back(first, blocks, first_back, grads, weights, given=(), deps=()):
    token = pl.BlockSpec((BLOCK, D), lambda s: (first + s, 0))
    return call(
        input_back_kernel,
        (first_back, *grads, weights, *given),
        deps,
        grid=(blocks,),
        in_specs=[token] * 4 + [whole(D, 2 * PROJ_BLOCK)] + [ANY] * len(given),
        out_specs=[token, whole(16, 128)],
        out_shape=[jax.ShapeDtypeStruct(first_back.shape, f32), jax.ShapeDtypeStruct((16, 128), f32)],
        input_output_aliases={5: 0} if given else {},
        compiler_params=pltpu.CompilerParams(vmem_limit_bytes=ALL_VMEM),
        cost_estimate=pl.CostEstimate(flops=10_000_000_000, bytes_accessed=MIB, transcendentals=0),
        name=f"input_back_{first}",
    )


def add_up_kernel(jobs, passed, place, *refs):
    refs[len(refs) - 1][...] = refs[0][0, 0:8, 0:128].astype(f32)
    first, out = 0, sum(count for count, _ in jobs) + passed
    for count, kind in jobs:
        terms = refs[first : first + count]
        first += count

        def total(slot):
            return sum((ref[slot].astype(f32) for ref in terms[1:]), terms[0][slot].astype(f32))

        slots = terms[0].shape[0]
        if kind == "upper":

            def one(i, _, total=total, ready=refs[out]):
                ready[i] = total(i).astype(bf16)
                return 0

            lax.fori_loop(0, slots, one, 0)
            out += 1
        elif kind == "both":
            half = slots // 2

            def one(i, _, total=total, ready=refs[out], rest=refs[out + 1], half=half):
                rest[i] = total(i)
                ready[i] = total(half + i).astype(bf16)
                return 0

            lax.fori_loop(0, half, one, 0)
            out += 2
        elif kind == "down":
            whole_sum = total(0)
            refs[out][0:PAIR_ROWS, :] = whole_sum[:, :D]
            refs[out][PAIR_ROWS:, :] = whole_sum[:, D:]
            out += 1
        else:
            whole_sum = total(0)
            low_core = place[1] == 0
            low, high = whole_sum[:SLAB], whole_sum[SLAB:]
            refs[out][...] = jnp.where(low_core, low, high)
            refs[out + 1][...] = jnp.where(low_core, high, low)
            out += 2


def add_up(place, *groups, passed=(), deps=(), vmem=ALL_VMEM):
    operands, specs, out_specs, shapes, jobs = [], [], [], [], []
    for size, terms, lazy in groups:
        _, rows, lanes = terms[0].shape
        half = size // 2
        kind = "upper" if lazy else "both" if size > 1 else "down" if lanes == DOWN_BLOCK else "halves"
        operands += terms
        take = (half, 1) if kind == "upper" else (size, 0)
        specs += [pl.BlockSpec((take[0], rows, lanes), lambda s, at=take[1]: (at, 0, 0))] * len(terms)
        if size > 1:
            kinds = [bf16] if kind == "upper" else [bf16, f32]
            out_specs += [whole(half, rows, lanes)] * len(kinds)
            shapes += [jax.ShapeDtypeStruct((half, rows, lanes), dtype) for dtype in kinds]
        else:
            ends = [(2 * PAIR_ROWS, D)] if kind == "down" else [(SLAB, lanes)] * 2
            out_specs += [whole(*end) for end in ends]
            shapes += [jax.ShapeDtypeStruct(end, f32) for end in ends]
        jobs.append((len(terms), kind))
    return call(
        lambda *refs: add_up_kernel(jobs, len(passed), refs[0], *refs[1:]),
        [place] + operands + list(passed),
        deps,
        grid=(1,),
        in_specs=[SMEM] + specs + [ANY] * len(passed),
        out_specs=out_specs + [ANY] * len(passed) + [whole(8, 128)],
        out_shape=shapes
        + [jax.ShapeDtypeStruct(v.shape, v.dtype) for v in passed]
        + [jax.ShapeDtypeStruct((8, 128), f32)],
        input_output_aliases={1 + len(operands) + i: len(shapes) + i for i in range(len(passed))},
        compiler_params=pltpu.CompilerParams(vmem_limit_bytes=vmem),
        cost_estimate=pl.CostEstimate(flops=1000, bytes_accessed=1000, transcendentals=0),
        name="add_up",
    )


def gate(value, deps, vmem=ALL_VMEM):
    return call(
        lambda value_ref, out_ref: None,
        [value],
        deps,
        grid=(1,),
        in_specs=[ANY],
        out_specs=ANY,
        out_shape=jax.ShapeDtypeStruct(value.shape, value.dtype),
        input_output_aliases={0: 0},
        compiler_params=pltpu.CompilerParams(vmem_limit_bytes=vmem),
        cost_estimate=pl.CostEstimate(flops=1000, bytes_accessed=1000, transcendentals=0),
        name="gate",
    )


def finish_inner_kernel(place, mine, other, out_g, inner_g, small):
    low_core = place[1] == 0
    low = jnp.where(low_core, mine[...], other[...])
    high = jnp.where(low_core, other[...], mine[...])
    out_g[:, :OUT_HALF], out_g[:, OUT_HALF:] = low[:, :OUT_HALF], high[:, :OUT_HALF]
    inner_g[:, :INNER_HALF], inner_g[:, INNER_HALF:] = low[:, OUT_HALF:], high[:, OUT_HALF:]
    small[...] = low[0:8, 0:128]


def finish_proj_kernel(place, mine, other, dq, dk, dv, bias, *vectors):
    low_core = place[1] == 0
    low = jnp.where(low_core, mine[...], other[...])
    high = jnp.where(low_core, other[...], mine[...])
    half = D // 2
    dq[...] = low[:, :D]
    dk[:, :half], dk[:, half:] = low[:, D:QKV_HALF], high[:, :half]
    dv[...] = high[:, half:QKV_HALF]
    bias[...] = high[0, QKV_HALF : QKV_HALF + 4 * SLAB]
    rows = low[:, QKV_HALF:].T
    for i, out in enumerate(vectors):
        out[...] = rows[i, 0:SLAB]


def finish(kernel, place, mine, other, shapes, name, deps=()):
    at = lambda shape: pl.BlockSpec(shape, lambda s: (0,) * len(shape))
    return call(
        kernel,
        (place, mine, other),
        deps,
        grid=(1,),
        in_specs=[SMEM, at(mine.shape), at(mine.shape)],
        out_specs=[at(shape) for shape in shapes],
        out_shape=[jax.ShapeDtypeStruct(shape, f32) for shape in shapes],
        compiler_params=pltpu.CompilerParams(vmem_limit_bytes=LITTLE),
        cost_estimate=pl.CostEstimate(flops=1000, bytes_accessed=1000, transcendentals=0),
        name=name,
    )


def finish_inner(place, mine, other):
    return finish(finish_inner_kernel, place, mine, other, [(SLAB, D), (SLAB, FF), (8, 128)], "finish_inner")


def finish_proj(place, mine, other, deps=()):
    shapes = [(SLAB, D)] * 3 + [(4 * SLAB,)] + [(SLAB,)] * 8
    return finish(finish_proj_kernel, place, mine, other, shapes, "finish_proj", deps)


AXES = ("dp", "fsdp")


CORE = (1, 1)
ALONG_Z_FIRST, ALONG_Z_THEN, ALONG_Z_BOTH, ALONG_XY_FIRST, ALONG_XY_THEN = (16, 8), (8, 16), (24, 24), (2, 4), (4, 2)
FAST_SHAPE = {"dp": 4, "fsdp": 8}


def move(v, masks):
    return lax.ppermute(v, AXES, [(i, i ^ masks[i & 1]) for i in range(SLABS)])


SUM_STEPS = (ALONG_XY_THEN, ALONG_XY_FIRST, ALONG_Z_THEN, ALONG_Z_FIRST)


def after(*values):
    return lax.optimization_barrier(values)


class Sums:
    def __init__(self, keep, got):
        self.size, self.terms, self.step = CHIPS, [keep, got], 0

    def send(self, outs, lazy):
        ready = outs.pop(0)
        if not lazy:
            self.terms = [outs.pop(0)]
        self.size //= 2
        self.terms = self.terms + [move(ready, SUM_STEPS[self.step])]
        self.step += 1


def add_and_send(place, *groups, lazy=False, **options):
    outs = list(add_up(place, *[(g.size, g.terms, lazy) for g in groups], **options))
    for g in groups:
        if g.size > 1:
            g.send(outs, lazy)
    return outs


def fast_blocks(shards, core):
    (qw, kw, vw, ow, qb, vb, ob, fg, fs, iw, ib, dw, db, sg, ss) = shards
    vectors = jnp.pad(jnp.stack([qb, vb, ob, fg, fs, db, sg, ss], axis=1), ((0, 0), (0, 120)))
    inner_bias = jnp.pad(ib.reshape(1, 4 * SLAB), ((0, SLAB - 1), (0, 128 - 4 * SLAB)))
    half = D // 2
    halves = [
        jnp.concatenate([qw, kw[:, :half], vectors, ow[:, :half], iw[:, :INNER_HALF]], axis=1),
        jnp.concatenate([kw[:, half:], vw, inner_bias, ow[:, half:], iw[:, INNER_HALF:]], axis=1),
    ]
    low_core = core == 0
    own = jnp.where(low_core, halves[0], halves[1])
    other = move(jnp.where(low_core, halves[1], halves[0]), CORE)
    rows = jnp.concatenate([jnp.where(low_core, own, other), jnp.where(low_core, other, own)], axis=0)
    return rows[:, :PROJ_BLOCK], rows[:, PROJ_BLOCK:], jnp.concatenate([dw[:PAIR_ROWS], dw[PAIR_ROWS:]], axis=1)


def gather_plain(shards):
    (qw, kw, vw, ow, qb, vb, ob, fg, fs, iw, ib, dw, db, sg, ss) = [
        lax.all_gather(v, AXES, axis=0, tiled=True) for v in shards
    ]
    vectors = jnp.pad(jnp.stack([qb, vb, ob, fg, fs, db, sg, ss], axis=1), ((0, 0), (0, 120)))
    inner_bias = jnp.pad(ib.reshape(SLABS, 1, 4 * SLAB), ((0, 0), (0, SLAB - 1), (0, 128 - 4 * SLAB))).reshape(D, 128)
    half = D // 2
    chips = lambda v: v.reshape(CHIPS, PAIR_ROWS, -1)
    down = dw.reshape(CHIPS, 2, 2, PAIR_ROWS, D)
    first = [
        chips(jnp.concatenate([qw, kw[:, :half], vectors, ow[:, :half]], axis=1)),
        chips(jnp.concatenate([kw[:, half:], vw, inner_bias, ow[:, half:]], axis=1)),
    ]
    second = [
        jnp.concatenate([chips(iw[:, c * INNER_HALF : (c + 1) * INNER_HALF]), down[:, c, 0], down[:, c, 1]], axis=2)
        for c in range(2)
    ]
    slots = lambda halves: [v[np.array(SLOT_CHIPS[c])] for c, v in enumerate(halves)]
    return slots(first), slots(second)


def local(fast, inputs, lengths, *rest):
    shards, cotangent = rest[:15], rest[15]
    both = lambda v, came: jnp.concatenate([v, came])
    if fast:
        linear = lax.axis_index(AXES)
        core = linear & 1
        place = jnp.stack([linear >> 1, core]).astype(jnp.int32)
        first, inner, down = fast_blocks(shards, core)
        first = first[None]
        first = both(first, move(first, ALONG_Z_FIRST))
        first, second = after(first, jnp.concatenate([inner, down], axis=1)[None])
        second = jnp.concatenate([second] + [move(second, steps) for steps in (ALONG_Z_FIRST, ALONG_Z_THEN, ALONG_Z_BOTH)])
        first = both(first, move(first, ALONG_Z_THEN))
        first_then, first_core = move(first, ALONG_XY_THEN), move(first, CORE)
        first_came = move(first, ALONG_XY_FIRST)
        first_last, came_core = move(first_came, ALONG_XY_THEN), move(first_came, CORE)
        first_then, first_last, second = after(first_then, first_last, second)
        first = [first, first_came, first_then, first_last]
        first += [first_core, came_core, move(first_then, CORE), move(first_last, CORE)]
        second_came, second_then, second_core = move(second, ALONG_XY_FIRST), move(second, ALONG_XY_THEN), move(second, CORE)
        meta = tuple((at, other) for other in (False, True) for at in range(0, CHIPS, 4))
    else:
        place = jnp.zeros((2,), jnp.int32)
        first, second = gather_plain(shards)
        meta = ((0, False), (0, True))
    qkv, attended, stats, weights, vectors = attend(place, lengths, inputs, first, meta)
    prob = probs(0, lengths, qkv, stats)
    if fast:
        second_came, second_then, prob = after(second_came, second_then, prob)
        second_last, came_core, then_core = move(second_came, ALONG_XY_THEN), move(second_came, CORE), move(second_then, CORE)
    prob, normed, rstd, hid, inputs_t, attended_t, hid_t = window(
        1, lengths, inputs, qkv, attended, stats, weights, vectors, prob
    )
    bias_at = PROJ_BLOCK + QKV_HALF
    inner_bias = weights[::SLAB, bias_at : bias_at + 4 * SLAB].reshape(1, FF).astype(f32)
    if fast:
        second_last, normed, inner_bias = after(second_last, normed, inner_bias)
        second = [second, second_came, second_then, second_last]
        second += [second_core, came_core, then_core, move(second_last, CORE)]
    output, first_back, back, inner_back, branch, small, db1, down_keep, down_send = feed_forward(
        place, normed, rstd, hid, cotangent, vectors, inner_bias, weights, second, meta
    )
    inner_keep, inner_send = inner_grads(place, hid_t, inner_back, attended_t, branch)
    pairs = lengths.shape[0] * (H // 2)
    third = pairs // 3
    deps = []
    if fast:
        down = Sums(down_keep, move(down_send, CORE))
        inner_send, *deps = add_and_send(place, down, lazy=True, passed=[inner_send], deps=[inner_keep])
        inner = Sums(inner_keep, move(inner_send, CORE))
    grads = attend_back(0, third, qkv, back, prob, deps=deps)
    if fast:
        deps = add_and_send(place, inner, lazy=True, deps=grads[:1])
    grads = attend_back(third, third, qkv, back, prob, grads, deps=deps)
    if fast:
        deps = add_and_send(place, down, lazy=True, deps=grads[:1])
    grads = attend_back(2 * third, pairs - 2 * third, qkv, back, prob, grads, deps=deps)
    if fast:
        deps = add_and_send(place, inner, down, lazy=True, deps=grads[:1])
    proj_keep, proj_send = proj_grads(place, inputs_t, small, db1, grads, deps=deps)
    blocks = inputs.shape[0] // BLOCK
    if fast:
        proj_send = gate(proj_send, [inner.terms[-1], down.terms[-1]])
        proj = Sums(proj_keep, move(proj_send, CORE))
        deps = add_and_send(place, inner, down, deps=[proj_keep])
        deps = add_and_send(place, proj, lazy=True, deps=deps)
        grad_input, came = input_back(0, blocks, first_back, grads, weights, deps=deps)
        proj.terms[-1] = gate(proj.terms[-1], [inner.terms[-1], down.terms[-1], came], MIB)
        deps = add_and_send(place, proj, vmem=LITTLE)
        down_grad, *deps = add_and_send(place, inner, down, deps=deps, vmem=LITTLE)
        proj.terms[-1] = gate(proj.terms[-1], [inner.terms[-1]], MIB)
        deps = add_and_send(place, proj, deps=deps, vmem=LITTLE)
        mine, other, *deps = add_and_send(place, proj, inner, deps=deps, vmem=LITTLE)
        out_grad, inner_grad, *deps = finish_inner(place, mine, move(other, CORE))
        mine, other, _ = add_and_send(place, proj, deps=deps, vmem=LITTLE)
        *square, bias, v0, v1, v2, v3, v4, v5, v6, v7 = finish_proj(place, mine, move(other, CORE))
        vectors = [v0, v1, v2, v3, v4, v5, v6, v7]
    else:
        grad_input, _ = input_back(0, blocks, first_back, grads, weights)
        shard = lambda *v: lax.psum_scatter(jnp.concatenate(v, axis=1), AXES, scatter_dimension=0, tiled=True)
        by_chip = lambda pair: [v[np.argsort(np.array(SLOT_CHIPS[c]))].astype(f32) for c, v in enumerate(pair)]
        low, high = (v.reshape(D, -1) for v in by_chip((inner_keep, inner_send)))
        out_grad, inner_grad = shard(low[:, :OUT_HALF], high[:, :OUT_HALF]), shard(low[:, OUT_HALF:], high[:, OUT_HALF:])
        parts = [jnp.stack([v[:, :, :D], v[:, :, D:]], axis=1) for v in by_chip((down_keep, down_send))]
        down_grad = shard(jnp.stack(parts, axis=1).reshape(FF, D))
        low, high = (v.reshape(D, -1) for v in by_chip((proj_keep, proj_send)))
        half = D // 2
        square = shard(low[:, :D]), shard(low[:, D:QKV_HALF], high[:, :half]), shard(high[:, half:QKV_HALF])
        columns = shard(low[:, QKV_HALF:])
        vectors = [columns[:, i] for i in range(8)]
        bias = shard(high[::SLAB, QKV_HALF : QKV_HALF + 4 * SLAB].reshape(FF, 1))[:, 0]
    return (
        output,
        grad_input,
        *square,
        out_grad,
        *vectors[:5],
        inner_grad,
        bias,
        down_grad,
        *vectors[5:],
    )


def solution(mesh):
    rows, flat = P(AXES, None), P(AXES)
    params = (rows,) * 4 + (flat,) * 5 + (rows, flat, rows, flat, flat, flat)
    return jax.shard_map(
        functools.partial(local, dict(mesh.shape) == FAST_SHAPE),
        mesh=mesh,
        in_specs=(rows, flat) + params + (rows,),
        out_specs=(rows, rows) + params,
        check_vma=False,
    )
```

```python
import functools
import math

import jax
import jax.numpy as jnp
import numpy as np
from jax import lax
from jax.experimental import pallas as pl
from jax.experimental.pallas import tpu as pltpu
from jax.sharding import PartitionSpec as P

D = 768
H = 12
DH = 64
FF = 3072
SLABS = 32
SLAB = D // SLABS
CHIPS = SLABS // 2
PAIR_ROWS = 2 * SLAB
NORM_EPSILON = 1e-12
MASKED_SCORE = -1000000000.0
GAUSS_DENSITY = 0.3989422804014327
LOG2E = 1.4426950408889634
MIB = 1 << 20
VMEM = 62 * MIB
ALL_VMEM = 127 * MIB // 2
LITTLE = 16 * MIB

QKV_HALF = 3 * D // 2
QKV_BLOCK = QKV_HALF + 128
OUT_HALF = D // 2
PROJ_BLOCK = QKV_BLOCK + OUT_HALF
INNER_HALF = FF // 2
INNER_BLOCK = OUT_HALF + INNER_HALF
DOWN_BLOCK = 2 * D

SLOT_BITS = ((8, 4, 1, 2), (4, 8, 2, 1))
SLOT_CHIPS = tuple(
    tuple(sum(bit for i, bit in enumerate(bits) if slot >> i & 1) for slot in range(CHIPS)) for bits in SLOT_BITS
)

bf16 = jnp.bfloat16
f32 = jnp.float32
ANY = pl.BlockSpec(memory_space=pl.ANY)
SMEM = pl.BlockSpec(memory_space=pltpu.SMEM)


def dot(a, b):
    return lax.dot_general(a, b, (((1,), (0,)), ((), ())), preferred_element_type=f32)


def dot_t(a, b):
    return lax.dot_general(a, b, (((1,), (1,)), ((), ())), preferred_element_type=f32)


def dot_l(a, b):
    return lax.dot_general(a, b, (((0,), (0,)), ((), ())), preferred_element_type=f32)


def call(kernel, operands, deps, in_specs, **options):
    count = len(operands)

    def body(*refs):
        kernel(*refs[:count], *refs[count + len(deps) :])

    in_specs = in_specs + [whole(8, 128) if v.shape == (8, 128) else ANY for v in deps]
    return pl.pallas_call(body, in_specs=in_specs, **options)(*operands, *deps)


def aligned(start, size, unit):
    return pl.ds(pl.multiple_of(start, unit), size)


def chip_of(slot, half):
    return jnp.where(half == 0, SLOT_CHIPS[0][slot], SLOT_CHIPS[1][slot])


def slot_of(chip, half):
    bits = SLOT_BITS[half]
    return sum(jnp.where((chip & bit) != 0, 1 << i, 0) for i, bit in enumerate(bits))


def blocks_of(place, pieces):
    for ref, (first, other) in pieces:
        half = 1 - place[1] if other else place[1]
        for i in range(ref.shape[0]):
            yield ref, i, place[0] ^ chip_of(first + i, half), half


def proj_blocks(place, pieces, weights, sem):
    for ref, i, chip, half in blocks_of(place, pieces):
        rows = aligned(chip * PAIR_ROWS, PAIR_ROWS, 16)
        yield pltpu.make_async_copy(ref.at[i], weights.at[rows, aligned(half * PROJ_BLOCK, PROJ_BLOCK, 128)], sem)


def inner_blocks(place, pieces, inner_w, sem):
    for ref, i, chip, half in blocks_of(place, pieces):
        rows = aligned(chip * PAIR_ROWS, PAIR_ROWS, 16)
        yield pltpu.make_async_copy(
            ref.at[i, :, pl.ds(0, INNER_HALF)],
            inner_w.at[rows, aligned(half * INNER_HALF, INNER_HALF, 128)],
            sem,
        )


def down_blocks(place, pieces, down_w, sem):
    for ref, i, chip, half in blocks_of(place, pieces):
        for k in range(2):
            at = (chip * 2 + half) * (2 * PAIR_ROWS) + k * PAIR_ROWS
            yield pltpu.make_async_copy(
                ref.at[i, :, pl.ds(INNER_HALF + k * D, D)], down_w.at[aligned(at, PAIR_ROWS, 16), :], sem
            )


def start_all(copies):
    for c in copies:
        c.start()


def whole(*shape):
    return pl.BlockSpec(shape, lambda *s: (0,) * len(shape))


def fold_rows(v):
    return jnp.sum(v.reshape(v.shape[0] // 8, 8, v.shape[1]), axis=0)


def hand_over(place, chip, half, keep, send, pairs, sem):
    slot = slot_of(chip ^ place[0], half)
    for mine, out in ((True, keep), (False, send)):

        @pl.when((place[1] == half) == mine)
        def _():
            for source, lanes in pairs:
                pltpu.make_async_copy(source, out.at[slot, :, lanes], sem).start()


def wait_whole(ref, sem):
    pltpu.make_async_copy(ref, ref, sem).wait()


def lane_masks():
    low = (lax.broadcasted_iota(jnp.int32, (1, 128), 1) < DH).astype(f32)
    return low.astype(bf16), (1.0 - low).astype(bf16)


def attend_kernel(meta, n_pieces, place, lengths, x_ref, *refs):
    piece_refs = refs[:n_pieces]
    qkv_ref, att_ref, stat_ref, weights, vectors = refs[n_pieces : n_pieces + 5]
    sem = refs[-1]
    seq = pl.program_id(0)
    rows = x_ref.shape[0]

    @pl.when(seq == 0)
    def _():
        start_all(proj_blocks(place, zip(piece_refs, meta), weights, sem))
        wait_whole(weights, sem)
        small = weights[:, QKV_HALF:QKV_BLOCK].astype(f32)
        vectors[...] = small.T[0:16, :]

    lowered = x_ref[...].astype(bf16)
    first = dot(lowered, weights[:, 0:QKV_HALF])
    qkv_ref[:, 0:D] = (first[:, 0:D] + vectors[0:1, :]).astype(bf16)
    qkv_ref[:, D:QKV_HALF] = first[:, D:QKV_HALF].astype(bf16)
    second = dot(lowered, weights[:, PROJ_BLOCK : PROJ_BLOCK + QKV_HALF])
    qkv_ref[:, QKV_HALF : 2 * D] = second[:, 0 : D // 2].astype(bf16)
    qkv_ref[:, 2 * D :] = (second[:, D // 2 :] + vectors[1:2, :]).astype(bf16)

    low, high = lane_masks()
    lane = lax.broadcasted_iota(jnp.int32, (1, 128), 1)
    key_at = lax.broadcasted_iota(jnp.int32, (1, rows), 1)
    hidden_keys = jnp.where(key_at < lengths[seq], 0.0, MASKED_SCORE).astype(f32)
    chunk = 256
    ones = jnp.ones((rows, 128), bf16)
    stats = [jnp.zeros((chunk, 128), f32) for _ in range(rows // chunk)]
    for pair in range(H // 2):
        at = pair * 128
        keys = qkv_ref[:, D + at : D + at + 128]
        values = jnp.concatenate([qkv_ref[:, 2 * D + at : 2 * D + at + 128], ones], axis=1)
        keys_of = (keys * low, keys * high)
        for c in range(rows // chunk):
            span = pl.ds(c * chunk, chunk)
            queries = qkv_ref[span, at : at + 128]
            outs = []
            for i in range(2):
                scores = dot_t(queries, keys_of[i]) * (0.125 * LOG2E) + hidden_keys
                peak = jnp.max(scores, axis=-1, keepdims=True)
                weight = jnp.exp2(scores - peak).astype(bf16)
                both = dot(weight, values)
                total = both[:, 128:]
                outs.append(both[:, :128] / total)
                log_total = peak + jnp.log2(total)
                stats[c] = jnp.where(lane == 2 * pair + i, log_total, stats[c])
            att_ref[span, at : at + 128] = jnp.where(lane < DH, outs[0], outs[1]).astype(bf16)
    for c in range(rows // chunk):
        stat_ref[0, :, c * chunk : (c + 1) * chunk] = stats[c].T[0:16, :]


def attend(place, lengths, x, pieces, meta):
    rows = x.shape[0] // lengths.shape[0]
    seqs = lengths.shape[0]
    return pl.pallas_call(
        functools.partial(attend_kernel, meta, len(pieces)),
        grid=(seqs,),
        in_specs=[SMEM, SMEM, pl.BlockSpec((rows, D), lambda s: (s, 0))] + [ANY] * len(pieces),
        out_specs=[
            pl.BlockSpec((rows, 3 * D), lambda s: (s, 0)),
            pl.BlockSpec((rows, D), lambda s: (s, 0)),
            pl.BlockSpec((1, 16, rows), lambda s: (s, 0, 0)),
            whole(D, 2 * PROJ_BLOCK),
            whole(16, D),
        ],
        out_shape=[
            jax.ShapeDtypeStruct((seqs * rows, 3 * D), bf16),
            jax.ShapeDtypeStruct((seqs * rows, D), bf16),
            jax.ShapeDtypeStruct((seqs, 16, rows), f32),
            jax.ShapeDtypeStruct((D, 2 * PROJ_BLOCK), bf16),
            jax.ShapeDtypeStruct((16, D), f32),
        ],
        scratch_shapes=[pltpu.SemaphoreType.DMA],
        compiler_params=pltpu.CompilerParams(vmem_limit_bytes=VMEM),
        cost_estimate=pl.CostEstimate(flops=18_000_000_000, bytes_accessed=20 * MIB, transcendentals=0),
        name="attend",
    )(place, lengths, x, *pieces)


def gelu_parts(u):
    size = jnp.abs(u)
    bell = jnp.exp2(u * u * (-0.5 * LOG2E))
    t = 1.0 / (1.0 + (0.3275911 * math.sqrt(0.5)) * size)
    poly = t * (0.127414796 + t * (-0.142248368 + t * (0.7107068705 + t * (-0.7265760135 + t * 0.5307027145))))
    tail = poly * bell
    below = jnp.where(u < 0.0, tail, 1.0 - tail)
    return below, bell


def mean_rows(v):
    return jnp.sum(v, axis=-1, keepdims=True) * (1.0 / D)


def norm_rows(total):
    center = total - mean_rows(total)
    rstd = lax.rsqrt(mean_rows(center * center) + NORM_EPSILON)
    return center * rstd, rstd


def norm_back(upstream, normed, rstd, gain):
    scaled = upstream * gain
    return rstd * (scaled - mean_rows(scaled) - normed * mean_rows(scaled * normed))


BLOCK = 256
WIDTH = 768
DOWN_STEPS = 4


def out_weight_copies(proj_w, out_w, sem):
    for half in range(2):
        lanes = pl.ds(half * PROJ_BLOCK + QKV_BLOCK, OUT_HALF)
        yield pltpu.make_async_copy(proj_w.at[:, lanes], out_w.at[:, pl.ds(half * OUT_HALF, OUT_HALF)], sem)


def probs_kernel(seq, lengths, q_ref, k_ref, stat_ref, *refs):
    prob_ref = refs[-1]
    pair = pl.program_id(0)
    rows = q_ref.shape[0]
    chunk = 256
    key_at = lax.broadcasted_iota(jnp.int32, (rows, 1), 0)
    hidden_keys = jnp.where(key_at < lengths[seq], 0.0, MASKED_SCORE).astype(f32)
    for i, mask in enumerate(lane_masks()):
        own_keys = k_ref[...] * mask
        for c in range(rows // chunk):
            span = slice(c * chunk, (c + 1) * chunk)
            log_total = stat_ref[0, pl.ds(2 * pair + i, 1), span]
            scores = dot_t(own_keys, q_ref[span, :]) * (0.125 * LOG2E) + hidden_keys
            prob_ref[i, :, span] = jnp.exp2(scores - log_total).astype(bf16)


def probs_specs(seq, rows):
    pairs = H // 2
    lane = lambda kind: pl.BlockSpec((rows, 128), lambda s: (seq, kind * pairs + s))
    specs = [SMEM, lane(0), lane(1), pl.BlockSpec((1, 16, rows), lambda s: (seq, 0, 0))]
    return specs, pl.BlockSpec((2, rows, rows), lambda s: (seq * pairs + s, 0, 0))


def probs(seq, lengths, qkv, stats, deps=()):
    seqs, _, rows = stats.shape
    specs, out = probs_specs(seq, rows)
    return call(
        functools.partial(probs_kernel, seq),
        (lengths, qkv, qkv, stats),
        deps,
        grid=(H // 2,),
        in_specs=specs,
        out_specs=out,
        out_shape=jax.ShapeDtypeStruct((seqs * H, rows, rows), bf16),
        compiler_params=pltpu.CompilerParams(vmem_limit_bytes=VMEM),
        cost_estimate=pl.CostEstimate(flops=8_000_000_000, bytes_accessed=MIB, transcendentals=0),
        name="probs",
    )


def window_kernel(seq, blocks, lengths, q_ref, k_ref, stat_ref, _, x_ref, att_ref, vec_ref, proj_w, *refs):
    prob_ref, normed_ref, rstd_ref, hid_ref, x_t, att_t, hid_t, out_w, sem = refs
    g = pl.program_id(0)

    @pl.when(g == 0)
    def _():
        start_all(out_weight_copies(proj_w, out_w, sem))

    probs_kernel(seq, lengths, q_ref, k_ref, stat_ref, prob_ref)

    @pl.when(g == 0)
    def _():
        wait_whole(out_w, sem)

    @pl.when(g < blocks)
    def _():
        x, attended = x_ref[...], att_ref[...]
        normed, rstd = norm_rows(x + dot(attended, out_w[...]) + vec_ref[2:3, :])
        normed_ref[...] = normed
        rstd_ref[...] = jnp.broadcast_to(rstd, rstd_ref.shape)
        hidden = normed * vec_ref[3:4, :] + vec_ref[4:5, :]
        hid_ref[...] = hidden.astype(bf16)
        x_t[...] = x.T.astype(bf16)
        att_t[...] = attended.astype(f32).T.astype(bf16)
        hid_t[...] = hidden.T.astype(bf16)


def window(seq, lengths, x, qkv, attended, stats, weights, vectors, prob, deps=()):
    count = x.shape[0]
    _, _, rows = stats.shape
    blocks = count // BLOCK
    block = lambda s: jnp.minimum(s, blocks - 1)
    token = lambda width: pl.BlockSpec((BLOCK, width), lambda s: (block(s), 0))
    turned = pl.BlockSpec((D, BLOCK), lambda s: (0, block(s)))
    specs, out = probs_specs(seq, rows)
    return call(
        functools.partial(window_kernel, seq, blocks),
        (lengths, qkv, qkv, stats, prob, x, attended, vectors, weights),
        deps,
        grid=(H // 2,),
        in_specs=specs + [ANY, token(D), token(D), whole(16, D), ANY],
        out_specs=[out, token(D), token(128), token(D)] + [turned] * 3,
        out_shape=[
            jax.ShapeDtypeStruct(prob.shape, bf16),
            jax.ShapeDtypeStruct((count, D), f32),
            jax.ShapeDtypeStruct((count, 128), f32),
            jax.ShapeDtypeStruct((count, D), bf16),
        ]
        + [jax.ShapeDtypeStruct((D, count), bf16)] * 3,
        input_output_aliases={4: 0},
        scratch_shapes=[pltpu.VMEM((D, D), bf16), pltpu.SemaphoreType.DMA],
        compiler_params=pltpu.CompilerParams(vmem_limit_bytes=VMEM),
        cost_estimate=pl.CostEstimate(flops=14_000_000_000, bytes_accessed=MIB, transcendentals=0),
        name="window",
    )


def ffn_kernel(meta, pieces, blocks, place, normed_ref, rstd_ref, hid_ref, cot_ref, vec_ref, b1_ref, proj_w, *refs):
    piece_refs = refs[:pieces]
    (out_ref, fb_ref, ab_ref, ib_ref, branch_ref, small_ref, db1_ref, keep, send) = refs[pieces : pieces + 9]
    (out_w, inner_w, down_w, act, down_back, sem, wsem) = refs[pieces + 9 :]
    step = pl.program_id(0)

    @pl.when(step == 0)
    def _():
        start_all(inner_blocks(place, zip(piece_refs, meta), inner_w, sem.at[0]))
        start_all(down_blocks(place, zip(piece_refs, meta), down_w, sem.at[1]))
        start_all(out_weight_copies(proj_w, out_w, sem.at[2]))
        small_ref[...] = jnp.zeros_like(small_ref)
        db1_ref[...] = jnp.zeros_like(db1_ref)
        wait_whole(inner_w, sem.at[0])
        wait_whole(down_w, sem.at[1])
        wait_whole(out_w, sem.at[2])

    @pl.when(step < blocks)
    def _():
        rows = aligned(step * BLOCK, BLOCK, BLOCK)
        first_gain, first_shift = vec_ref[3:4, :], vec_ref[4:5, :]
        second_gain, second_shift = vec_ref[6:7, :], vec_ref[7:8, :]
        first_normed = normed_ref[...]
        hidden_low = hid_ref[...]
        total = first_normed * first_gain + first_shift + vec_ref[5:6, :]
        slopes = []
        for c in range(FF // WIDTH):
            cols = pl.ds(c * WIDTH, WIDTH)
            u = dot(hidden_low, inner_w[:, cols]) + b1_ref[:, cols]
            below, bell = gelu_parts(u)
            active = (u * below).astype(bf16)
            act[rows, cols] = active
            slopes.append(below + u * bell * GAUSS_DENSITY)
            total = total + dot(active, down_w[cols, :])
        second_normed, second_rstd = norm_rows(total)
        out_ref[...] = second_normed * second_gain + second_shift
        cot = cot_ref[...]
        second_back = norm_back(cot, second_normed, second_rstd, second_gain)
        back_low = second_back.astype(bf16)
        down_back[rows, :] = back_low
        hidden_back = second_back
        for c in range(FF // WIDTH):
            cols = pl.ds(c * WIDTH, WIDTH)
            ib = (dot_t(back_low, down_w[cols, :]) * slopes[c]).astype(bf16)
            ib_ref[:, cols] = ib
            db1_ref[:, cols] += fold_rows(ib.astype(f32))
            hidden_back = hidden_back + dot_t(ib, inner_w[:, cols])
        first_back = norm_back(hidden_back, first_normed, rstd_ref[:, 0:1], first_gain)
        fb_ref[...] = first_back
        branch_low = first_back.astype(bf16)
        branch_ref[...] = branch_low
        ab_ref[...] = dot_t(branch_low, out_w[...]).astype(bf16)
        sums = (
            branch_low.astype(f32),
            hidden_back * first_normed,
            hidden_back,
            back_low.astype(f32),
            cot * second_normed,
            cot,
        )
        for i, v in enumerate(sums):
            small_ref[i] += fold_rows(v)

    @pl.when(step >= blocks)
    def _():
        chunk = step - blocks
        width = FF // DOWN_STEPS
        rows = aligned(chunk * width, width, 128)
        down_w[rows, :] = dot_l(act[:, rows], down_back[...]).astype(bf16)
        for i in range(CHIPS // DOWN_STEPS):
            chip = chunk * (CHIPS // DOWN_STEPS) + i
            for half in range(2):
                at = (chip * 2 + half) * (2 * PAIR_ROWS)
                pairs = [
                    (down_w.at[aligned(at + k * PAIR_ROWS, PAIR_ROWS, 16)], pl.ds(k * D, D)) for k in range(2)
                ]
                hand_over(place, chip, half, keep, send, pairs, wsem)

    @pl.when(step == blocks + DOWN_STEPS - 1)
    def _():
        wait_whole(keep, wsem)
        wait_whole(send, wsem)


def feed_forward(place, normed, rstd, hid, cotangent, vectors, inner_bias, weights, pieces, meta):
    count = normed.shape[0]
    blocks = count // BLOCK
    token = lambda width: pl.BlockSpec((BLOCK, width), lambda s: (jnp.minimum(s, blocks - 1), 0))
    return pl.pallas_call(
        functools.partial(ffn_kernel, meta, len(pieces), blocks),
        grid=(blocks + DOWN_STEPS,),
        in_specs=[SMEM, token(D), token(128), token(D), token(D), whole(16, D), whole(1, FF), ANY]
        + [ANY] * len(pieces),
        out_specs=[token(D), token(D), token(D), token(FF), token(D), whole(6, 8, D), whole(8, FF), ANY, ANY],
        out_shape=[
            jax.ShapeDtypeStruct((count, D), f32),
            jax.ShapeDtypeStruct((count, D), f32),
            jax.ShapeDtypeStruct((count, D), bf16),
            jax.ShapeDtypeStruct((count, FF), bf16),
            jax.ShapeDtypeStruct((count, D), bf16),
            jax.ShapeDtypeStruct((6, 8, D), f32),
            jax.ShapeDtypeStruct((8, FF), f32),
            jax.ShapeDtypeStruct((CHIPS, PAIR_ROWS, DOWN_BLOCK), bf16),
            jax.ShapeDtypeStruct((CHIPS, PAIR_ROWS, DOWN_BLOCK), bf16),
        ],
        scratch_shapes=[
            pltpu.VMEM((D, D), bf16),
            pltpu.VMEM((D, FF), bf16),
            pltpu.VMEM((FF, D), bf16),
            pltpu.VMEM((count, FF), bf16),
            pltpu.VMEM((count, D), bf16),
            pltpu.SemaphoreType.DMA((3,)),
            pltpu.SemaphoreType.DMA,
        ],
        compiler_params=pltpu.CompilerParams(vmem_limit_bytes=ALL_VMEM),
        cost_estimate=pl.CostEstimate(flops=52_000_000_000, bytes_accessed=40 * MIB, transcendentals=0),
        name="feed_forward",
    )(place, normed, rstd, hid, cotangent, vectors, inner_bias, weights, *pieces)


def inner_grads_kernel(hid_t, ib_ref, place, att_in, branch_in, keep, send, att_t, branch, out_g, inner_g, sem, wsem):
    step = pl.program_id(0)
    steps = FF // D
    later = [pltpu.make_async_copy(att_in, att_t, sem.at[0]), pltpu.make_async_copy(branch_in, branch, sem.at[1])]

    @pl.when(step == 0)
    def _():
        start_all(later)

    def give(grads, half, width, lane):
        for chip in range(CHIPS):
            block = grads.at[pl.ds(chip * PAIR_ROWS, PAIR_ROWS), pl.ds(half * width, width)]
            hand_over(place, chip, half, keep, send, [(block, pl.ds(lane, width))], wsem)

    @pl.when(step < steps)
    def _():
        cols = aligned(step * D, D, 128)
        inner_g[:, cols] = dot(hid_t[...], ib_ref[...]).astype(bf16)
        for half in range(2):

            @pl.when(step == (half + 1) * (steps // 2) - 1)
            def _():
                give(inner_g, half, INNER_HALF, OUT_HALF)

    @pl.when(step == steps)
    def _():
        for copy in later:
            copy.wait()
        out_g[...] = dot(att_t[...], branch[...]).astype(bf16)
        for half in range(2):
            give(out_g, half, OUT_HALF, 0)
        wait_whole(keep, wsem)
        wait_whole(send, wsem)


def inner_grads(place, hid_t, inner_back, att_t, branch):
    count = hid_t.shape[1]
    steps = FF // D
    return pl.pallas_call(
        inner_grads_kernel,
        grid=(steps + 1,),
        in_specs=[
            whole(D, count),
            pl.BlockSpec((count, D), lambda s: (0, jnp.minimum(s, steps - 1))),
            SMEM,
            ANY,
            ANY,
        ],
        out_specs=[ANY, ANY],
        out_shape=[jax.ShapeDtypeStruct((CHIPS, PAIR_ROWS, INNER_BLOCK), bf16)] * 2,
        scratch_shapes=[
            pltpu.VMEM((D, count), bf16),
            pltpu.VMEM((count, D), bf16),
            pltpu.VMEM((D, D), bf16),
            pltpu.VMEM((D, FF), bf16),
            pltpu.SemaphoreType.DMA((2,)),
            pltpu.SemaphoreType.DMA,
        ],
        compiler_params=pltpu.CompilerParams(vmem_limit_bytes=ALL_VMEM),
        cost_estimate=pl.CostEstimate(flops=4_000_000_000, bytes_accessed=MIB, transcendentals=0),
        name="inner_grads",
    )(hid_t, inner_back, place, att_t, branch)


def attend_back_pair(queries, keys, values, upstream, prob_ref, dq_ref, dk_ref, dv_ref):
    lows, backs = [], []
    masks = lane_masks()
    for i, mask in enumerate(masks):
        low = prob_ref[i]
        weight = low.astype(f32)
        weight_back = dot_t(values * mask, upstream)
        mean = jnp.sum(weight * weight_back, axis=0, keepdims=True)
        lows.append(low)
        backs.append((weight * (weight_back - mean)).astype(bf16))
    each = lambda v: jnp.concatenate([v * mask for mask in masks], axis=0)
    dv_ref[...] = dot(jnp.concatenate(lows, axis=1), each(upstream)).astype(bf16)
    dk_ref[...] = (dot(jnp.concatenate(backs, axis=1), each(queries)) * 0.125).astype(bf16)
    dq_ref[...] = (dot_l(jnp.concatenate(backs, axis=0), each(keys)) * 0.125).astype(bf16)


def attend_back_kernel(q_ref, k_ref, v_ref, up_ref, prob_ref, *refs):
    attend_back_pair(q_ref[...], k_ref[...], v_ref[...], up_ref[...], prob_ref, *refs[-3:])


def pair_specs(rows, first, last):
    pairs = H // 2
    pair = lambda s: jnp.minimum(first + s, last)
    lane = lambda kind: pl.BlockSpec((rows, 128), lambda s: (pair(s) // pairs, kind * pairs + pair(s) % pairs))
    return [lane(0), lane(1), lane(2), lane(0), pl.BlockSpec((2, rows, rows), lambda s: (pair(s), 0, 0))]


def attend_back(first, count, qkv, back, prob, grads=(), deps=()):
    specs = pair_specs(prob.shape[1], first, first + count - 1)
    return call(
        attend_back_kernel,
        (qkv, qkv, qkv, back, prob, *grads),
        deps,
        grid=(count,),
        in_specs=specs + [ANY] * len(grads),
        out_specs=[specs[0]] * 3,
        out_shape=[jax.ShapeDtypeStruct(back.shape, bf16)] * 3,
        input_output_aliases={5 + i: i for i in range(len(grads))},
        compiler_params=pltpu.CompilerParams(vmem_limit_bytes=ALL_VMEM),
        cost_estimate=pl.CostEstimate(flops=3_000_000_000, bytes_accessed=MIB, transcendentals=0),
        name=f"attend_back_{first}",
    )


def proj_grads_kernel(place, turned, small_ref, db1_ref, dq, dk, dv, keep, send, grads, packed, bias, sem, wsem):
    step = pl.program_id(0)
    copies = [pltpu.make_async_copy(v, grads.at[i], sem.at[i]) for i, v in enumerate((dq, dk, dv))]

    @pl.when(step == 0)
    def _():
        start_all([copies[1], copies[2], copies[0]])

    for turn, which in enumerate((1, 2, 0)):

        @pl.when(step == turn)
        def _():
            copies[which].wait()
            g = dot(turned[...], grads[which]).astype(bf16)
            if which == 1:
                packed[:, D:QKV_HALF] = g[:, : D // 2]
                packed[:, QKV_BLOCK : QKV_BLOCK + D // 2] = g[:, D // 2 :]
            else:
                at = 0 if which == 0 else QKV_BLOCK + D // 2
                packed[:, at : at + D] = g
                bias[which // 2] = fold_rows(grads[which].astype(f32))

    @pl.when(step == 0)
    def _():
        owner = lax.broadcasted_iota(jnp.int32, (SLABS, FF), 1) // (4 * SLAB)
        one = lax.broadcasted_iota(jnp.int32, (SLABS, FF), 0)
        mine = jnp.where(owner == one, jnp.sum(db1_ref[...], axis=0, keepdims=True), 0.0)
        place_of = lax.broadcasted_iota(jnp.int32, (FF, 128), 0) % (4 * SLAB)
        pick = place_of == lax.broadcasted_iota(jnp.int32, (FF, 128), 1)
        table = dot(mine.astype(bf16), pick.astype(bf16))
        spread = jnp.broadcast_to(table[:, None, :], (SLABS, SLAB, 128)).reshape(D, 128)
        packed[:, QKV_BLOCK + QKV_HALF :] = spread.astype(bf16)

    def give(half):
        for chip in range(CHIPS):
            block = packed.at[pl.ds(chip * PAIR_ROWS, PAIR_ROWS), pl.ds(half * QKV_BLOCK, QKV_BLOCK)]
            hand_over(place, chip, half, keep, send, [(block, pl.ds(0, QKV_BLOCK))], wsem)

    @pl.when(step == 1)
    def _():
        give(1)

    @pl.when(step == 2)
    def _():
        rows_of = [bias[...], small_ref[...], jnp.zeros((120, 8, D), f32)]
        packed[:, QKV_HALF:QKV_BLOCK] = jnp.sum(jnp.concatenate(rows_of, axis=0), axis=1).T.astype(bf16)
        give(0)
        wait_whole(keep, wsem)
        wait_whole(send, wsem)


def proj_grads(place, turned, small, inner_bias_grad, grads, deps=()):
    count = turned.shape[1]
    return call(
        proj_grads_kernel,
        (place, turned, small, inner_bias_grad, *grads),
        deps,
        grid=(3,),
        in_specs=[SMEM, whole(D, count), whole(6, 8, D), whole(8, FF), ANY, ANY, ANY],
        out_specs=[ANY, ANY],
        out_shape=[jax.ShapeDtypeStruct((CHIPS, PAIR_ROWS, QKV_BLOCK), bf16)] * 2,
        scratch_shapes=[
            pltpu.VMEM((3, count, D), bf16),
            pltpu.VMEM((D, 2 * QKV_BLOCK), bf16),
            pltpu.VMEM((2, 8, D), f32),
            pltpu.SemaphoreType.DMA((3,)),
            pltpu.SemaphoreType.DMA,
        ],
        compiler_params=pltpu.CompilerParams(vmem_limit_bytes=ALL_VMEM),
        cost_estimate=pl.CostEstimate(flops=4_000_000_000, bytes_accessed=MIB, transcendentals=0),
        name="proj_grads",
    )


def input_back_kernel(fb_ref, dq_ref, dk_ref, dv_ref, w_ref, *refs):
    half = D // 2
    total = fb_ref[...] + dot_t(dq_ref[...], w_ref[:, 0:D])
    total = total + dot_t(dk_ref[:, :half], w_ref[:, D:QKV_HALF])
    total = total + dot_t(dk_ref[:, half:], w_ref[:, PROJ_BLOCK : PROJ_BLOCK + half])
    out_ref, small_ref = refs[-2:]
    small_ref[...] = total[0:16, 0:128]
    out_ref[...] = total + dot_t(dv_ref[...], w_ref[:, PROJ_BLOCK + half : PROJ_BLOCK + QKV_HALF])


def input_back(first, blocks, first_back, grads, weights, given=(), deps=()):
    token = pl.BlockSpec((BLOCK, D), lambda s: (first + s, 0))
    return call(
        input_back_kernel,
        (first_back, *grads, weights, *given),
        deps,
        grid=(blocks,),
        in_specs=[token] * 4 + [whole(D, 2 * PROJ_BLOCK)] + [ANY] * len(given),
        out_specs=[token, whole(16, 128)],
        out_shape=[jax.ShapeDtypeStruct(first_back.shape, f32), jax.ShapeDtypeStruct((16, 128), f32)],
        input_output_aliases={5: 0} if given else {},
        compiler_params=pltpu.CompilerParams(vmem_limit_bytes=ALL_VMEM),
        cost_estimate=pl.CostEstimate(flops=10_000_000_000, bytes_accessed=MIB, transcendentals=0),
        name=f"input_back_{first}",
    )


def add_up_kernel(jobs, passed, place, *refs):
    refs[len(refs) - 1][...] = refs[0][0, 0:8, 0:128].astype(f32)
    first, out = 0, sum(count for count, _ in jobs) + passed
    for count, kind in jobs:
        terms = refs[first : first + count]
        first += count

        def total(slot):
            return sum((ref[slot].astype(f32) for ref in terms[1:]), terms[0][slot].astype(f32))

        slots = terms[0].shape[0]
        if kind == "upper":

            def one(i, _, total=total, ready=refs[out]):
                ready[i] = total(i).astype(bf16)
                return 0

            lax.fori_loop(0, slots, one, 0)
            out += 1
        elif kind == "both":
            half = slots // 2

            def one(i, _, total=total, ready=refs[out], rest=refs[out + 1], half=half):
                rest[i] = total(i)
                ready[i] = total(half + i).astype(bf16)
                return 0

            lax.fori_loop(0, half, one, 0)
            out += 2
        elif kind == "down":
            whole_sum = total(0)
            refs[out][0:PAIR_ROWS, :] = whole_sum[:, :D]
            refs[out][PAIR_ROWS:, :] = whole_sum[:, D:]
            out += 1
        else:
            whole_sum = total(0)
            low_core = place[1] == 0
            low, high = whole_sum[:SLAB], whole_sum[SLAB:]
            refs[out][...] = jnp.where(low_core, low, high)
            refs[out + 1][...] = jnp.where(low_core, high, low)
            out += 2


def add_up(place, *groups, passed=(), deps=(), vmem=ALL_VMEM):
    operands, specs, out_specs, shapes, jobs = [], [], [], [], []
    for size, terms, lazy in groups:
        _, rows, lanes = terms[0].shape
        half = size // 2
        kind = "upper" if lazy else "both" if size > 1 else "down" if lanes == DOWN_BLOCK else "halves"
        operands += terms
        take = (half, 1) if kind == "upper" else (size, 0)
        specs += [pl.BlockSpec((take[0], rows, lanes), lambda s, at=take[1]: (at, 0, 0))] * len(terms)
        if size > 1:
            kinds = [bf16] if kind == "upper" else [bf16, f32]
            out_specs += [whole(half, rows, lanes)] * len(kinds)
            shapes += [jax.ShapeDtypeStruct((half, rows, lanes), dtype) for dtype in kinds]
        else:
            ends = [(2 * PAIR_ROWS, D)] if kind == "down" else [(SLAB, lanes)] * 2
            out_specs += [whole(*end) for end in ends]
            shapes += [jax.ShapeDtypeStruct(end, f32) for end in ends]
        jobs.append((len(terms), kind))
    return call(
        lambda *refs: add_up_kernel(jobs, len(passed), refs[0], *refs[1:]),
        [place] + operands + list(passed),
        deps,
        grid=(1,),
        in_specs=[SMEM] + specs + [ANY] * len(passed),
        out_specs=out_specs + [ANY] * len(passed) + [whole(8, 128)],
        out_shape=shapes
        + [jax.ShapeDtypeStruct(v.shape, v.dtype) for v in passed]
        + [jax.ShapeDtypeStruct((8, 128), f32)],
        input_output_aliases={1 + len(operands) + i: len(shapes) + i for i in range(len(passed))},
        compiler_params=pltpu.CompilerParams(vmem_limit_bytes=vmem),
        cost_estimate=pl.CostEstimate(flops=1000, bytes_accessed=1000, transcendentals=0),
        name="add_up",
    )


def gate(value, deps, vmem=ALL_VMEM):
    return call(
        lambda value_ref, out_ref: None,
        [value],
        deps,
        grid=(1,),
        in_specs=[ANY],
        out_specs=ANY,
        out_shape=jax.ShapeDtypeStruct(value.shape, value.dtype),
        input_output_aliases={0: 0},
        compiler_params=pltpu.CompilerParams(vmem_limit_bytes=vmem),
        cost_estimate=pl.CostEstimate(flops=1000, bytes_accessed=1000, transcendentals=0),
        name="gate",
    )


def finish_inner_kernel(place, mine, other, out_g, inner_g, small):
    low_core = place[1] == 0
    low = jnp.where(low_core, mine[...], other[...])
    high = jnp.where(low_core, other[...], mine[...])
    out_g[:, :OUT_HALF], out_g[:, OUT_HALF:] = low[:, :OUT_HALF], high[:, :OUT_HALF]
    inner_g[:, :INNER_HALF], inner_g[:, INNER_HALF:] = low[:, OUT_HALF:], high[:, OUT_HALF:]
    small[...] = low[0:8, 0:128]


def finish_proj_kernel(place, mine, other, dq, dk, dv, bias, *vectors):
    low_core = place[1] == 0
    low = jnp.where(low_core, mine[...], other[...])
    high = jnp.where(low_core, other[...], mine[...])
    half = D // 2
    dq[...] = low[:, :D]
    dk[:, :half], dk[:, half:] = low[:, D:QKV_HALF], high[:, :half]
    dv[...] = high[:, half:QKV_HALF]
    bias[...] = high[0, QKV_HALF : QKV_HALF + 4 * SLAB]
    rows = low[:, QKV_HALF:].T
    for i, out in enumerate(vectors):
        out[...] = rows[i, 0:SLAB]


def finish(kernel, place, mine, other, shapes, name, deps=()):
    at = lambda shape: pl.BlockSpec(shape, lambda s: (0,) * len(shape))
    return call(
        kernel,
        (place, mine, other),
        deps,
        grid=(1,),
        in_specs=[SMEM, at(mine.shape), at(mine.shape)],
        out_specs=[at(shape) for shape in shapes],
        out_shape=[jax.ShapeDtypeStruct(shape, f32) for shape in shapes],
        compiler_params=pltpu.CompilerParams(vmem_limit_bytes=LITTLE),
        cost_estimate=pl.CostEstimate(flops=1000, bytes_accessed=1000, transcendentals=0),
        name=name,
    )


def finish_inner(place, mine, other):
    return finish(finish_inner_kernel, place, mine, other, [(SLAB, D), (SLAB, FF), (8, 128)], "finish_inner")


def finish_proj(place, mine, other, deps=()):
    shapes = [(SLAB, D)] * 3 + [(4 * SLAB,)] + [(SLAB,)] * 8
    return finish(finish_proj_kernel, place, mine, other, shapes, "finish_proj", deps)


AXES = ("dp", "fsdp")


CORE = (1, 1)
ALONG_Z_FIRST, ALONG_Z_THEN, ALONG_Z_BOTH, ALONG_XY_FIRST, ALONG_XY_THEN = (16, 8), (8, 16), (24, 24), (2, 4), (4, 2)
FAST_SHAPE = {"dp": 4, "fsdp": 8}


def move(v, masks):
    return lax.ppermute(v, AXES, [(i, i ^ masks[i & 1]) for i in range(SLABS)])


SUM_STEPS = (ALONG_XY_THEN, ALONG_XY_FIRST, ALONG_Z_THEN, ALONG_Z_FIRST)


def after(*values):
    return lax.optimization_barrier(values)


class Sums:
    def __init__(self, keep, got):
        self.size, self.terms, self.step = CHIPS, [keep, got], 0

    def send(self, outs, lazy):
        ready = outs.pop(0)
        if not lazy:
            self.terms = [outs.pop(0)]
        self.size //= 2
        self.terms = self.terms + [move(ready, SUM_STEPS[self.step])]
        self.step += 1


def add_and_send(place, *groups, lazy=False, **options):
    outs = list(add_up(place, *[(g.size, g.terms, lazy) for g in groups], **options))
    for g in groups:
        if g.size > 1:
            g.send(outs, lazy)
    return outs


def fast_blocks(shards, core):
    (qw, kw, vw, ow, qb, vb, ob, fg, fs, iw, ib, dw, db, sg, ss) = shards
    vectors = jnp.pad(jnp.stack([qb, vb, ob, fg, fs, db, sg, ss], axis=1), ((0, 0), (0, 120)))
    inner_bias = jnp.pad(ib.reshape(1, 4 * SLAB), ((0, SLAB - 1), (0, 128 - 4 * SLAB)))
    half = D // 2
    halves = [
        jnp.concatenate([qw, kw[:, :half], vectors, ow[:, :half], iw[:, :INNER_HALF]], axis=1),
        jnp.concatenate([kw[:, half:], vw, inner_bias, ow[:, half:], iw[:, INNER_HALF:]], axis=1),
    ]
    low_core = core == 0
    own = jnp.where(low_core, halves[0], halves[1])
    other = move(jnp.where(low_core, halves[1], halves[0]), CORE)
    rows = jnp.concatenate([jnp.where(low_core, own, other), jnp.where(low_core, other, own)], axis=0)
    return rows[:, :PROJ_BLOCK], rows[:, PROJ_BLOCK:], jnp.concatenate([dw[:PAIR_ROWS], dw[PAIR_ROWS:]], axis=1)


def gather_plain(shards):
    (qw, kw, vw, ow, qb, vb, ob, fg, fs, iw, ib, dw, db, sg, ss) = [
        lax.all_gather(v, AXES, axis=0, tiled=True) for v in shards
    ]
    vectors = jnp.pad(jnp.stack([qb, vb, ob, fg, fs, db, sg, ss], axis=1), ((0, 0), (0, 120)))
    inner_bias = jnp.pad(ib.reshape(SLABS, 1, 4 * SLAB), ((0, 0), (0, SLAB - 1), (0, 128 - 4 * SLAB))).reshape(D, 128)
    half = D // 2
    chips = lambda v: v.reshape(CHIPS, PAIR_ROWS, -1)
    down = dw.reshape(CHIPS, 2, 2, PAIR_ROWS, D)
    first = [
        chips(jnp.concatenate([qw, kw[:, :half], vectors, ow[:, :half]], axis=1)),
        chips(jnp.concatenate([kw[:, half:], vw, inner_bias, ow[:, half:]], axis=1)),
    ]
    second = [
        jnp.concatenate([chips(iw[:, c * INNER_HALF : (c + 1) * INNER_HALF]), down[:, c, 0], down[:, c, 1]], axis=2)
        for c in range(2)
    ]
    slots = lambda halves: [v[np.array(SLOT_CHIPS[c])] for c, v in enumerate(halves)]
    return slots(first), slots(second)


def local(fast, inputs, lengths, *rest):
    shards, cotangent = rest[:15], rest[15]
    both = lambda v, came: jnp.concatenate([v, came])
    if fast:
        linear = lax.axis_index(AXES)
        core = linear & 1
        place = jnp.stack([linear >> 1, core]).astype(jnp.int32)
        first, inner, down = fast_blocks(shards, core)
        first = first[None]
        first = both(first, move(first, ALONG_Z_FIRST))
        first, second = after(first, jnp.concatenate([inner, down], axis=1)[None])
        second = jnp.concatenate([second] + [move(second, steps) for steps in (ALONG_Z_FIRST, ALONG_Z_THEN, ALONG_Z_BOTH)])
        first = both(first, move(first, ALONG_Z_THEN))
        first_then, first_core = move(first, ALONG_XY_THEN), move(first, CORE)
        first_came = move(first, ALONG_XY_FIRST)
        first_last, came_core = move(first_came, ALONG_XY_THEN), move(first_came, CORE)
        first = [first, first_came, first_then, first_last]
        first += [first_core, came_core, move(first_then, CORE), move(first_last, CORE)]
        second_came, second_then, second_core = move(second, ALONG_XY_FIRST), move(second, ALONG_XY_THEN), move(second, CORE)
        meta = tuple((at, other) for other in (False, True) for at in range(0, CHIPS, 4))
    else:
        place = jnp.zeros((2,), jnp.int32)
        first, second = gather_plain(shards)
        meta = ((0, False), (0, True))
    qkv, attended, stats, weights, vectors = attend(place, lengths, inputs, first, meta)
    prob = probs(0, lengths, qkv, stats)
    if fast:
        second_came, second_then, prob = after(second_came, second_then, prob)
        second_last, came_core, then_core = move(second_came, ALONG_XY_THEN), move(second_came, CORE), move(second_then, CORE)
    prob, normed, rstd, hid, inputs_t, attended_t, hid_t = window(
        1, lengths, inputs, qkv, attended, stats, weights, vectors, prob
    )
    bias_at = PROJ_BLOCK + QKV_HALF
    inner_bias = weights[::SLAB, bias_at : bias_at + 4 * SLAB].reshape(1, FF).astype(f32)
    if fast:
        second_last, normed, inner_bias = after(second_last, normed, inner_bias)
        second = [second, second_came, second_then, second_last]
        second += [second_core, came_core, then_core, move(second_last, CORE)]
    output, first_back, back, inner_back, branch, small, db1, down_keep, down_send = feed_forward(
        place, normed, rstd, hid, cotangent, vectors, inner_bias, weights, second, meta
    )
    inner_keep, inner_send = inner_grads(place, hid_t, inner_back, attended_t, branch)
    pairs = lengths.shape[0] * (H // 2)
    third = pairs // 3
    deps = []
    if fast:
        down = Sums(down_keep, move(down_send, CORE))
        inner_send, *deps = add_and_send(place, down, lazy=True, passed=[inner_send], deps=[inner_keep])
        inner = Sums(inner_keep, move(inner_send, CORE))
    grads = attend_back(0, third, qkv, back, prob, deps=deps)
    if fast:
        deps = add_and_send(place, inner, lazy=True, deps=grads[:1])
    grads = attend_back(third, third, qkv, back, prob, grads, deps=deps)
    if fast:
        deps = add_and_send(place, down, lazy=True, deps=grads[:1])
    grads = attend_back(2 * third, pairs - 2 * third, qkv, back, prob, grads, deps=deps)
    if fast:
        deps = add_and_send(place, inner, down, lazy=True, deps=grads[:1])
    proj_keep, proj_send = proj_grads(place, inputs_t, small, db1, grads, deps=deps)
    blocks = inputs.shape[0] // BLOCK
    if fast:
        proj_send = gate(proj_send, [inner.terms[-1], down.terms[-1]])
        proj = Sums(proj_keep, move(proj_send, CORE))
        deps = add_and_send(place, inner, down, deps=[proj_keep])
        deps = add_and_send(place, proj, lazy=True, deps=deps)
        grad_input, came = input_back(0, blocks, first_back, grads, weights, deps=deps)
        proj.terms[-1] = gate(proj.terms[-1], [inner.terms[-1], down.terms[-1], came], MIB)
        deps = add_and_send(place, proj, vmem=LITTLE)
        down_grad, *deps = add_and_send(place, inner, down, deps=deps, vmem=LITTLE)
        proj.terms[-1] = gate(proj.terms[-1], [inner.terms[-1]], MIB)
        deps = add_and_send(place, proj, deps=deps, vmem=LITTLE)
        mine, other, *deps = add_and_send(place, proj, inner, deps=deps, vmem=LITTLE)
        out_grad, inner_grad, *deps = finish_inner(place, mine, move(other, CORE))
        mine, other, _ = add_and_send(place, proj, deps=deps, vmem=LITTLE)
        *square, bias, v0, v1, v2, v3, v4, v5, v6, v7 = finish_proj(place, mine, move(other, CORE))
        vectors = [v0, v1, v2, v3, v4, v5, v6, v7]
    else:
        grad_input, _ = input_back(0, blocks, first_back, grads, weights)
        shard = lambda *v: lax.psum_scatter(jnp.concatenate(v, axis=1), AXES, scatter_dimension=0, tiled=True)
        by_chip = lambda pair: [v[np.argsort(np.array(SLOT_CHIPS[c]))].astype(f32) for c, v in enumerate(pair)]
        low, high = (v.reshape(D, -1) for v in by_chip((inner_keep, inner_send)))
        out_grad, inner_grad = shard(low[:, :OUT_HALF], high[:, :OUT_HALF]), shard(low[:, OUT_HALF:], high[:, OUT_HALF:])
        parts = [jnp.stack([v[:, :, :D], v[:, :, D:]], axis=1) for v in by_chip((down_keep, down_send))]
        down_grad = shard(jnp.stack(parts, axis=1).reshape(FF, D))
        low, high = (v.reshape(D, -1) for v in by_chip((proj_keep, proj_send)))
        half = D // 2
        square = shard(low[:, :D]), shard(low[:, D:QKV_HALF], high[:, :half]), shard(high[:, half:QKV_HALF])
        columns = shard(low[:, QKV_HALF:])
        vectors = [columns[:, i] for i in range(8)]
        bias = shard(high[::SLAB, QKV_HALF : QKV_HALF + 4 * SLAB].reshape(FF, 1))[:, 0]
    return (
        output,
        grad_input,
        *square,
        out_grad,
        *vectors[:5],
        inner_grad,
        bias,
        down_grad,
        *vectors[5:],
    )


def solution(mesh):
    rows, flat = P(AXES, None), P(AXES)
    params = (rows,) * 4 + (flat,) * 5 + (rows, flat, rows, flat, flat, flat)
    return jax.shard_map(
        functools.partial(local, dict(mesh.shape) == FAST_SHAPE),
        mesh=mesh,
        in_specs=(rows, flat) + params + (rows,),
        out_specs=(rows, rows) + params,
        check_vma=False,
    )
```
